32 devices in a mesh: expert: 8 (over z, x), shard: 4 (over y, core).
Axes of the slice: x: 2, y: 2, z: 4, core: 2. Of those that a mesh axis runs over, the one named last changes fastest.
Arguments:
- tokens: bfloat16 [4096, 2048], P(('expert', 'shard')), may hold values from -6 to 6
- first_gain: float32 [2048], replicated, may hold values from 0.25 to 1.75
- attention_in: bfloat16 [2048, 3, 2048], P('expert', None, 'shard'), may hold values from -0.125 to 0.125
- attention_bias: bfloat16 [3, 16, 128], P(None, 'shard', 'expert'), may hold values from -0.59765625 to 0.59765625
- attention_out: bfloat16 [2048, 2048], P('shard', 'expert'), may hold values from -0.5 to 0.5
- second_gain: float32 [2048], replicated, may hold values from 0.25 to 1.75
- router: bfloat16 [2048, 16], P('expert'), may hold values from -0.0625 to 0.0625
- shared_gate: bfloat16 [2048], P('expert'), may hold values from -0.125 to 0.125
- shared_in: bfloat16 [2048, 2, 5632], P('expert', None, 'shard'), may hold values from -0.125 to 0.125
- shared_out: bfloat16 [5632, 2048], P('shard', 'expert'), may hold values from -0.21875 to 0.21875
- expert_in: bfloat16 [16, 2048, 2, 1408], P('expert', None, None, 'shard'), may hold values from -0.125 to 0.125
- expert_out: bfloat16 [16, 1408, 2048], P('expert', 'shard'), may hold values from -4 to 4
- cotangent: bfloat16 [4096, 2048], P(('expert', 'shard')), may hold values from -6 to 6
- expert_picks: int32 [4096, 4], P(('expert', 'shard')), may hold values from 0 to 15, all different within a row; in each aligned block of 128 rows (0 to 127, 128 to 255, ...) at most 64 rows name the same one
Outputs:
- output: bfloat16 [4096, 2048], P(('expert', 'shard'))
- input_grad: float32 [4096, 2048], P(('expert', 'shard'))
- first_gain_grad: float32 [2048], replicated
- attention_in_grad: float32 [2048, 3, 2048], P('expert', None, 'shard')
- attention_bias_grad: float32 [3, 16, 128], P(None, 'shard', 'expert')
- attention_out_grad: float32 [2048, 2048], P('shard', 'expert')
- second_gain_grad: float32 [2048], replicated
- router_grad: float32 [2048, 16], P('expert')
- shared_gate_grad: float32 [2048], P('expert')
- shared_in_grad: float32 [2048, 2, 5632], P('expert', None, 'shard')
- shared_out_grad: float32 [5632, 2048], P('shard', 'expert')
- expert_in_grad: float32 [16, 2048, 2, 1408], P('expert', None, None, 'shard')
- expert_out_grad: float32 [16, 1408, 2048], P('expert', 'shard')
The draws below stay inside these ranges and needn't reach their ends.
Inputs may be any that keep to these rules, and one draw needn't show every extreme that they name: `expert_picks`: each row names 4 different experts. Among the rows of one device no expert is named more than 64 times, and in every draw some device names some expert exactly 64 times.
All inputs are finite; a program needn't handle non-finite values.
Results may differ from the reference program's by a relative error of at most 0.03.
Values may be sent and summed in bfloat16 or wider, within the bound.
A program may use at most 320 MiB of HBM per device.

```python
import math
import jax
import jax.numpy as jnp
import numpy as np
from jax import lax

D = 2048
HEADS = 16
HEAD_DIM = 128
FF = 1408
SFF = 5632
TOPK = 4
TOK_DEV = 128
EXPERTS = 16
SEQ = 512
TOKENS = 4096
CAP = 64


def level_of(own_key, extent, cuts, least, largest):
    def one(dim, shards_of):
        draws = jax.random.uniform(jax.random.fold_in(jax.random.fold_in(own_key, 6), dim), (shards_of,), jnp.float32, least / len(cuts), largest / len(cuts))
        return jnp.repeat(jnp.exp(draws), extent[dim] // shards_of).reshape((-1,) + (1,) * (len(extent) - dim - 1))

    loudness = one(*cuts[0])
    for cut in cuts[1:]:
        loudness = loudness * one(*cut)
    return loudness


def deal_out(rng, own, number, rows, number_of, top, bound, slope):
    order = jax.random.permutation(rng, number_of)
    heavy_load, usual = portions_of(number_of, rows * top, bound, slope, True), portions_of(number_of, rows * top, bound, slope, False)
    places = jnp.arange(number_of)

    def named(sizes, turn):
        used = int((sizes > 0).sum())
        fixed = max(1, used // 4)
        shifted = fixed + (places - fixed + turn * (used - fixed)) % max(1, number_of - fixed)
        return jnp.zeros((number_of,), jnp.int32).at[order[jnp.where(places < fixed, places, shifted)]].set(jnp.asarray(sizes, jnp.int32))

    sizes = jnp.where(number % 4 == 0, named(heavy_load, number // 4), named(usual, number - number // 4 - 1))
    mixed = jax.random.permutation(jax.random.fold_in(own, 3), number_of)
    source_of, sink = mixed[0:number_of // 2 * 2:2], mixed[1:number_of // 2 * 2:2]
    room = jnp.minimum(sizes[source_of] - 1, bound - sizes[sink]) // 2
    room = jnp.where((source_of == order[0]) | (sink == order[0]) | (sizes[sink] == 0), 0, jnp.maximum(room, 0))
    shifted = jax.random.randint(jax.random.fold_in(own, 4), (number_of // 2,), 0, 1 << 20) % (room + 1)
    sizes = sizes.at[source_of].add(-shifted).at[sink].add(shifted)
    items = jnp.searchsorted(jnp.cumsum(sizes), jnp.arange(rows * top), side="right").astype(jnp.int32)
    table = items.reshape(top, rows).T
    table = table[jax.random.permutation(jax.random.fold_in(own, 1), rows)]
    turn = jax.random.randint(jax.random.fold_in(own, 2), (rows, 1), 0, top)
    return jnp.take_along_axis(table, (jnp.arange(top)[None, :] + turn) % top, axis=1)


def portions_of(count, total, reach, slope, full):
    weights = [(1 << 20) // math.isqrt(standing ** slope) + 1 for standing in range(1, count + 1)]
    largest = reach if full else min(reach, max(-(-total // count), total * weights[0] // sum(weights)))
    least = 1 if total - largest >= count - 1 else 0
    holding, spare = [largest] + [least] * (count - 1), total - largest - least * (count - 1)
    while spare > 0:
        candidates = [i for i in range(1, count) if holding[i] < largest] or [i for i in range(1, count) if holding[i] < reach]
        pool, remaining = sum([weights[i] for i in candidates]), spare
        for i in candidates:
            extra = min(reach - holding[i], max(1, remaining * weights[i] // pool), spare)
            holding[i] = holding[i] + extra
            spare = spare - extra
    return np.array(holding)


def centred(key, extent, deviation, bound, split=(), held_as=jnp.bfloat16):
    array = jax.random.normal(key, extent, jnp.float32) * deviation
    if len(split) > 0:
        array = level_of(key, extent, split, -0.22, 0.18) * array
    return jnp.clip(array, min=-bound, max=bound).astype(held_as)


def setup_inputs(seed: int = 0) -> dict:
    key_of = jax.random.split(jax.random.key(seed), 15)
    tokens = centred(key_of[0], (TOKENS, D), 1.0, 6.0, ((0, 32),))
    first_gain = jnp.clip(1.0 + 0.15 * jax.random.normal(key_of[1], (D,), jnp.float32), 0.25, 1.75)
    attention_in = centred(key_of[2], (D, 3, D), D ** -0.5, 0.125, ((0, 8), (2, 4)))
    attention_bias = centred(key_of[3], (3, HEADS, HEAD_DIM), 0.1, 0.59765625, ((1, 4), (2, 8)))
    attention_out = centred(key_of[4], (D, D), (D // 16) ** -0.5, 0.5, ((0, 4), (1, 8)))
    second_gain = jnp.clip(1.0 + 0.15 * jax.random.normal(key_of[5], (D,), jnp.float32), 0.25, 1.75)
    router = centred(key_of[6], (D, EXPERTS), (4 * D) ** -0.5, 0.0625, ((0, 8),))
    shared_gate = centred(key_of[7], (D,), D ** -0.5, 0.125, ((0, 8),))
    shared_in = centred(key_of[8], (D, 2, SFF), D ** -0.5, 0.125, ((0, 8), (2, 4)))
    shared_out = centred(key_of[9], (SFF, D), (SFF // 8) ** -0.5, 0.21875, ((0, 4), (1, 8)))
    expert_in = centred(key_of[10], (EXPERTS, D, 2, FF), D ** -0.5, 0.125, ((0, 8), (3, 4)))
    expert_out = centred(key_of[11], (EXPERTS, FF, D), (max(1, FF // 512)) ** -0.5, 4.0, ((0, 8), (1, 4)))
    cotangent = centred(key_of[12], (TOKENS, D), 1.0, 6.0, ((0, 32),))
    expert_picks_keys = jax.random.split(jax.random.fold_in(key_of[13], 1), TOKENS // TOK_DEV)
    expert_picks_turns = jax.random.permutation(jax.random.fold_in(key_of[13], 3), TOKENS // TOK_DEV)
    expert_picks = jax.vmap(lambda own, number: deal_out(jax.random.fold_in(key_of[13], 2), own, number, TOK_DEV, EXPERTS, TOPK, CAP, 1))(expert_picks_keys, expert_picks_turns).reshape((TOKENS, TOPK))
    return {"tokens": tokens, "first_gain": first_gain, "attention_in": attention_in, "attention_bias": attention_bias, "attention_out": attention_out, "second_gain": second_gain, "router": router, "shared_gate": shared_gate, "shared_in": shared_in, "shared_out": shared_out, "expert_in": expert_in, "expert_out": expert_out, "cotangent": cotangent, "expert_picks": expert_picks}


EPSILON = 1e-06
ROPE_BASE = 1000000.0
MASKED = -1e+30

@jax.custom_vjp
def low(v):
    return lax.optimization_barrier(v.astype(jnp.bfloat16)).astype(jnp.float32)

@jax.custom_vjp
def low_back(v):
    return v

def low_keep(v):
    return (low(v), None)

def low_pass(kept, grad):
    return (grad,)

def back_keep(v):
    return (v, None)

def back_low(kept, grad):
    return (low(grad),)
low.defvjp(low_keep, low_pass)
low_back.defvjp(back_keep, back_low)

def exact_dot(left_side, right_side):
    return jnp.dot(left_side, right_side, precision=lax.Precision.HIGHEST)

def normalize(activations):
    return activations * lax.rsqrt(lax.optimization_barrier(jnp.mean(activations * activations, axis=-1, keepdims=True)) + EPSILON)

def rope_tables(length, head_dim):
    half_dim = head_dim // 2
    frequency = jnp.power(ROPE_BASE, -jnp.arange(half_dim, dtype=jnp.float32) * (2.0 / head_dim))
    angles = jnp.arange(length, dtype=jnp.float32)[:, None] * frequency[None, :]
    return (jnp.concatenate([jnp.cos(angles), jnp.cos(angles)], axis=-1), jnp.concatenate([jnp.sin(angles), jnp.sin(angles)], axis=-1))

def rotate(values, cosine_table, sine_table):
    half_dim = values.shape[-1] // 2
    turned = jnp.concatenate([-values[..., half_dim:], values[..., :half_dim]], axis=-1)
    return values * cosine_table[:, None, :] + turned * sine_table[:, None, :]

def attend_sequence(packed):
    queries = packed[:, 0]
    keys_all = packed[:, 1]
    values = packed[:, 2]
    scores = jnp.einsum('qhd,khd->hqk', queries, keys_all, precision=lax.Precision.HIGHEST) * HEAD_DIM ** (-0.5)
    positions = jnp.arange(SEQ, dtype=jnp.int32)
    scores = jnp.where(positions[None, None, :] <= positions[None, :, None], scores, MASKED)
    scores = low_back(scores)
    weights = low(jax.nn.softmax(scores, axis=-1))
    return jnp.einsum('hqk,khd->qhd', weights, values, precision=lax.Precision.HIGHEST)

def expert_apply(operands):
    activations, weight_in, weight_out = operands
    raised = low_back(exact_dot(activations, weight_in.reshape(D, 2 * FF)).reshape(-1, 2, FF))
    hidden = low(jax.nn.silu(raised[:, 0]) * raised[:, 1])
    return exact_dot(hidden, weight_out)

def slot_positions(expert_picks):
    blocks = TOKENS // TOK_DEV
    flat_picks = expert_picks.reshape(blocks, TOK_DEV * TOPK)
    onehot = (flat_picks[:, :, None] == jnp.arange(EXPERTS, dtype=jnp.int32)[None, None, :]).astype(jnp.int32)
    slot_ranks = lax.optimization_barrier(jnp.sum((jnp.cumsum(onehot, axis=1) - onehot) * onehot, axis=2)).astype(jnp.int32)
    offset = jnp.arange(blocks, dtype=jnp.int32)[:, None] * EXPERTS
    return ((offset + flat_picks) * CAP + slot_ranks).reshape(-1).astype(jnp.int32)

def forward(arrays, slot_rows, picked):
    inputs, first_gain, attention_in, attention_bias, attention_out, second_gain, router, shared_gate, shared_in, shared_out, expert_in, expert_out = arrays
    first_low = low(normalize(inputs) * first_gain)
    projected = exact_dot(first_low, attention_in.reshape(D, 3 * D)).reshape(TOKENS, 3, HEADS, HEAD_DIM)
    projected = low_back(projected + attention_bias[None])
    projected = projected.reshape(TOKENS // SEQ, SEQ, 3, HEADS, HEAD_DIM)
    cosine_table, sine_table = rope_tables(SEQ, HEAD_DIM)
    packed = low(jnp.stack([rotate(projected[:, :, 0], cosine_table, sine_table), rotate(projected[:, :, 1], cosine_table, sine_table), projected[:, :, 2]], axis=2))
    attended = lax.map(jax.checkpoint(attend_sequence), packed).reshape(TOKENS, D)
    attended = low_back(low(attended))
    residual = inputs + low_back(exact_dot(attended, attention_out))
    second_low = low(normalize(residual) * second_gain)
    route_probs = jax.nn.softmax(low_back(exact_dot(second_low, router)), axis=-1)
    gate_values = lax.optimization_barrier(jnp.sum(picked * route_probs[:, None, :], axis=-1))
    shared_scale = jax.nn.sigmoid(low_back(exact_dot(second_low, shared_gate)))
    raised = low_back(exact_dot(second_low, shared_in.reshape(D, 2 * SFF)).reshape(TOKENS, 2, SFF))
    hidden = low(jax.nn.silu(raised[:, 0]) * raised[:, 1])
    shared_rows = low_back(exact_dot(hidden, shared_out))
    blocks = TOKENS // TOK_DEV
    spread = jnp.zeros((blocks * EXPERTS * CAP, D), second_low.dtype)
    spread = spread.at[slot_rows].set(jnp.repeat(second_low, TOPK, axis=0))
    grouped = low_back(spread).reshape(blocks, EXPERTS, CAP, D).transpose(1, 0, 2, 3).reshape(EXPERTS, blocks * CAP, D)
    results = low_back(low(lax.map(jax.checkpoint(expert_apply), (grouped, expert_in, expert_out))))
    returned = results.reshape(EXPERTS, blocks, CAP, D).transpose(1, 0, 2, 3).reshape(blocks * EXPERTS * CAP, D)[slot_rows]
    routed = lax.optimization_barrier(jnp.sum(gate_values[:, :, None] * returned.reshape(TOKENS, TOPK, D), axis=1))
    return residual + shared_scale[:, None] * shared_rows + routed

def reference(tokens, first_gain, attention_in, attention_bias, attention_out, second_gain, router, shared_gate, shared_in, shared_out, expert_in, expert_out, cotangent, expert_picks):
    slot_rows = slot_positions(expert_picks)
    picked = (expert_picks[:, :, None] == jnp.arange(EXPERTS, dtype=jnp.int32)[None, None, :]).astype(jnp.float32)
    params = tuple((member.astype(jnp.float32) for member in (tokens, first_gain, attention_in, attention_bias, attention_out, second_gain, router, shared_gate, shared_in, shared_out, expert_in, expert_out)))
    output, pullback = jax.vjp(lambda arrays: forward(arrays, slot_rows, picked), params)
    gradients, = pullback(cotangent.astype(jnp.float32))
    return (output.astype(jnp.bfloat16), gradients[0], gradients[1], gradients[2], gradients[3], gradients[4], gradients[5], gradients[6], gradients[7], gradients[8], gradients[9], gradients[10], gradients[11])
```

```python
import functools

import jax
import jax.numpy as jnp
from jax import lax
from jax.experimental import pallas as pl
from jax.experimental.pallas import tpu as pltpu
from jax.sharding import PartitionSpec as P

EPSILON = 1e-06
ROPE_BASE = 1000000.0
MASKED = -1e30
EXPERT, SHARD = "expert", "shard"
CORE, ROW, COLUMN = "kc", "ky", "kx"
SUM_CORES, SHARE, TOTAL = "sc", "share", "t"


def normalize(activations):
    factor = lax.rsqrt(jnp.mean(activations * activations, axis=-1, keepdims=True) + EPSILON)
    return (activations * factor, factor)


def norm_back(incoming, normed, factor, gain_vec):
    scaled = incoming * gain_vec
    inner_mean = jnp.mean(scaled * normed, axis=-1, keepdims=True)
    return (factor * (scaled - normed * inner_mean), jnp.sum(incoming * normed, axis=0))


def rope_tables(length, head_dim):
    half_dim = head_dim // 2
    frequency = jnp.power(ROPE_BASE, -jnp.arange(half_dim, dtype=jnp.float32) * (2.0 / head_dim))
    angles = jnp.arange(length, dtype=jnp.float32)[:, None] * frequency[None, :]
    return (
        jnp.concatenate([jnp.cos(angles), jnp.cos(angles)], axis=-1),
        jnp.concatenate([jnp.sin(angles), jnp.sin(angles)], axis=-1),
    )


def rotate(values, cosine_table, sine_table):
    half_dim = values.shape[-1] // 2
    turned = jnp.concatenate([-values[..., half_dim:], values[..., :half_dim]], axis=-1)
    return values * cosine_table[:, None, :] + turned * sine_table[:, None, :]


def rotate_back(incoming, cosine_table, sine_table):
    half_dim = incoming.shape[-1] // 2
    scaled = incoming * sine_table[:, None, :]
    turned = jnp.concatenate([scaled[..., half_dim:], -scaled[..., :half_dim]], axis=-1)
    return incoming * cosine_table[:, None, :] + turned


def block_scores(query_block, keys_all, first_row, score_scale):
    scores = (
        jnp.einsum("qhd,khd->hqk", query_block, keys_all, preferred_element_type=jnp.float32)
        * score_scale
    )
    row_pos = first_row + jnp.arange(query_block.shape[0], dtype=jnp.int32)
    col_pos = jnp.arange(keys_all.shape[0], dtype=jnp.int32)
    return jnp.where(col_pos[None, None, :] <= row_pos[None, :, None], scores, MASKED)


def attend(queries, keys_all, values, block_rows, score_scale):
    blocks = queries.shape[0] // block_rows
    starts = jnp.arange(blocks, dtype=jnp.int32) * block_rows

    def one_block(block_item):
        query_block, first_row = block_item
        scores = block_scores(query_block, keys_all, first_row, score_scale)
        highest = jnp.max(scores, axis=-1, keepdims=True)
        raised = jnp.exp(scores - highest)
        row_total = jnp.sum(raised, axis=-1, keepdims=True)
        weights = (raised / row_total).astype(jnp.bfloat16)
        mixed_out = jnp.einsum("hqk,khd->qhd", weights, values, preferred_element_type=jnp.float32)
        return (mixed_out, (highest + jnp.log(row_total))[..., 0])

    shape_blocks = (blocks, block_rows) + queries.shape[1:]
    mixed_out, logsum = lax.map(one_block, (queries.reshape(shape_blocks), starts))
    return (mixed_out.reshape(queries.shape), logsum)


def attend_back(queries, keys_all, values, logsum, grad_out, block_rows, score_scale):
    blocks = queries.shape[0] // block_rows
    starts = jnp.arange(blocks, dtype=jnp.int32) * block_rows
    shape_blocks = (blocks, block_rows) + queries.shape[1:]

    def one_block(running, block_item):
        key_grad, value_grad = running
        query_block, grad_block, logsum_block, first_row = block_item
        scores = block_scores(query_block, keys_all, first_row, score_scale)
        block_probs = jnp.exp(scores - logsum_block[..., None])
        value_grad = value_grad + jnp.einsum(
            "hqk,qhd->khd",
            block_probs.astype(jnp.bfloat16),
            grad_block,
            preferred_element_type=jnp.float32,
        )
        prob_grad = jnp.einsum(
            "qhd,khd->hqk", grad_block, values, preferred_element_type=jnp.float32
        )
        score_grad = (
            block_probs * (prob_grad - jnp.sum(prob_grad * block_probs, axis=-1, keepdims=True))
        ).astype(jnp.bfloat16)
        query_grad = (
            jnp.einsum("hqk,khd->qhd", score_grad, keys_all, preferred_element_type=jnp.float32)
            * score_scale
        )
        key_grad = (
            key_grad
            + jnp.einsum(
                "hqk,qhd->khd", score_grad, query_block, preferred_element_type=jnp.float32
            )
            * score_scale
        )
        return ((key_grad, value_grad), query_grad)

    zero_keys = jnp.zeros(keys_all.shape, jnp.float32)
    (key_grad, value_grad), query_grad = lax.scan(
        one_block,
        (zero_keys, zero_keys),
        (queries.reshape(shape_blocks), grad_out.reshape(shape_blocks), logsum, starts),
    )
    return (query_grad.reshape(queries.shape), key_grad, value_grad)


def gate_up_forward(activations, weight_in, weight_out):
    raised = jnp.einsum(
        "rekd,edcf->rekcf", activations, weight_in, preferred_element_type=jnp.float32
    )
    hidden = (jax.nn.silu(raised[..., 0, :]) * raised[..., 1, :]).astype(jnp.bfloat16)
    result = jnp.einsum("rekf,efd->rekd", hidden, weight_out, preferred_element_type=jnp.float32)
    return (raised, hidden, result)


def gate_up_back(activations, weight_in, weight_out, raised, hidden, incoming):
    out_grad = jnp.einsum("rekf,rekd->efd", hidden, incoming, preferred_element_type=jnp.float32)
    hidden_grad = jnp.einsum(
        "rekd,efd->rekf", incoming, weight_out, preferred_element_type=jnp.float32
    )
    gate_part = raised[..., 0, :]
    up_part = raised[..., 1, :]
    sigmoid_gate = jax.nn.sigmoid(gate_part)
    gate_grad = (
        hidden_grad * up_part * sigmoid_gate * (1.0 + gate_part * (1.0 - sigmoid_gate))
    ).astype(jnp.bfloat16)
    up_grad = (hidden_grad * gate_part * sigmoid_gate).astype(jnp.bfloat16)
    gate_wgrad = jnp.einsum(
        "rekd,rekf->edf", activations, gate_grad, preferred_element_type=jnp.float32
    )
    up_wgrad = jnp.einsum(
        "rekd,rekf->edf", activations, up_grad, preferred_element_type=jnp.float32
    )
    both_grad = jnp.stack([gate_grad, up_grad], axis=-2)
    row_grad = jnp.einsum(
        "rekcf,edcf->rekd", both_grad, weight_in, preferred_element_type=jnp.float32
    )
    return (gate_wgrad, up_wgrad, out_grad, row_grad)


def local_exchange(
    tokens,
    first_gain,
    attention_in,
    attention_bias,
    attention_out,
    second_gain,
    router,
    shared_gate,
    shared_in,
    shared_out,
    expert_in,
    expert_out,
    cotangent,
    expert_picks,
):
    local_rows, model_width = tokens.shape
    shard_count = lax.axis_size(SHARD)
    owner_count = lax.axis_size(EXPERT)
    seq_length = local_rows * shard_count
    expert_count = router.shape[1]
    pick_count = expert_picks.shape[1]
    owned_count = expert_in.shape[0]
    capacity = max(2, 2 * local_rows * pick_count // expert_count)
    heads_here = attention_bias.shape[1]
    head_dim = attention_bias.shape[2] * owner_count
    score_scale = head_dim ** (-0.5)
    block_rows = min(seq_length, 512)
    cosine_table, sine_table = rope_tables(seq_length, head_dim)

    def fetch_dense():
        return (
            lax.all_gather(attention_in, EXPERT, axis=0, tiled=True),
            lax.all_gather(attention_bias, EXPERT, axis=2, tiled=True),
            lax.all_gather(attention_out, EXPERT, axis=1, tiled=True),
            lax.all_gather(router, EXPERT, axis=0, tiled=True),
            lax.all_gather(shared_gate, EXPERT, axis=0, tiled=True),
            lax.all_gather(shared_in, EXPERT, axis=0, tiled=True),
            lax.all_gather(shared_out, EXPERT, axis=1, tiled=True),
        )

    def fetch_rows(normed_low):
        return (
            lax.all_gather(normed_low, SHARD, axis=0, tiled=True),
            lax.all_gather(expert_in, SHARD, axis=3, tiled=True),
            lax.all_gather(expert_out, SHARD, axis=1, tiled=True),
        )

    inputs = tokens.astype(jnp.float32)
    first_norm, first_factor = normalize(inputs)
    first_low = (first_norm * first_gain).astype(jnp.bfloat16)
    att_in, att_bias, att_out, router_full, gate_full, shared_inw, shared_outw = fetch_dense()
    normed_all, expert_inw, expert_outw = fetch_rows(first_low)
    projected = jnp.einsum("sd,dcf->scf", normed_all, att_in, preferred_element_type=jnp.float32)
    projected = projected + att_bias.reshape(3, -1).astype(jnp.float32)[None]
    projected = projected.reshape(seq_length, 3, heads_here, head_dim)
    queries = rotate(projected[:, 0], cosine_table, sine_table).astype(jnp.bfloat16)
    keys_all = rotate(projected[:, 1], cosine_table, sine_table).astype(jnp.bfloat16)
    values = projected[:, 2].astype(jnp.bfloat16)
    attended, logsum = attend(queries, keys_all, values, block_rows, score_scale)
    attended_low = attended.astype(jnp.bfloat16).reshape(seq_length, -1)
    attn_part = jnp.dot(attended_low, att_out, preferred_element_type=jnp.float32)
    attn_local = lax.psum_scatter(
        attn_part.astype(jnp.bfloat16), SHARD, scatter_dimension=0, tiled=True
    ).astype(jnp.float32)
    residual = inputs + attn_local
    second_norm, second_factor = normalize(residual)
    second_low = (second_norm * second_gain).astype(jnp.bfloat16)
    logits = jnp.dot(second_low, router_full, preferred_element_type=jnp.float32)
    route_probs = jax.nn.softmax(logits, axis=-1)
    picked = (
        expert_picks[:, :, None] == jnp.arange(expert_count, dtype=jnp.int32)[None, None, :]
    ).astype(jnp.float32)
    gate_values = jnp.sum(picked * route_probs[:, None, :], axis=-1)
    flat_picks = expert_picks.reshape(-1)
    flat_hot = (flat_picks[:, None] == jnp.arange(expert_count, dtype=jnp.int32)[None, :]).astype(
        jnp.int32
    )
    slot_ranks = jnp.sum((jnp.cumsum(flat_hot, axis=0) - flat_hot) * flat_hot, axis=1)
    slot_rows = flat_picks * capacity + slot_ranks
    outgoing = jnp.zeros((expert_count * capacity, model_width), jnp.bfloat16)
    outgoing = outgoing.at[slot_rows].set(jnp.repeat(second_low, pick_count, axis=0))
    arrived = lax.all_to_all(
        outgoing.reshape(owner_count, owned_count, capacity, model_width),
        EXPERT,
        split_axis=0,
        concat_axis=0,
        tiled=True,
    )
    mixed_all = lax.all_gather(second_low, SHARD, axis=0, tiled=True)
    shared_raised, shared_hidden, shared_part = gate_up_forward(
        mixed_all[:, None, None, :], shared_inw[None], shared_outw[None]
    )
    shared_rows = lax.psum_scatter(
        shared_part[:, 0, 0, :].astype(jnp.bfloat16), SHARD, scatter_dimension=0, tiled=True
    ).astype(jnp.float32)
    expert_raised, expert_hidden, expert_part = gate_up_forward(arrived, expert_inw, expert_outw)
    expert_result = expert_part.astype(jnp.bfloat16)
    shared_scale = jax.nn.sigmoid(
        jnp.dot(second_low, gate_full, preferred_element_type=jnp.float32)
    )
    out_grad = cotangent.astype(jnp.float32)
    slot_values = (
        (gate_values[:, :, None] * out_grad[:, None, :])
        .reshape(-1, model_width)
        .astype(jnp.bfloat16)
    )
    grad_send = (
        jnp.zeros((expert_count * capacity, model_width), jnp.bfloat16)
        .at[slot_rows]
        .set(slot_values)
    )
    returned, owner_grads = (
        lax.all_to_all(expert_result, EXPERT, split_axis=0, concat_axis=0, tiled=True),
        lax.all_to_all(
            grad_send.reshape(owner_count, owned_count, capacity, model_width),
            EXPERT,
            split_axis=0,
            concat_axis=0,
            tiled=True,
        ),
    )
    gathered_out = returned.reshape(expert_count * capacity, model_width)[slot_rows]
    gathered_out = gathered_out.reshape(local_rows, pick_count, model_width).astype(jnp.float32)
    routed = jnp.sum(gate_values[:, :, None] * gathered_out, axis=1)
    output = (residual + shared_scale[:, None] * shared_rows + routed).astype(jnp.bfloat16)
    pick_grad = jnp.sum(out_grad[:, None, :] * gathered_out, axis=-1)
    route_grad = jnp.sum(picked * pick_grad[:, :, None], axis=1)
    logit_grad = (
        route_probs * (route_grad - jnp.sum(route_grad * route_probs, axis=-1, keepdims=True))
    ).astype(jnp.bfloat16)
    scale_grad = jnp.sum(out_grad * shared_rows, axis=-1)
    gate_logit_grad = (scale_grad * shared_scale * (1.0 - shared_scale)).astype(jnp.bfloat16)
    shared_grad = (shared_scale[:, None] * out_grad).astype(jnp.bfloat16)
    shared_grad_all, logit_grad_all, gate_grad_all = (
        lax.all_gather(shared_grad, SHARD, axis=0, tiled=True),
        lax.all_gather(logit_grad, SHARD, axis=0, tiled=True),
        lax.all_gather(gate_logit_grad, SHARD, axis=0, tiled=True),
    )
    att_in, att_bias, att_out, router_full, gate_full, shared_inw, shared_outw = fetch_dense()
    normed_all, expert_inw, expert_outw = fetch_rows(first_low)
    expert_gate_w, expert_up_w, expert_down_w, owner_row_grad = gate_up_back(
        arrived, expert_inw, expert_outw, expert_raised, expert_hidden, owner_grads
    )
    shared_gate_w, shared_up_w, shared_down_w, shared_row_grad = gate_up_back(
        mixed_all[:, None, None, :],
        shared_inw[None],
        shared_outw[None],
        shared_raised,
        shared_hidden,
        shared_grad_all[:, None, None, :],
    )
    owner_low = owner_row_grad.astype(jnp.bfloat16)
    shared_back = lax.psum_scatter(
        shared_row_grad[:, 0, 0, :].astype(jnp.bfloat16), SHARD, scatter_dimension=0, tiled=True
    ).astype(jnp.float32)
    returned_grad = lax.all_to_all(owner_low, EXPERT, split_axis=0, concat_axis=0, tiled=True)
    routed_back = returned_grad.reshape(expert_count * capacity, model_width)[slot_rows]
    routed_back = jnp.sum(
        routed_back.reshape(local_rows, pick_count, model_width).astype(jnp.float32), axis=1
    )
    local_back = jnp.einsum(
        "te,de->td", logit_grad, router_full, preferred_element_type=jnp.float32
    )
    local_back = (
        local_back
        + gate_logit_grad.astype(jnp.float32)[:, None] * gate_full.astype(jnp.float32)[None, :]
    )
    second_grad = local_back + shared_back + routed_back
    residual_back, second_gain_grad = norm_back(
        second_grad, second_norm, second_factor, second_gain
    )
    residual_grad = out_grad + residual_back
    residual_all = lax.all_gather(residual_grad.astype(jnp.bfloat16), SHARD, axis=0, tiled=True)
    att_out_grad = jnp.einsum(
        "sf,sd->fd", attended_low, residual_all, preferred_element_type=jnp.float32
    )
    attended_grad = jnp.einsum(
        "sd,fd->sf", residual_all, att_out, preferred_element_type=jnp.float32
    )
    attended_grad = attended_grad.astype(jnp.bfloat16).reshape(seq_length, heads_here, head_dim)
    query_grad, key_grad, value_grad = attend_back(
        queries, keys_all, values, logsum, attended_grad, block_rows, score_scale
    )
    projected_grad = jnp.stack(
        [
            rotate_back(query_grad, cosine_table, sine_table),
            rotate_back(key_grad, cosine_table, sine_table),
            value_grad,
        ],
        axis=1,
    )
    projected_grad = projected_grad.astype(jnp.bfloat16).reshape(
        seq_length, 3, heads_here * head_dim
    )
    att_in_grad = jnp.einsum(
        "sd,scf->dcf", normed_all, projected_grad, preferred_element_type=jnp.float32
    )
    att_bias_grad = jnp.sum(projected_grad.astype(jnp.float32), axis=0).reshape(
        3, heads_here, head_dim
    )
    first_part = jnp.einsum(
        "scf,dcf->sd", projected_grad, att_in, preferred_element_type=jnp.float32
    )
    first_grad, expert_gate_l, expert_up_l, expert_down_l = (
        lax.psum_scatter(
            first_part.astype(jnp.bfloat16), SHARD, scatter_dimension=0, tiled=True
        ).astype(jnp.float32),
        lax.psum_scatter(
            expert_gate_w.astype(jnp.bfloat16), SHARD, scatter_dimension=2, tiled=True
        ).astype(jnp.float32),
        lax.psum_scatter(
            expert_up_w.astype(jnp.bfloat16), SHARD, scatter_dimension=2, tiled=True
        ).astype(jnp.float32),
        lax.psum_scatter(
            expert_down_w.astype(jnp.bfloat16), SHARD, scatter_dimension=1, tiled=True
        ).astype(jnp.float32),
    )
    input_back, first_gain_grad = norm_back(first_grad, first_norm, first_factor, first_gain)
    input_grad = residual_grad + input_back
    router_grad = jnp.einsum(
        "sd,se->de", mixed_all, logit_grad_all, preferred_element_type=jnp.float32
    )
    gate_vec_grad = jnp.einsum(
        "sd,s->d", mixed_all, gate_grad_all, preferred_element_type=jnp.float32
    )
    shared_in_grad = jnp.stack([shared_gate_w[0], shared_up_w[0]], axis=1)
    (
        att_in_local,
        att_bias_local,
        att_out_local,
        router_local,
        gate_vec_local,
        shared_in_local,
        shared_out_local,
    ) = (
        lax.psum_scatter(
            att_in_grad.astype(jnp.bfloat16), EXPERT, scatter_dimension=0, tiled=True
        ).astype(jnp.float32),
        lax.psum_scatter(
            att_bias_grad.astype(jnp.bfloat16), EXPERT, scatter_dimension=2, tiled=True
        ).astype(jnp.float32),
        lax.psum_scatter(
            att_out_grad.astype(jnp.bfloat16), EXPERT, scatter_dimension=1, tiled=True
        ).astype(jnp.float32),
        lax.psum_scatter(
            router_grad.astype(jnp.bfloat16), EXPERT, scatter_dimension=0, tiled=True
        ).astype(jnp.float32),
        lax.psum_scatter(
            gate_vec_grad.astype(jnp.bfloat16), EXPERT, scatter_dimension=0, tiled=True
        ).astype(jnp.float32),
        lax.psum_scatter(
            shared_in_grad.astype(jnp.bfloat16), EXPERT, scatter_dimension=0, tiled=True
        ).astype(jnp.float32),
        lax.psum_scatter(
            shared_down_w[0].astype(jnp.bfloat16), EXPERT, scatter_dimension=1, tiled=True
        ).astype(jnp.float32),
    )
    first_gain_all, second_gain_all = lax.psum(
        (first_gain_grad, second_gain_grad), (EXPERT, SHARD)
    )
    expert_in_grad = jnp.stack([expert_gate_l, expert_up_l], axis=2)
    return (
        output,
        input_grad,
        first_gain_all,
        att_in_local,
        att_bias_local,
        att_out_local,
        second_gain_all,
        router_local,
        gate_vec_local,
        shared_in_local,
        shared_out_local,
        expert_in_grad,
        expert_down_l,
    )


MESH = pl.DeviceIdType.MESH
EXTRA = 128
NT_DIMS = (((1,), (1,)), ((), ()))


class Place:
    def __init__(self):
        e, s = lax.axis_index(EXPERT), lax.axis_index(SHARD)
        self.z, self.x, self.y, self.c = e // 2, e % 2, s // 2, s % 2

    def z_of(self, kz):
        z = self.z
        return (z, z + 1 - 2 * (z % 2), (z + 2) % 4, 3 - z)[kz]

    def x_of(self, kx):
        return (self.x, 1 - self.x)[kx]

    def y_of(self, ky):
        return (self.y, 1 - self.y)[ky]

    def c_of(self, kc):
        return (self.c, 1 - self.c)[kc]

    def device(self, kz=0, kx=0, ky=0, kc=0):
        return (self.z_of(kz) * 2 + self.x_of(kx), self.y_of(ky) * 2 + self.c_of(kc))

    def sequence(self, kz, kx):
        return self.z_of(kz) * 2 + self.x_of(kx)

    def block(self, kz, kx, ky, kc):
        return self.sequence(kz, kx) * 4 + self.y_of(ky) * 2 + self.c_of(kc)


PARTNERS = [dict(kz=1), dict(kz=2), dict(kz=3), dict(kx=1), dict(ky=1), dict(kc=1)]
FARTHER = [dict(kz=1, kx=1), dict(kz=2, kx=1), dict(kz=3, kx=1)]


def greet(place, partners):
    barrier = pltpu.get_barrier_semaphore()
    for partner in partners:
        pl.semaphore_signal(
            barrier, inc=1, device_id=place.device(**partner), device_id_type=MESH
        )
    pl.semaphore_wait(barrier, len(partners))


class Copies:
    def __init__(self, place, send_sems, recv_sems):
        self.place, self.send_sems, self.recv_sems = place, send_sems, recv_sems
        self.made = {}

    def start(self, name, source, target, **partner):
        at = len(self.made)
        copy = pltpu.make_async_remote_copy(
            src_ref=source,
            dst_ref=target,
            send_sem=self.send_sems.at[at],
            recv_sem=self.recv_sems.at[at],
            device_id=self.place.device(**partner),
            device_id_type=MESH,
        )
        copy.start()
        self.made[name] = copy

    def arrived(self, name):
        self.made[name].wait_recv()

    def sent(self, name):
        self.made[name].wait_send()


GATHER_COPIES = 55
SUM_COPIES = 43


class Gather:
    def __init__(self, place, copies, block_ref, all_ref, rows):
        self.place, self.copies = place, copies
        self.block_ref, self.all_ref, self.rows = block_ref, all_ref, rows

    def view(self, kz, kx, ky, piece, own=False):
        half = self.rows // 2
        first = 0 if piece in (None, 0) else half
        count = self.rows if piece is None else half
        if own and (kz, kx, ky) == (0, 0, 0):
            return self.block_ref.at[pl.ds(first, count)]
        start = self.place.block(kz, kx, ky, 0) * self.rows + first
        return self.all_ref.at[pl.ds(pl.multiple_of(start, half), count)]

    def send(self, name, from_z, from_x, from_y, piece, **partner):
        self.copies.start(
            name,
            self.view(from_z, from_x, from_y, piece, own=True),
            self.view(from_z, from_x, from_y, piece),
            **partner,
        )

    def begin(self, kz):
        self.send(("z", kz), 0, 0, 0, None, kz=kz)

    def first(self, kz):
        if kz:
            self.copies.arrived(("z", kz))
        self.send(("y0", kz, 0), kz, 0, 0, 0, ky=1)
        self.send(("y1", kz), kz, 0, 0, 1, ky=1)
        self.send(("x0", kz), kz, 0, 0, 0, kx=1)
        self.send(("x1", kz, 0), kz, 0, 0, 1, kx=1)
        self.send(("c", kz), kz, 0, 0, None, kc=1)

    def second_y(self, kz):
        self.copies.arrived(("y1", kz))
        self.send(("x1", kz, 1), kz, 0, 1, 1, kx=1)
        self.send(("c01", kz), kz, 0, 1, 1, kc=1)
        self.copies.arrived(("y0", kz, 0))
        self.send(("c00", kz), kz, 0, 1, 0, kc=1)

    def second_x(self, kz):
        self.copies.arrived(("x0", kz))
        self.send(("y0", kz, 1), kz, 1, 0, 0, ky=1)
        self.send(("c10", kz), kz, 1, 0, 0, kc=1)
        self.copies.arrived(("x1", kz, 0))
        self.send(("c11", kz), kz, 1, 0, 1, kc=1)

    def third(self, kz):
        self.copies.arrived(("y0", kz, 1))
        self.send(("c20", kz), kz, 1, 1, 0, kc=1)
        self.copies.arrived(("x1", kz, 1))
        self.send(("c21", kz), kz, 1, 1, 1, kc=1)

    def have(self, kz, kx):
        for name in ("c10", "c11", "c20", "c21") if kx else ("c", "c00", "c01"):
            self.copies.arrived((name, kz))


class Sums:
    def __init__(self, place, copies, tag, held, from_y0, from_y1, from_x0, from_x1, from_z):
        self.place, self.copies, self.tag, self.held = place, copies, tag, held
        self.from_y0, self.from_y1 = from_y0, from_y1
        self.from_x0, self.from_x1, self.from_z = from_x0, from_x1, from_z
        self.rows = held.shape[1]
        self.half = self.rows // 2

    def slot(self, kz, kx, ky, piece=None):
        at = kz * 4 + kx * 2 + ky
        if piece is None:
            return self.held.at[at]
        return self.held.at[at, pl.ds(piece * self.half, self.half)]

    def staged_part(self, staged):
        def view(ky, kc):
            start = (self.place.y_of(ky) * 2 + self.place.c_of(kc)) * self.rows
            return staged.at[pl.ds(pl.multiple_of(start, self.rows), self.rows)]

        return view

    def add(self, into, other):
        into[...] = into[...] + other[...]

    def cores(self, kz, kx, part):
        for ky in (1, 0):
            self.copies.start((SUM_CORES, self.tag, kz, kx, ky), part(ky, 1), self.slot(kz, kx, ky), kc=1)

    def first(self, kz, kx, part):
        for ky in (1, 0):
            self.copies.arrived((SUM_CORES, self.tag, kz, kx, ky))
            self.add(self.slot(kz, kx, ky), part(ky, 0))
            if ky:
                self.copies.start(
                    ("sy0", self.tag, kz, kx), self.slot(kz, kx, 1, 0), self.from_y0.at[kz * 2 + kx], ky=1
                )
            if kx:
                self.copies.start(
                    ("sx1", self.tag, kz, ky), self.slot(kz, 1, ky, 1), self.from_x1.at[kz * 2 + ky], kx=1
                )
        for ky in (1, 0):
            self.copies.sent((SUM_CORES, self.tag, kz, kx, ky))

    def second_away(self, kz):
        self.copies.arrived(("sy0", self.tag, kz, 1))
        self.add(self.slot(kz, 1, 0, 0), self.from_y0.at[kz * 2 + 1])
        self.copies.start(("sx0", self.tag, kz), self.slot(kz, 1, 0, 0), self.from_x0.at[kz], kx=1)

    def second_here(self, kz):
        self.copies.arrived(("sx1", self.tag, kz, 1))
        self.add(self.slot(kz, 0, 1, 1), self.from_x1.at[kz * 2 + 1])
        self.copies.start(("sy1", self.tag, kz), self.slot(kz, 0, 1, 1), self.from_y1.at[kz], ky=1)
        self.copies.arrived(("sx1", self.tag, kz, 0))
        self.add(self.slot(kz, 0, 0, 1), self.from_x1.at[kz * 2])
        self.copies.arrived(("sy0", self.tag, kz, 0))
        self.add(self.slot(kz, 0, 0, 0), self.from_y0.at[kz * 2])
        self.copies.arrived(("sx0", self.tag, kz))
        self.add(self.slot(kz, 0, 0, 0), self.from_x0.at[kz])

    def third(self, kz):
        self.copies.arrived(("sy1", self.tag, kz))
        self.add(self.slot(kz, 0, 0, 1), self.from_y1.at[kz])
        if kz:
            self.copies.start(("sz", self.tag, kz), self.slot(kz, 0, 0), self.from_z.at[kz - 1], kz=kz)

    def total(self):
        total = self.slot(0, 0, 0)[...].astype(jnp.float32)
        for kz in (1, 2, 3):
            self.copies.arrived(("sz", self.tag, kz))
            total = total + self.from_z.at[kz - 1][...].astype(jnp.float32)
        return total


def mixture_kernel(
    sizes,
    block_ref,
    cot_ref,
    expert_in_ref,
    shared_in_ref,
    expert_out_ref,
    shared_out_ref,
    select_ref,
    place_ref,
    residual_ref,
    output_ref,
    sum_ref,
    rows_ref,
    units_ref,
    weight_in,
    weight_out,
    rows_buf,
    cot_buf,
    units_buf,
    dots,
    staged_out,
    staged_back,
    *rest,
):
    rows, seq, width, owned, part, shared_part, padded = sizes
    out_slots, back_slots = rest[:6], rest[6:12]
    send_sems, recv_sems, load_sems, misc_sems = rest[12:]
    bf16, f32 = jnp.bfloat16, jnp.float32
    place = Place()
    copies = Copies(place, send_sems, recv_sems)
    gather = Gather(place, copies, block_ref, rows_ref, rows)
    sums_out = Sums(place, copies, 0, *out_slots)
    sums_back = Sums(place, copies, 1, *back_slots)
    both = (sums_out, sums_back)

    own = pltpu.make_async_copy(block_ref, gather.view(0, 0, 0, None), misc_sems.at[0])
    own.start()
    moves = []
    for c in (0, 1):
        for e in range(owned):
            moves.append(
                (
                    expert_in_ref.at[pl.ds((2 * e + c) * part, part)],
                    weight_in.at[pl.ds(c * padded + e * part, part)],
                )
            )
        moves.append(
            (
                shared_in_ref.at[pl.ds(c * shared_part, shared_part)],
                weight_in.at[pl.ds(c * padded + owned * part, shared_part)],
            )
        )
    moves.append((expert_out_ref, weight_out.at[pl.ds(0, owned * part)]))
    moves.append((shared_out_ref, weight_out.at[pl.ds(owned * part, shared_part)]))
    loads = [
        pltpu.make_async_copy(source, target, load_sems.at[i])
        for i, (source, target) in enumerate(moves)
    ]
    for load in loads:
        load.start()

    order = [(0, 1), (1, 1), (1, 0), (2, 1), (2, 0), (3, 1), (3, 0), (0, 0)]

    def span(step):
        return pl.ds(pl.multiple_of(place.sequence(*order[step]) * seq, seq), seq)

    def rows_load(step):
        return pltpu.make_async_copy(rows_ref.at[span(step)], rows_buf, misc_sems.at[1])

    def cot_load(step):
        return pltpu.make_async_copy(cot_ref.at[span(step)], cot_buf, misc_sems.at[2])

    def units_write(step):
        return pltpu.make_async_copy(units_buf, units_ref.at[span(step)], misc_sems.at[3])

    cot_load(0).start()
    greet(place, PARTNERS)
    gather.first(0)
    gather.begin(1)
    used = owned * part + shared_part
    for at in (used, padded + used):
        weight_in[pl.ds(at, padded - used), :] = jnp.zeros((padded - used, width), bf16)
    weight_out[pl.ds(used, padded - used), :] = jnp.zeros((padded - used, width), bf16)
    gather.second_x(0)
    gather.second_y(0)
    gather.begin(2)
    gather.third(0)
    gather.first(1)
    own.wait()
    gather.have(0, 1)
    rows_load(0).start()
    for load in loads:
        load.wait()

    def raise_tile(at, count):
        here, above = pl.ds(at, count), pl.ds(at + padded, count)
        pair = jnp.concatenate([weight_in[here, :], weight_in[above, :]], axis=0)
        raised = lax.dot_general(
            rows_buf[:, pl.ds(0, width)], pair, NT_DIMS, preferred_element_type=f32
        )
        back = lax.dot_general(
            cot_buf[...], weight_out[here, :], NT_DIMS, preferred_element_type=f32
        )
        scale = jnp.dot(
            rows_buf[:, pl.ds(width, EXTRA)], select_ref[:, here], preferred_element_type=f32
        )
        gate, up = raised[:, :count], raised[:, count:]
        sigmoid_gate = jax.nn.sigmoid(gate)
        active = gate * sigmoid_gate
        hidden = active * up
        dots[...] += jnp.dot(
            (back * hidden).astype(bf16), place_ref[here, :], preferred_element_type=f32
        )
        scaled = back * scale
        units_buf[:, pl.ds(at + 2 * padded, count)] = (hidden * scale).astype(bf16)
        units_buf[:, here] = (
            scaled * up * sigmoid_gate * (1.0 + gate * (1.0 - sigmoid_gate))
        ).astype(bf16)
        units_buf[:, above] = (scaled * active).astype(bf16)

    tile, wide = 256, 512

    def raise_and_back():
        dots[...] = jnp.zeros_like(dots)

        @pl.loop(0, padded // tile)
        def _(j):
            raise_tile(pl.multiple_of(j * tile, tile), tile)

        if padded % tile:
            raise_tile(padded // tile * tile, padded % tile)

    def project_out():
        @pl.loop(0, width // wide)
        def _(n):
            at = pl.ds(pl.multiple_of(n * wide, wide), wide)
            staged_out[:, at] = jnp.dot(
                units_buf[:, pl.ds(2 * padded, padded)],
                weight_out[:, at],
                preferred_element_type=f32,
            ).astype(bf16)

    def project_back():
        @pl.loop(0, width // wide)
        def _(n):
            at = pl.ds(pl.multiple_of(n * wide, wide), wide)
            staged_back[:, at] = jnp.dot(
                units_buf[:, pl.ds(0, 2 * padded)], weight_in[:, at], preferred_element_type=f32
            ).astype(bf16)

        staged_back[:, pl.ds(width, EXTRA)] = dots[...].astype(bf16)

    def sums_first(done):
        sums_out.first(*order[done], sums_out.staged_part(staged_out))
        sums_back.first(*order[done], sums_back.staged_part(staged_back))

    def second_gather(kz):
        gather.second_y(kz)
        gather.second_x(kz)

    def next_rows(step):
        if step + 1 < len(order):
            gather.have(*order[step + 1])
            rows_load(step + 1).start()

    def after_raise(step):
        if step:
            sums_first(step - 1)
        if step == 0:
            second_gather(1)
            gather.begin(3)
        elif step == 1:
            gather.first(2)
        elif step == 2:
            gather.third(2)
            gather.first(3)
            for sums in both:
                sums.second_away(0)
        elif step == 3:
            second_gather(3)
            for sums in both:
                sums.second_away(1)
        elif step == 4:
            gather.third(3)
            for sums in both:
                sums.second_here(1)
        elif step == 5:
            for sums in both:
                sums.second_away(2)
            for sums in both:
                sums.third(1)
        elif step == 6:
            for sums in both:
                sums.second_here(2)
        elif step == 7:
            for sums in both:
                sums.second_away(3)
            for sums in both:
                sums.third(2)

    def after_out(step):
        if step == 0:
            gather.third(1)
        else:
            next_rows(step)

    def after_back(step):
        if step == 0:
            next_rows(step)
        elif step == 1:
            second_gather(2)
        elif step == 7:
            for sums in both:
                sums.second_here(3)

    for step in range(len(order)):
        rows_load(step).wait()
        cot_load(step).wait()
        if step:
            units_write(step - 1).wait()
        raise_and_back()
        units_write(step).start()
        if step + 1 < len(order):
            cot_load(step + 1).start()
        after_raise(step)
        project_out()
        sums_out.cores(*order[step], sums_out.staged_part(staged_out))
        after_out(step)
        project_back()
        sums_back.cores(*order[step], sums_back.staged_part(staged_back))
        after_back(step)
    last = len(order) - 1
    sums_first(last)
    for sums in both:
        sums.third(3)
    for sums in both:
        sums.second_here(0)
    for sums in both:
        sums.third(0)
    output_ref[...] = (residual_ref[...] + sums_out.total()).astype(bf16)
    sum_ref[...] = sums_back.total()
    units_write(last).wait()
    for name in copies.made:
        if name[0] != SUM_CORES:
            copies.sent(name)


def sum_slots(rows, packed):
    half = rows // 2
    bf16 = jnp.bfloat16
    return [
        pltpu.VMEM((16, rows, packed), bf16),
        pltpu.VMEM((8, half, packed), bf16),
        pltpu.VMEM((4, half, packed), bf16),
        pltpu.VMEM((4, half, packed), bf16),
        pltpu.VMEM((8, half, packed), bf16),
        pltpu.VMEM((3, rows, packed), bf16),
    ]


def mixture(
    row_pack, cot_all, expert_in, shared_win, expert_out, shared_wout, select, spots, residual
):
    rows, packed = row_pack.shape
    width = packed - EXTRA
    total_rows = cot_all.shape[0]
    owned, part = expert_out.shape[0], expert_out.shape[1]
    shared_part = shared_wout.shape[0]
    seq = total_rows // lax.axis_size(EXPERT)
    padded = select.shape[1]
    bf16, f32 = jnp.bfloat16, jnp.float32
    vmem = pl.BlockSpec(memory_space=pltpu.VMEM)
    anywhere = pl.BlockSpec(memory_space=pl.ANY)
    copies = GATHER_COPIES + 2 * SUM_COPIES
    return pl.pallas_call(
        functools.partial(
            mixture_kernel, (rows, seq, width, owned, part, shared_part, padded)
        ),
        out_shape=(
            jax.ShapeDtypeStruct((rows, width), bf16),
            jax.ShapeDtypeStruct((rows, packed), f32),
            jax.ShapeDtypeStruct((total_rows, packed), bf16),
            jax.ShapeDtypeStruct((total_rows, 3 * padded), bf16),
        ),
        in_specs=[anywhere] * 6 + [vmem] * 3,
        out_specs=(vmem,) * 2 + (anywhere,) * 2,
        scratch_shapes=[
            pltpu.VMEM((2 * padded, width), bf16),
            pltpu.VMEM((padded, width), bf16),
            pltpu.VMEM((seq, packed), bf16),
            pltpu.VMEM((seq, width), bf16),
            pltpu.VMEM((seq, 3 * padded), bf16),
            pltpu.VMEM((seq, EXTRA), f32),
            pltpu.VMEM((seq, width), bf16),
            pltpu.VMEM((seq, packed), bf16),
        ]
        + sum_slots(rows, width)
        + sum_slots(rows, packed)
        + [
            pltpu.SemaphoreType.DMA((copies,)),
            pltpu.SemaphoreType.DMA((copies,)),
            pltpu.SemaphoreType.DMA((2 * owned + 4,)),
            pltpu.SemaphoreType.DMA((4,)),
        ],
        compiler_params=pltpu.CompilerParams(
            collective_id=0, has_side_effects=True, vmem_limit_bytes=63 * 2**20
        ),
        cost_estimate=pl.CostEstimate(
            flops=2 * total_rows * width * padded * 6,
            bytes_accessed=100 * 2**20,
            transcendentals=total_rows * padded,
        ),
        name="mixture",
    )(
        row_pack,
        cot_all,
        expert_in.transpose(0, 2, 3, 1).reshape(2 * owned * part, width),
        shared_win,
        expert_out.reshape(owned * part, width),
        shared_wout,
        select,
        spots,
        residual,
    )


class Totals:
    def __init__(self, place, copies, value, from_c, from_y, from_x, by_z):
        self.place, self.copies, self.value = place, copies, value
        self.slots = {CORE: from_c, ROW: from_y, COLUMN: from_x}
        self.by_z = by_z

    def send(self, axis):
        self.copies.start((TOTAL, axis), self.value, self.slots[axis], **{axis: 1})

    def add(self, axis):
        self.copies.arrived((TOTAL, axis))
        self.copies.sent((TOTAL, axis))
        self.value[...] = self.value[...] + self.slots[axis][...]

    def send_z(self):
        mine = self.by_z.at[self.place.z]
        mine[...] = self.value[...]
        for kz in (1, 2, 3):
            self.copies.start(("tz", kz), mine, mine, kz=kz)

    def finish(self):
        for kz in (1, 2, 3):
            self.copies.arrived(("tz", kz))
        by_z = self.by_z
        return (by_z[0] + by_z[1]) + (by_z[2] + by_z[3])


class OwnerSums:
    def __init__(self, place, copies, sources, mine, from_x, from_z, sems):
        self.place, self.copies, self.sources = place, copies, sources
        self.mine, self.from_x, self.from_z, self.sems = mine, from_x, from_z, sems

    def view(self, i, kz, kx):
        width = self.mine[i].shape[-2] if i == 0 else self.mine[i].shape[-1]
        at = pl.ds(pl.multiple_of(self.place.sequence(kz, kx) * width, width), width)
        return self.sources[i].at[:, at]

    def begin(self, kz):
        for i in (0, 1):
            self.copies.start(("ox", i, kz), self.view(i, kz, 1), self.from_x[i].at[kz], kx=1)

    def load(self, kz):
        return [
            pltpu.make_async_copy(
                self.view(i, kz, 0), self.mine[i].at[kz % 2], self.sems.at[2 * (kz % 2) + i]
            )
            for i in (0, 1)
        ]

    def add(self, kz):
        for load in self.load(kz):
            load.wait()
        for i in (0, 1):
            self.copies.arrived(("ox", i, kz))
            held = self.from_x[i].at[kz]
            held[...] = held[...] + self.mine[i][kz % 2]
            if kz:
                self.copies.start(("oz", i, kz), held, self.from_z[i].at[kz - 1], kz=kz)

    def finish(self, i, out_ref):
        total = self.from_x[i][0].astype(jnp.float32)
        for kz in (1, 2, 3):
            self.copies.arrived(("oz", i, kz))
            total = total + self.from_z[i][kz - 1].astype(jnp.float32)
        out_ref[...] = total


CLOSING_COPIES = 14 + 14 + 6


def closing_kernel(
    sizes,
    rows_ref,
    cot_ref,
    units_ref,
    att_in_ref,
    att_out_ref,
    small_ref,
    att_in_out,
    att_out_out,
    small_out,
    expert_in_out,
    expert_out_out,
    shared_in_out,
    shared_out_out,
    chunks,
    turned,
    columns,
    grads,
    shared_in_send,
    shared_out_send,
    own_in,
    own_out,
    in_x,
    out_x,
    in_z,
    out_z,
    small,
    small_c,
    small_y,
    small_x,
    small_z,
    send_sems,
    recv_sems,
    own_sems,
    chunk_sems,
    column_sems,
    write_sems,
    keep_sems,
):
    width, owned, part, shared_part, owner_width, padded = sizes
    f32, bf16 = jnp.float32, jnp.bfloat16
    place = Place()
    copies = Copies(place, send_sems, recv_sems)
    totals = Totals(place, copies, small, small_c, small_y, small_x, small_z)
    owners = OwnerSums(
        place,
        copies,
        (att_in_ref, att_out_ref),
        (own_in, own_out),
        (in_x, out_x),
        (in_z, out_z),
        own_sems,
    )
    wide = 2 * owner_width
    cut = owned * part
    lanes = 128
    per_kind = padded // lanes

    def chunk_load(i, slot):
        at = pl.ds(pl.multiple_of(i * lanes, lanes), lanes)
        return pltpu.make_async_copy(
            units_ref.at[:, at], chunks.at[slot], chunk_sems.at[slot]
        )

    def column_load(kz, which):
        source = (rows_ref, cot_ref)[which]
        at = pl.ds(pl.multiple_of(place.z_of(kz) * wide, wide), wide)
        return pltpu.make_async_copy(source.at[:, at], columns.at[which], column_sems.at[which])

    chunk_load(0, 0).start()
    for load in owners.load(3) + owners.load(2):
        load.start()
    small[...] = small_ref[...]
    greet(place, PARTNERS + FARTHER)
    totals.send(CORE)
    owners.begin(3)
    owners.begin(2)
    column_load(3, 0).start()
    column_load(3, 1).start()

    def turn(kind):
        @pl.loop(kind * per_kind, (kind + 1) * per_kind)
        def _(i):
            slot = i % 2
            chunk_load(i, slot).wait()

            @pl.when(i + 1 < 3 * per_kind)
            def _():
                chunk_load(i + 1, 1 - slot).start()

            to = pl.ds(pl.multiple_of(i * lanes, lanes), lanes)

            @pl.loop(0, turned.shape[1] // wide)
            def _(r):
                at = pl.ds(pl.multiple_of(r * wide, wide), wide)
                turned[to, at] = chunks[slot, at, :].T

    def owners_add(kz):
        owners.add(kz)
        if kz >= 2:
            for load in owners.load(kz - 2):
                load.start()
            owners.begin(kz - 2)

    def span(kz):
        return pl.ds(pl.multiple_of(place.z_of(kz) * wide, wide), wide)

    def writes(kz, kind):
        found = []
        for e in range(owned):
            if kind < 2:
                target = expert_in_out.at[pl.ds((2 * e + kind) * part, part), span(kz)]
            else:
                target = expert_out_out.at[pl.ds(e * part, part), span(kz)]
            found.append(
                pltpu.make_async_copy(
                    grads.at[kind, pl.ds(e * part, part)], target, write_sems.at[kind * owned + e]
                )
            )
        return found

    def share(kz, which):
        sent = (shared_in_send, shared_out_send)[which]
        target = (shared_in_out, shared_out_out)[which].at[place.sequence(0, 0)]
        for kx in (1, 0):
            at = pl.ds(pl.multiple_of(place.x_of(kx) * owner_width, owner_width), owner_width)
            source = sent.at[kz, :, at]
            if kz or kx:
                copies.start((SHARE, which, kz, kx), source, target, kz=kz, kx=kx)
            else:
                pltpu.make_async_copy(source, target, keep_sems.at[which]).start()

    def product(kz, kind):
        which = kind // 2
        if kind != 1:
            column_load(kz, which).wait()
        if kz < 3:
            for write in writes(kz + 1, kind):
                write.wait()

        @pl.loop(0, 2)
        def _(n):
            at = pl.ds(pl.multiple_of(n * owner_width, owner_width), owner_width)
            grads[kind, :, at] = jnp.dot(
                turned[pl.ds(kind * padded, padded), :],
                columns[which, :, at],
                preferred_element_type=f32,
            ).astype(bf16)

        if kz and kind:
            column_load(kz - 1, which).start()
        for write in writes(kz, kind):
            write.start()
        shared = grads[kind, pl.ds(cut, shared_part), :]
        if kind < 2:
            shared_in_send[kz, pl.ds(kind * shared_part, shared_part), :] = shared
        else:
            shared_out_send[kz] = shared
        if kind:
            share(kz, which)

    turn(0)
    totals.add(CORE)
    totals.send(ROW)
    turn(1)
    owners_add(3)
    turn(2)
    totals.add(ROW)
    totals.send(COLUMN)
    product(3, 0)
    product(3, 1)
    owners_add(2)
    product(3, 2)
    totals.add(COLUMN)
    totals.send_z()
    product(2, 0)
    product(2, 1)
    product(2, 2)
    owners_add(1)
    product(1, 0)
    product(1, 1)
    product(1, 2)
    owners_add(0)
    product(0, 0)
    product(0, 1)
    product(0, 2)
    small_out[...] = totals.finish()
    owners.finish(0, att_in_out)
    owners.finish(1, att_out_out)
    for kind in (0, 1, 2):
        for write in writes(0, kind):
            write.wait()
    for which in (0, 1):
        sent = (shared_in_send, shared_out_send)[which]
        target = (shared_in_out, shared_out_out)[which].at[place.sequence(0, 0)]
        at = pl.ds(pl.multiple_of(place.x_of(0) * owner_width, owner_width), owner_width)
        pltpu.make_async_copy(sent.at[0, :, at], target, keep_sems.at[which]).wait()
    for name in copies.made:
        if name[0] == SHARE:
            copies.arrived(name)
    for name in copies.made:
        if name[0] != TOTAL:
            copies.sent(name)


def closing(rows_all, cot_all, units_all, att_in, att_out, small, owned, part, shared_part):
    total_rows, width = cot_all.shape
    padded = units_all.shape[1] // 3
    owners = lax.axis_size(EXPERT)
    owner_width = width // owners
    wide = 2 * owner_width
    heads_width = att_in.shape[2]
    bf16, f32 = jnp.bfloat16, jnp.float32
    vmem = pl.BlockSpec(memory_space=pltpu.VMEM)
    anywhere = pl.BlockSpec(memory_space=pl.ANY)
    block_in = (3, owner_width, heads_width)
    block_out = (heads_width, owner_width)
    return pl.pallas_call(
        functools.partial(
            closing_kernel, (width, owned, part, shared_part, owner_width, padded)
        ),
        out_shape=(
            jax.ShapeDtypeStruct(block_in, f32),
            jax.ShapeDtypeStruct(block_out, f32),
            jax.ShapeDtypeStruct(small.shape, f32),
            jax.ShapeDtypeStruct((2 * owned * part, width), bf16),
            jax.ShapeDtypeStruct((owned * part, width), bf16),
            jax.ShapeDtypeStruct((owners, 2 * shared_part, owner_width), bf16),
            jax.ShapeDtypeStruct((owners, shared_part, owner_width), bf16),
        ),
        in_specs=[anywhere] * 5 + [vmem],
        out_specs=(vmem,) * 3 + (anywhere,) * 4,
        scratch_shapes=[
            pltpu.VMEM((2, total_rows, 128), bf16),
            pltpu.VMEM((3 * padded, total_rows), bf16),
            pltpu.VMEM((2, total_rows, wide), bf16),
            pltpu.VMEM((3, padded, wide), bf16),
            pltpu.VMEM((4, 2 * shared_part, wide), bf16),
            pltpu.VMEM((4, shared_part, wide), bf16),
            pltpu.VMEM((2,) + block_in, bf16),
            pltpu.VMEM((2,) + block_out, bf16),
            pltpu.VMEM((4,) + block_in, bf16),
            pltpu.VMEM((4,) + block_out, bf16),
            pltpu.VMEM((3,) + block_in, bf16),
            pltpu.VMEM((3,) + block_out, bf16),
        ]
        + [pltpu.VMEM(small.shape, f32)] * 4
        + [
            pltpu.VMEM((4,) + small.shape, f32),
            pltpu.SemaphoreType.DMA((CLOSING_COPIES,)),
            pltpu.SemaphoreType.DMA((CLOSING_COPIES,)),
            pltpu.SemaphoreType.DMA((4,)),
            pltpu.SemaphoreType.DMA((2,)),
            pltpu.SemaphoreType.DMA((2,)),
            pltpu.SemaphoreType.DMA((3 * owned,)),
            pltpu.SemaphoreType.DMA((2,)),
        ],
        compiler_params=pltpu.CompilerParams(
            collective_id=1, has_side_effects=True, vmem_limit_bytes=62 * 2**20
        ),
        cost_estimate=pl.CostEstimate(
            flops=2 * total_rows * width * padded * 3,
            bytes_accessed=150 * 2**20,
            transcendentals=0,
        ),
        name="closing",
    )(rows_all, cot_all, units_all, att_in, att_out, small)


OPENING_COPIES = 6 + 8 + 3 + 14


def opening_kernel(
    sizes,
    normed_ref,
    att_in_ref,
    att_out_ref,
    shared_in_ref,
    shared_out_ref,
    normed_all,
    att_in_all,
    att_out_all,
    shared_in_all,
    shared_out_all,
    send_sems,
    recv_sems,
    own_sems,
):
    rows, owner_width, shared_part = sizes
    place = Place()
    copies = Copies(place, send_sems, recv_sems)

    def in_view(kz, kx):
        at = pl.ds(pl.multiple_of(place.sequence(kz, kx) * owner_width, owner_width), owner_width)
        return att_in_all.at[:, at]

    def out_view(kz, kx):
        return att_out_all.at[place.sequence(kz, kx)]

    here = pl.ds(
        pl.multiple_of(place.sequence(0, 0) * owner_width, owner_width), owner_width
    )
    spot = pl.ds(pl.multiple_of((place.y * 2 + place.c) * rows, rows), rows)

    def shared_block(kz, kx):
        owner = place.sequence(kz, kx)
        at = pl.ds(pl.multiple_of(owner * shared_part, shared_part), shared_part)
        return (
            (shared_in_ref.at[owner], shared_in_all.at[:, here]),
            (shared_out_ref.at[at], shared_out_all.at[:, here]),
        )

    keeps = [
        (normed_ref, normed_all.at[spot]),
        (att_in_ref, in_view(0, 0)),
        (att_out_ref, out_view(0, 0)),
    ] + list(shared_block(0, 0))
    keeps = [
        pltpu.make_async_copy(source, target, own_sems.at[i])
        for i, (source, target) in enumerate(keeps)
    ]
    for keep in keeps:
        keep.start()
    greet(place, PARTNERS + FARTHER + [dict(ky=1, kc=1)])

    def spread_z(kz):
        copies.start(("zi", kz), att_in_ref, in_view(0, 0), kz=kz)
        copies.start(("zo", kz), att_out_ref, out_view(0, 0), kz=kz)

    def pass_x(kz):
        if kz:
            copies.arrived(("zi", kz))
        source = in_view(kz, 0) if kz else att_in_ref
        copies.start(("xi", kz), source, in_view(kz, 0), kx=1)
        if kz:
            copies.arrived(("zo", kz))
        source = out_view(kz, 0) if kz else att_out_ref
        copies.start(("xo", kz), source, out_view(kz, 0), kx=1)

    def share(kz, kx):
        for which, (source, target) in enumerate(shared_block(kz, kx)):
            copies.start((SHARE, which, kz, kx), source, target, kz=kz, kx=kx)

    spread_z(1)
    pass_x(0)
    spread_z(2)
    for ky, kc in ((0, 1), (1, 0), (1, 1)):
        copies.start(("n", ky, kc), normed_ref, normed_all.at[spot], ky=ky, kc=kc)
    pass_x(1)
    spread_z(3)
    pass_x(2)
    share(1, 0)
    share(1, 1)
    pass_x(3)
    share(3, 0)
    share(3, 1)
    share(2, 0)
    share(2, 1)
    share(0, 1)
    for keep in keeps:
        keep.wait()
    for name in copies.made:
        if name[0] not in ("zi", "zo") :
            copies.arrived(name)
    for name in copies.made:
        copies.sent(name)


def opening(normed, att_in, att_out, shared_in, shared_out):
    rows, width = normed.shape
    parts, owner_width, heads_width = att_in.shape
    owners = lax.axis_size(EXPERT)
    shards = lax.axis_size(SHARD)
    shared_part = shared_out.shape[0] // owners
    anywhere = pl.BlockSpec(memory_space=pl.ANY)
    bf16 = jnp.bfloat16
    return pl.pallas_call(
        functools.partial(opening_kernel, (rows, owner_width, shared_part)),
        out_shape=(
            jax.ShapeDtypeStruct((rows * shards, width), bf16),
            jax.ShapeDtypeStruct((parts, owner_width * owners, heads_width), bf16),
            jax.ShapeDtypeStruct((owners,) + att_out.shape, bf16),
            jax.ShapeDtypeStruct((2 * shared_part, width), bf16),
            jax.ShapeDtypeStruct((shared_part, width), bf16),
        ),
        in_specs=[anywhere] * 5,
        out_specs=(anywhere,) * 5,
        scratch_shapes=[
            pltpu.SemaphoreType.DMA((OPENING_COPIES,)),
            pltpu.SemaphoreType.DMA((OPENING_COPIES,)),
            pltpu.SemaphoreType.DMA((5,)),
        ],
        compiler_params=pltpu.CompilerParams(
            collective_id=2, has_side_effects=True, vmem_limit_bytes=62 * 2**20
        ),
        cost_estimate=pl.CostEstimate(
            flops=10**11, bytes_accessed=600 * 2**20, transcendentals=0
        ),
        name="opening",
    )(normed, att_in, att_out, shared_in, shared_out)


def attention_forward(queries, keys_all, values, score_scale):
    scores = block_scores(queries, keys_all, 0, score_scale)
    highest = jnp.max(scores, axis=-1, keepdims=True)
    raised = jnp.exp(scores - highest)
    probs = raised / jnp.sum(raised, axis=-1, keepdims=True)
    mixed_out = jnp.einsum(
        "hqk,khd->qhd", probs.astype(jnp.bfloat16), values, preferred_element_type=jnp.float32
    )
    return mixed_out, probs


def attention_backward(queries, keys_all, values, probs, grad_out, score_scale):
    value_grad = jnp.einsum(
        "hqk,qhd->khd", probs.astype(jnp.bfloat16), grad_out, preferred_element_type=jnp.float32
    )
    prob_grad = jnp.einsum("qhd,khd->hqk", grad_out, values, preferred_element_type=jnp.float32)
    score_grad = (
        probs * (prob_grad - jnp.sum(prob_grad * probs, axis=-1, keepdims=True))
    ).astype(jnp.bfloat16)
    query_grad = jnp.einsum(
        "hqk,khd->qhd", score_grad, keys_all, preferred_element_type=jnp.float32
    )
    key_grad = jnp.einsum("hqk,qhd->khd", score_grad, queries, preferred_element_type=jnp.float32)
    return query_grad * score_scale, key_grad * score_scale, value_grad


def local_gather(
    tokens,
    first_gain,
    attention_in,
    attention_bias,
    attention_out,
    second_gain,
    router,
    shared_gate,
    shared_in,
    shared_out,
    expert_in,
    expert_out,
    cotangent,
    expert_picks,
):
    bf16, f32 = jnp.bfloat16, jnp.float32
    axes = (EXPERT, SHARD)
    local_rows, width = tokens.shape
    shards = lax.axis_size(SHARD)
    owners = lax.axis_size(EXPERT)
    owner = lax.axis_index(EXPERT)
    seq_length = local_rows * shards
    experts = router.shape[1]
    owned = expert_in.shape[0]
    part = expert_in.shape[3]
    heads_here = attention_bias.shape[1]
    head_dim = attention_bias.shape[2] * owners
    score_scale = head_dim ** (-0.5)
    shared_part = shared_in.shape[2] // owners
    slice_rows = width // owners
    cosine_table, sine_table = rope_tables(seq_length, head_dim)

    inputs = tokens.astype(f32)
    first_norm, first_factor = normalize(inputs)
    first_low = (first_norm * first_gain).astype(bf16)
    small = jnp.concatenate(
        [router.reshape(-1), shared_gate, attention_bias.reshape(-1)]
    )
    small_rows = -(-small.shape[0] // slice_rows)
    small_rows = -(-small_rows // 16) * 16
    small = jnp.pad(small, (0, small_rows * slice_rows - small.shape[0]))
    small = small.reshape(small_rows, slice_rows)
    shared_blocks = shared_in.transpose(1, 2, 0).reshape(2, owners, shared_part, slice_rows)
    shared_blocks = shared_blocks.transpose(1, 0, 2, 3).reshape(owners, -1, slice_rows)
    cot_all = lax.all_gather(cotangent, axes, axis=0, tiled=True)
    normed_all, att_in, out_small, shared_win, shared_wout = opening(
        first_low,
        attention_in.transpose(1, 0, 2),
        jnp.concatenate([attention_out, small], axis=0),
        shared_blocks,
        shared_out,
    )
    normed_all, att_in, cot_all = lax.optimization_barrier((normed_all, att_in, cot_all))
    att_out = out_small[:, : attention_out.shape[0]].transpose(1, 0, 2)
    att_out = att_out.reshape(attention_out.shape[0], width)
    small_all = out_small[:, attention_out.shape[0] :].reshape(owners, -1)
    router_size = router.size
    router_full = small_all[:, :router_size].reshape(width, experts)
    gate_full = small_all[:, router_size : router_size + slice_rows].reshape(width)
    bias_start = router_size + slice_rows
    att_bias = small_all[:, bias_start : bias_start + attention_bias.size]
    att_bias = att_bias.reshape((owners,) + attention_bias.shape).transpose(1, 2, 0, 3)
    att_bias = att_bias.reshape(3, heads_here * head_dim)

    projected = jnp.einsum("sd,cdf->scf", normed_all, att_in, preferred_element_type=f32)
    projected = projected + att_bias.astype(f32)[None]
    projected = projected.reshape(seq_length, 3, heads_here, head_dim)
    queries = rotate(projected[:, 0], cosine_table, sine_table).astype(bf16)
    keys_all = rotate(projected[:, 1], cosine_table, sine_table).astype(bf16)
    values = projected[:, 2].astype(bf16)
    attended, probs = attention_forward(queries, keys_all, values, score_scale)
    attended_low = attended.astype(bf16).reshape(seq_length, -1)
    attn_part = jnp.dot(attended_low, att_out, preferred_element_type=f32)
    attn_local = lax.psum_scatter(
        attn_part.astype(bf16), SHARD, scatter_dimension=0, tiled=True
    ).astype(f32)
    residual = inputs + attn_local
    second_norm, second_factor = normalize(residual)
    second_low = (second_norm * second_gain).astype(bf16)
    logits = jnp.dot(second_low, router_full, preferred_element_type=f32)
    route_probs = jax.nn.softmax(logits, axis=-1)
    picked = jnp.sum(
        (
            expert_picks[:, :, None] == jnp.arange(experts, dtype=jnp.int32)[None, None, :]
        ).astype(f32),
        axis=1,
    )
    shared_scale = jax.nn.sigmoid(jnp.dot(second_low, gate_full, preferred_element_type=f32))

    weights_here = jnp.concatenate([picked * route_probs, shared_scale[:, None]], axis=1)
    coarse = weights_here.astype(bf16)
    fine = (weights_here - coarse.astype(f32)).astype(bf16)
    filler = jnp.zeros((local_rows, EXTRA - 2 * (experts + 1)), bf16)
    row_pack = jnp.concatenate([second_low, coarse, fine, filler], axis=1)
    units = owned * part + shared_part
    padded = -(-units // 128) * 128
    unit = jnp.arange(padded)
    column = jnp.where(unit < owned * part, owner * owned + unit // part, experts)
    column = jnp.where(unit < units, column, -1)
    kinds = jnp.arange(EXTRA)
    spots = (kinds[None, :] == column[:, None]).astype(bf16)
    finer = jnp.where(unit < units, column + experts + 1, -1)
    select = (kinds[:, None] == column[None, :]) | (kinds[:, None] == finer[None, :])
    output, back_local, rows_all, units_all = mixture(
        row_pack,
        cot_all,
        expert_in,
        shared_win,
        expert_out,
        shared_wout,
        select.astype(bf16),
        spots,
        residual,
    )
    first_dims = (((0,), (0,)), ((), ()))
    out_grad = cotangent.astype(f32)
    pick_grads = back_local[:, width : width + experts] * picked
    logit_grad = (
        route_probs
        * (pick_grads - jnp.sum(pick_grads * route_probs, axis=-1, keepdims=True))
    ).astype(bf16)
    gate_logit_grad = (
        back_local[:, width + experts] * shared_scale * (1.0 - shared_scale)
    ).astype(bf16)
    local_back = lax.dot_general(
        logit_grad, router_full, (((1,), (1,)), ((), ())), preferred_element_type=f32
    )
    local_back = local_back + gate_logit_grad.astype(f32)[:, None] * gate_full.astype(f32)[None]
    second_grad = local_back + back_local[:, :width]
    residual_back, second_gain_grad = norm_back(
        second_grad, second_norm, second_factor, second_gain
    )
    residual_grad = out_grad + residual_back
    residual_all = lax.all_gather(residual_grad.astype(bf16), SHARD, axis=0, tiled=True)
    att_out_grad = lax.dot_general(
        attended_low, residual_all, first_dims, preferred_element_type=f32
    )
    attended_grad = lax.dot_general(
        residual_all, att_out, (((1,), (1,)), ((), ())), preferred_element_type=f32
    )
    attended_grad = attended_grad.astype(bf16).reshape(seq_length, heads_here, head_dim)
    query_grad, key_grad, value_grad = attention_backward(
        queries, keys_all, values, probs, attended_grad, score_scale
    )
    projected_grad = jnp.stack(
        [
            rotate_back(query_grad, cosine_table, sine_table),
            rotate_back(key_grad, cosine_table, sine_table),
            value_grad,
        ],
        axis=1,
    )
    projected_grad = projected_grad.astype(bf16).reshape(seq_length, 3, heads_here * head_dim)
    att_in_grad = jnp.einsum("sd,scf->cdf", normed_all, projected_grad, preferred_element_type=f32)
    att_bias_grad = jnp.sum(projected_grad.astype(f32), axis=0)
    first_part = jnp.einsum("scf,cdf->sd", projected_grad, att_in, preferred_element_type=f32)
    first_grad = lax.psum_scatter(
        first_part.astype(bf16), SHARD, scatter_dimension=0, tiled=True
    ).astype(f32)
    input_back, first_gain_grad = norm_back(first_grad, first_norm, first_factor, first_gain)
    input_grad = residual_grad + input_back

    vec_grads = jnp.concatenate([logit_grad, gate_logit_grad[:, None]], axis=1)
    vec_grads = lax.dot_general(vec_grads, second_low, first_dims, preferred_element_type=f32)
    bias_wide = jnp.zeros((3, shards, heads_here * head_dim), f32)
    bias_wide = lax.dynamic_update_slice_in_dim(
        bias_wide, att_bias_grad[:, None], lax.axis_index(SHARD), 1
    )
    bias_rows = bias_wide.size // width
    first_bias = experts + 3
    small = jnp.concatenate(
        [vec_grads, second_gain_grad[None], first_gain_grad[None], bias_wide.reshape(-1, width)]
    )
    small = jnp.pad(small, ((0, -small.shape[0] % 8), (0, 0)))
    (
        att_in_local,
        att_out_local,
        summed,
        expert_in_grad,
        expert_out_grad,
        shared_in_local,
        shared_out_local,
    ) = closing(
        rows_all,
        cot_all,
        units_all,
        att_in_grad.astype(bf16),
        att_out_grad.astype(bf16),
        small,
        owned,
        part,
        shared_part,
    )
    expert_in_grad = expert_in_grad.reshape(owned, 2, part, width).transpose(0, 3, 1, 2)
    expert_in_grad = expert_in_grad.astype(f32)
    expert_out_grad = expert_out_grad.reshape(owned, part, width).astype(f32)
    shared_in_local = shared_in_local.reshape(owners, 2, shared_part, slice_rows)
    shared_in_local = shared_in_local.transpose(3, 1, 0, 2).reshape(slice_rows, 2, -1).astype(f32)
    shared_out_local = shared_out_local.reshape(-1, slice_rows).astype(f32)
    vec_local = lax.dynamic_slice_in_dim(
        summed[: experts + 1], owner * slice_rows, slice_rows, axis=1
    )
    bias_all = summed[first_bias : first_bias + bias_rows].reshape(
        3, shards, heads_here, owners, head_dim // owners
    )
    att_bias_local = lax.dynamic_index_in_dim(bias_all, lax.axis_index(SHARD), 1, False)
    att_bias_local = lax.dynamic_index_in_dim(att_bias_local, owner, 2, False)
    return (
        output,
        input_grad,
        summed[experts + 2],
        att_in_local.transpose(1, 0, 2),
        att_bias_local,
        att_out_local,
        summed[experts + 1],
        vec_local[:experts].T,
        vec_local[experts],
        shared_in_local,
        shared_out_local,
        expert_in_grad,
        expert_out_grad,
    )


def solution(mesh):
    in_specs = (
        P((EXPERT, SHARD), None),
        P(),
        P(EXPERT, None, SHARD),
        P(None, SHARD, EXPERT),
        P(SHARD, EXPERT),
        P(),
        P(EXPERT, None),
        P(EXPERT),
        P(EXPERT, None, SHARD),
        P(SHARD, EXPERT),
        P(EXPERT, None, None, SHARD),
        P(EXPERT, SHARD, None),
        P((EXPERT, SHARD), None),
        P((EXPERT, SHARD), None),
    )
    out_specs = (
        P((EXPERT, SHARD), None),
        P((EXPERT, SHARD), None),
        P(),
        P(EXPERT, None, SHARD),
        P(None, SHARD, EXPERT),
        P(SHARD, EXPERT),
        P(),
        P(EXPERT, None),
        P(EXPERT),
        P(EXPERT, None, SHARD),
        P(SHARD, EXPERT),
        P(EXPERT, None, None, SHARD),
        P(EXPERT, SHARD, None),
    )
    plan = local_gather if mesh.size <= 32 else local_exchange
    return jax.shard_map(plan, mesh=mesh, in_specs=in_specs, out_specs=out_specs, check_vma=False)
```

```python
import functools

import jax
import jax.numpy as jnp
from jax import lax
from jax.experimental import pallas as pl
from jax.experimental.pallas import tpu as pltpu
from jax.sharding import PartitionSpec as P

EPSILON = 1e-06
ROPE_BASE = 1000000.0
MASKED = -1e30
EXPERT, SHARD = "expert", "shard"
CORE, ROW, COLUMN = "kc", "ky", "kx"
SUM_CORES, SHARE, TOTAL = "sc", "share", "t"


def normalize(activations):
    factor = lax.rsqrt(jnp.mean(activations * activations, axis=-1, keepdims=True) + EPSILON)
    return (activations * factor, factor)


def norm_back(incoming, normed, factor, gain_vec):
    scaled = incoming * gain_vec
    inner_mean = jnp.mean(scaled * normed, axis=-1, keepdims=True)
    return (factor * (scaled - normed * inner_mean), jnp.sum(incoming * normed, axis=0))


def rope_tables(length, head_dim):
    half_dim = head_dim // 2
    frequency = jnp.power(ROPE_BASE, -jnp.arange(half_dim, dtype=jnp.float32) * (2.0 / head_dim))
    angles = jnp.arange(length, dtype=jnp.float32)[:, None] * frequency[None, :]
    return (
        jnp.concatenate([jnp.cos(angles), jnp.cos(angles)], axis=-1),
        jnp.concatenate([jnp.sin(angles), jnp.sin(angles)], axis=-1),
    )


def rotate(values, cosine_table, sine_table):
    half_dim = values.shape[-1] // 2
    turned = jnp.concatenate([-values[..., half_dim:], values[..., :half_dim]], axis=-1)
    return values * cosine_table[:, None, :] + turned * sine_table[:, None, :]


def rotate_back(incoming, cosine_table, sine_table):
    half_dim = incoming.shape[-1] // 2
    scaled = incoming * sine_table[:, None, :]
    turned = jnp.concatenate([scaled[..., half_dim:], -scaled[..., :half_dim]], axis=-1)
    return incoming * cosine_table[:, None, :] + turned


def block_scores(query_block, keys_all, first_row, score_scale):
    scores = (
        jnp.einsum("qhd,khd->hqk", query_block, keys_all, preferred_element_type=jnp.float32)
        * score_scale
    )
    row_pos = first_row + jnp.arange(query_block.shape[0], dtype=jnp.int32)
    col_pos = jnp.arange(keys_all.shape[0], dtype=jnp.int32)
    return jnp.where(col_pos[None, None, :] <= row_pos[None, :, None], scores, MASKED)


def attend(queries, keys_all, values, block_rows, score_scale):
    blocks = queries.shape[0] // block_rows
    starts = jnp.arange(blocks, dtype=jnp.int32) * block_rows

    def one_block(block_item):
        query_block, first_row = block_item
        scores = block_scores(query_block, keys_all, first_row, score_scale)
        highest = jnp.max(scores, axis=-1, keepdims=True)
        raised = jnp.exp(scores - highest)
        row_total = jnp.sum(raised, axis=-1, keepdims=True)
        weights = (raised / row_total).astype(jnp.bfloat16)
        mixed_out = jnp.einsum("hqk,khd->qhd", weights, values, preferred_element_type=jnp.float32)
        return (mixed_out, (highest + jnp.log(row_total))[..., 0])

    shape_blocks = (blocks, block_rows) + queries.shape[1:]
    mixed_out, logsum = lax.map(one_block, (queries.reshape(shape_blocks), starts))
    return (mixed_out.reshape(queries.shape), logsum)


def attend_back(queries, keys_all, values, logsum, grad_out, block_rows, score_scale):
    blocks = queries.shape[0] // block_rows
    starts = jnp.arange(blocks, dtype=jnp.int32) * block_rows
    shape_blocks = (blocks, block_rows) + queries.shape[1:]

    def one_block(running, block_item):
        key_grad, value_grad = running
        query_block, grad_block, logsum_block, first_row = block_item
        scores = block_scores(query_block, keys_all, first_row, score_scale)
        block_probs = jnp.exp(scores - logsum_block[..., None])
        value_grad = value_grad + jnp.einsum(
            "hqk,qhd->khd",
            block_probs.astype(jnp.bfloat16),
            grad_block,
            preferred_element_type=jnp.float32,
        )
        prob_grad = jnp.einsum(
            "qhd,khd->hqk", grad_block, values, preferred_element_type=jnp.float32
        )
        score_grad = (
            block_probs * (prob_grad - jnp.sum(prob_grad * block_probs, axis=-1, keepdims=True))
        ).astype(jnp.bfloat16)
        query_grad = (
            jnp.einsum("hqk,khd->qhd", score_grad, keys_all, preferred_element_type=jnp.float32)
            * score_scale
        )
        key_grad = (
            key_grad
            + jnp.einsum(
                "hqk,qhd->khd", score_grad, query_block, preferred_element_type=jnp.float32
            )
            * score_scale
        )
        return ((key_grad, value_grad), query_grad)

    zero_keys = jnp.zeros(keys_all.shape, jnp.float32)
    (key_grad, value_grad), query_grad = lax.scan(
        one_block,
        (zero_keys, zero_keys),
        (queries.reshape(shape_blocks), grad_out.reshape(shape_blocks), logsum, starts),
    )
    return (query_grad.reshape(queries.shape), key_grad, value_grad)


def gate_up_forward(activations, weight_in, weight_out):
    raised = jnp.einsum(
        "rekd,edcf->rekcf", activations, weight_in, preferred_element_type=jnp.float32
    )
    hidden = (jax.nn.silu(raised[..., 0, :]) * raised[..., 1, :]).astype(jnp.bfloat16)
    result = jnp.einsum("rekf,efd->rekd", hidden, weight_out, preferred_element_type=jnp.float32)
    return (raised, hidden, result)


def gate_up_back(activations, weight_in, weight_out, raised, hidden, incoming):
    out_grad = jnp.einsum("rekf,rekd->efd", hidden, incoming, preferred_element_type=jnp.float32)
    hidden_grad = jnp.einsum(
        "rekd,efd->rekf", incoming, weight_out, preferred_element_type=jnp.float32
    )
    gate_part = raised[..., 0, :]
    up_part = raised[..., 1, :]
    sigmoid_gate = jax.nn.sigmoid(gate_part)
    gate_grad = (
        hidden_grad * up_part * sigmoid_gate * (1.0 + gate_part * (1.0 - sigmoid_gate))
    ).astype(jnp.bfloat16)
    up_grad = (hidden_grad * gate_part * sigmoid_gate).astype(jnp.bfloat16)
    gate_wgrad = jnp.einsum(
        "rekd,rekf->edf", activations, gate_grad, preferred_element_type=jnp.float32
    )
    up_wgrad = jnp.einsum(
        "rekd,rekf->edf", activations, up_grad, preferred_element_type=jnp.float32
    )
    both_grad = jnp.stack([gate_grad, up_grad], axis=-2)
    row_grad = jnp.einsum(
        "rekcf,edcf->rekd", both_grad, weight_in, preferred_element_type=jnp.float32
    )
    return (gate_wgrad, up_wgrad, out_grad, row_grad)


def local_exchange(
    tokens,
    first_gain,
    attention_in,
    attention_bias,
    attention_out,
    second_gain,
    router,
    shared_gate,
    shared_in,
    shared_out,
    expert_in,
    expert_out,
    cotangent,
    expert_picks,
):
    local_rows, model_width = tokens.shape
    shard_count = lax.axis_size(SHARD)
    owner_count = lax.axis_size(EXPERT)
    seq_length = local_rows * shard_count
    expert_count = router.shape[1]
    pick_count = expert_picks.shape[1]
    owned_count = expert_in.shape[0]
    capacity = max(2, 2 * local_rows * pick_count // expert_count)
    heads_here = attention_bias.shape[1]
    head_dim = attention_bias.shape[2] * owner_count
    score_scale = head_dim ** (-0.5)
    block_rows = min(seq_length, 512)
    cosine_table, sine_table = rope_tables(seq_length, head_dim)

    def fetch_dense():
        return (
            lax.all_gather(attention_in, EXPERT, axis=0, tiled=True),
            lax.all_gather(attention_bias, EXPERT, axis=2, tiled=True),
            lax.all_gather(attention_out, EXPERT, axis=1, tiled=True),
            lax.all_gather(router, EXPERT, axis=0, tiled=True),
            lax.all_gather(shared_gate, EXPERT, axis=0, tiled=True),
            lax.all_gather(shared_in, EXPERT, axis=0, tiled=True),
            lax.all_gather(shared_out, EXPERT, axis=1, tiled=True),
        )

    def fetch_rows(normed_low):
        return (
            lax.all_gather(normed_low, SHARD, axis=0, tiled=True),
            lax.all_gather(expert_in, SHARD, axis=3, tiled=True),
            lax.all_gather(expert_out, SHARD, axis=1, tiled=True),
        )

    inputs = tokens.astype(jnp.float32)
    first_norm, first_factor = normalize(inputs)
    first_low = (first_norm * first_gain).astype(jnp.bfloat16)
    att_in, att_bias, att_out, router_full, gate_full, shared_inw, shared_outw = fetch_dense()
    normed_all, expert_inw, expert_outw = fetch_rows(first_low)
    projected = jnp.einsum("sd,dcf->scf", normed_all, att_in, preferred_element_type=jnp.float32)
    projected = projected + att_bias.reshape(3, -1).astype(jnp.float32)[None]
    projected = projected.reshape(seq_length, 3, heads_here, head_dim)
    queries = rotate(projected[:, 0], cosine_table, sine_table).astype(jnp.bfloat16)
    keys_all = rotate(projected[:, 1], cosine_table, sine_table).astype(jnp.bfloat16)
    values = projected[:, 2].astype(jnp.bfloat16)
    attended, logsum = attend(queries, keys_all, values, block_rows, score_scale)
    attended_low = attended.astype(jnp.bfloat16).reshape(seq_length, -1)
    attn_part = jnp.dot(attended_low, att_out, preferred_element_type=jnp.float32)
    attn_local = lax.psum_scatter(
        attn_part.astype(jnp.bfloat16), SHARD, scatter_dimension=0, tiled=True
    ).astype(jnp.float32)
    residual = inputs + attn_local
    second_norm, second_factor = normalize(residual)
    second_low = (second_norm * second_gain).astype(jnp.bfloat16)
    logits = jnp.dot(second_low, router_full, preferred_element_type=jnp.float32)
    route_probs = jax.nn.softmax(logits, axis=-1)
    picked = (
        expert_picks[:, :, None] == jnp.arange(expert_count, dtype=jnp.int32)[None, None, :]
    ).astype(jnp.float32)
    gate_values = jnp.sum(picked * route_probs[:, None, :], axis=-1)
    flat_picks = expert_picks.reshape(-1)
    flat_hot = (flat_picks[:, None] == jnp.arange(expert_count, dtype=jnp.int32)[None, :]).astype(
        jnp.int32
    )
    slot_ranks = jnp.sum((jnp.cumsum(flat_hot, axis=0) - flat_hot) * flat_hot, axis=1)
    slot_rows = flat_picks * capacity + slot_ranks
    outgoing = jnp.zeros((expert_count * capacity, model_width), jnp.bfloat16)
    outgoing = outgoing.at[slot_rows].set(jnp.repeat(second_low, pick_count, axis=0))
    arrived = lax.all_to_all(
        outgoing.reshape(owner_count, owned_count, capacity, model_width),
        EXPERT,
        split_axis=0,
        concat_axis=0,
        tiled=True,
    )
    mixed_all = lax.all_gather(second_low, SHARD, axis=0, tiled=True)
    shared_raised, shared_hidden, shared_part = gate_up_forward(
        mixed_all[:, None, None, :], shared_inw[None], shared_outw[None]
    )
    shared_rows = lax.psum_scatter(
        shared_part[:, 0, 0, :].astype(jnp.bfloat16), SHARD, scatter_dimension=0, tiled=True
    ).astype(jnp.float32)
    expert_raised, expert_hidden, expert_part = gate_up_forward(arrived, expert_inw, expert_outw)
    expert_result = expert_part.astype(jnp.bfloat16)
    shared_scale = jax.nn.sigmoid(
        jnp.dot(second_low, gate_full, preferred_element_type=jnp.float32)
    )
    out_grad = cotangent.astype(jnp.float32)
    slot_values = (
        (gate_values[:, :, None] * out_grad[:, None, :])
        .reshape(-1, model_width)
        .astype(jnp.bfloat16)
    )
    grad_send = (
        jnp.zeros((expert_count * capacity, model_width), jnp.bfloat16)
        .at[slot_rows]
        .set(slot_values)
    )
    returned, owner_grads = (
        lax.all_to_all(expert_result, EXPERT, split_axis=0, concat_axis=0, tiled=True),
        lax.all_to_all(
            grad_send.reshape(owner_count, owned_count, capacity, model_width),
            EXPERT,
            split_axis=0,
            concat_axis=0,
            tiled=True,
        ),
    )
    gathered_out = returned.reshape(expert_count * capacity, model_width)[slot_rows]
    gathered_out = gathered_out.reshape(local_rows, pick_count, model_width).astype(jnp.float32)
    routed = jnp.sum(gate_values[:, :, None] * gathered_out, axis=1)
    output = (residual + shared_scale[:, None] * shared_rows + routed).astype(jnp.bfloat16)
    pick_grad = jnp.sum(out_grad[:, None, :] * gathered_out, axis=-1)
    route_grad = jnp.sum(picked * pick_grad[:, :, None], axis=1)
    logit_grad = (
        route_probs * (route_grad - jnp.sum(route_grad * route_probs, axis=-1, keepdims=True))
    ).astype(jnp.bfloat16)
    scale_grad = jnp.sum(out_grad * shared_rows, axis=-1)
    gate_logit_grad = (scale_grad * shared_scale * (1.0 - shared_scale)).astype(jnp.bfloat16)
    shared_grad = (shared_scale[:, None] * out_grad).astype(jnp.bfloat16)
    shared_grad_all, logit_grad_all, gate_grad_all = (
        lax.all_gather(shared_grad, SHARD, axis=0, tiled=True),
        lax.all_gather(logit_grad, SHARD, axis=0, tiled=True),
        lax.all_gather(gate_logit_grad, SHARD, axis=0, tiled=True),
    )
    att_in, att_bias, att_out, router_full, gate_full, shared_inw, shared_outw = fetch_dense()
    normed_all, expert_inw, expert_outw = fetch_rows(first_low)
    expert_gate_w, expert_up_w, expert_down_w, owner_row_grad = gate_up_back(
        arrived, expert_inw, expert_outw, expert_raised, expert_hidden, owner_grads
    )
    shared_gate_w, shared_up_w, shared_down_w, shared_row_grad = gate_up_back(
        mixed_all[:, None, None, :],
        shared_inw[None],
        shared_outw[None],
        shared_raised,
        shared_hidden,
        shared_grad_all[:, None, None, :],
    )
    owner_low = owner_row_grad.astype(jnp.bfloat16)
    shared_back = lax.psum_scatter(
        shared_row_grad[:, 0, 0, :].astype(jnp.bfloat16), SHARD, scatter_dimension=0, tiled=True
    ).astype(jnp.float32)
    returned_grad = lax.all_to_all(owner_low, EXPERT, split_axis=0, concat_axis=0, tiled=True)
    routed_back = returned_grad.reshape(expert_count * capacity, model_width)[slot_rows]
    routed_back = jnp.sum(
        routed_back.reshape(local_rows, pick_count, model_width).astype(jnp.float32), axis=1
    )
    local_back = jnp.einsum(
        "te,de->td", logit_grad, router_full, preferred_element_type=jnp.float32
    )
    local_back = (
        local_back
        + gate_logit_grad.astype(jnp.float32)[:, None] * gate_full.astype(jnp.float32)[None, :]
    )
    second_grad = local_back + shared_back + routed_back
    residual_back, second_gain_grad = norm_back(
        second_grad, second_norm, second_factor, second_gain
    )
    residual_grad = out_grad + residual_back
    residual_all = lax.all_gather(residual_grad.astype(jnp.bfloat16), SHARD, axis=0, tiled=True)
    att_out_grad = jnp.einsum(
        "sf,sd->fd", attended_low, residual_all, preferred_element_type=jnp.float32
    )
    attended_grad = jnp.einsum(
        "sd,fd->sf", residual_all, att_out, preferred_element_type=jnp.float32
    )
    attended_grad = attended_grad.astype(jnp.bfloat16).reshape(seq_length, heads_here, head_dim)
    query_grad, key_grad, value_grad = attend_back(
        queries, keys_all, values, logsum, attended_grad, block_rows, score_scale
    )
    projected_grad = jnp.stack(
        [
            rotate_back(query_grad, cosine_table, sine_table),
            rotate_back(key_grad, cosine_table, sine_table),
            value_grad,
        ],
        axis=1,
    )
    projected_grad = projected_grad.astype(jnp.bfloat16).reshape(
        seq_length, 3, heads_here * head_dim
    )
    att_in_grad = jnp.einsum(
        "sd,scf->dcf", normed_all, projected_grad, preferred_element_type=jnp.float32
    )
    att_bias_grad = jnp.sum(projected_grad.astype(jnp.float32), axis=0).reshape(
        3, heads_here, head_dim
    )
    first_part = jnp.einsum(
        "scf,dcf->sd", projected_grad, att_in, preferred_element_type=jnp.float32
    )
    first_grad, expert_gate_l, expert_up_l, expert_down_l = (
        lax.psum_scatter(
            first_part.astype(jnp.bfloat16), SHARD, scatter_dimension=0, tiled=True
        ).astype(jnp.float32),
        lax.psum_scatter(
            expert_gate_w.astype(jnp.bfloat16), SHARD, scatter_dimension=2, tiled=True
        ).astype(jnp.float32),
        lax.psum_scatter(
            expert_up_w.astype(jnp.bfloat16), SHARD, scatter_dimension=2, tiled=True
        ).astype(jnp.float32),
        lax.psum_scatter(
            expert_down_w.astype(jnp.bfloat16), SHARD, scatter_dimension=1, tiled=True
        ).astype(jnp.float32),
    )
    input_back, first_gain_grad = norm_back(first_grad, first_norm, first_factor, first_gain)
    input_grad = residual_grad + input_back
    router_grad = jnp.einsum(
        "sd,se->de", mixed_all, logit_grad_all, preferred_element_type=jnp.float32
    )
    gate_vec_grad = jnp.einsum(
        "sd,s->d", mixed_all, gate_grad_all, preferred_element_type=jnp.float32
    )
    shared_in_grad = jnp.stack([shared_gate_w[0], shared_up_w[0]], axis=1)
    (
        att_in_local,
        att_bias_local,
        att_out_local,
        router_local,
        gate_vec_local,
        shared_in_local,
        shared_out_local,
    ) = (
        lax.psum_scatter(
            att_in_grad.astype(jnp.bfloat16), EXPERT, scatter_dimension=0, tiled=True
        ).astype(jnp.float32),
        lax.psum_scatter(
            att_bias_grad.astype(jnp.bfloat16), EXPERT, scatter_dimension=2, tiled=True
        ).astype(jnp.float32),
        lax.psum_scatter(
            att_out_grad.astype(jnp.bfloat16), EXPERT, scatter_dimension=1, tiled=True
        ).astype(jnp.float32),
        lax.psum_scatter(
            router_grad.astype(jnp.bfloat16), EXPERT, scatter_dimension=0, tiled=True
        ).astype(jnp.float32),
        lax.psum_scatter(
            gate_vec_grad.astype(jnp.bfloat16), EXPERT, scatter_dimension=0, tiled=True
        ).astype(jnp.float32),
        lax.psum_scatter(
            shared_in_grad.astype(jnp.bfloat16), EXPERT, scatter_dimension=0, tiled=True
        ).astype(jnp.float32),
        lax.psum_scatter(
            shared_down_w[0].astype(jnp.bfloat16), EXPERT, scatter_dimension=1, tiled=True
        ).astype(jnp.float32),
    )
    first_gain_all, second_gain_all = lax.psum(
        (first_gain_grad, second_gain_grad), (EXPERT, SHARD)
    )
    expert_in_grad = jnp.stack([expert_gate_l, expert_up_l], axis=2)
    return (
        output,
        input_grad,
        first_gain_all,
        att_in_local,
        att_bias_local,
        att_out_local,
        second_gain_all,
        router_local,
        gate_vec_local,
        shared_in_local,
        shared_out_local,
        expert_in_grad,
        expert_down_l,
    )


MESH = pl.DeviceIdType.MESH
EXTRA = 128
NT_DIMS = (((1,), (1,)), ((), ()))


class Place:
    def __init__(self):
        e, s = lax.axis_index(EXPERT), lax.axis_index(SHARD)
        self.z, self.x, self.y, self.c = e // 2, e % 2, s // 2, s % 2

    def z_of(self, kz):
        z = self.z
        return (z, z + 1 - 2 * (z % 2), (z + 2) % 4, 3 - z)[kz]

    def x_of(self, kx):
        return (self.x, 1 - self.x)[kx]

    def y_of(self, ky):
        return (self.y, 1 - self.y)[ky]

    def c_of(self, kc):
        return (self.c, 1 - self.c)[kc]

    def device(self, kz=0, kx=0, ky=0, kc=0):
        return (self.z_of(kz) * 2 + self.x_of(kx), self.y_of(ky) * 2 + self.c_of(kc))

    def sequence(self, kz, kx):
        return self.z_of(kz) * 2 + self.x_of(kx)

    def block(self, kz, kx, ky, kc):
        return self.sequence(kz, kx) * 4 + self.y_of(ky) * 2 + self.c_of(kc)


PARTNERS = [dict(kz=1), dict(kz=2), dict(kz=3), dict(kx=1), dict(ky=1), dict(kc=1)]
FARTHER = [dict(kz=1, kx=1), dict(kz=2, kx=1), dict(kz=3, kx=1)]


def greet(place, partners):
    barrier = pltpu.get_barrier_semaphore()
    for partner in partners:
        pl.semaphore_signal(
            barrier, inc=1, device_id=place.device(**partner), device_id_type=MESH
        )
    pl.semaphore_wait(barrier, len(partners))


class Copies:
    def __init__(self, place, send_sems, recv_sems):
        self.place, self.send_sems, self.recv_sems = place, send_sems, recv_sems
        self.made, self.got, self.left = {}, set(), set()

    def start(self, name, source, target, **partner):
        at = len(self.made)
        copy = pltpu.make_async_remote_copy(
            src_ref=source,
            dst_ref=target,
            send_sem=self.send_sems.at[at],
            recv_sem=self.recv_sems.at[at],
            device_id=self.place.device(**partner),
            device_id_type=MESH,
        )
        copy.start()
        self.made[name] = copy

    def arrived(self, name):
        if name not in self.got:
            self.got.add(name)
            self.made[name].wait_recv()

    def sent(self, name):
        if name not in self.left:
            self.left.add(name)
            self.made[name].wait_send()


GATHER_COPIES = 55
SUM_COPIES = 43


class Gather:
    def __init__(self, place, copies, block_ref, all_ref, rows):
        self.place, self.copies = place, copies
        self.block_ref, self.all_ref, self.rows = block_ref, all_ref, rows

    def view(self, kz, kx, ky, piece, own=False):
        half = self.rows // 2
        first = 0 if piece in (None, 0) else half
        count = self.rows if piece is None else half
        if own and (kz, kx, ky) == (0, 0, 0):
            return self.block_ref.at[pl.ds(first, count)]
        start = self.place.block(kz, kx, ky, 0) * self.rows + first
        return self.all_ref.at[pl.ds(pl.multiple_of(start, half), count)]

    def send(self, name, from_z, from_x, from_y, piece, **partner):
        self.copies.start(
            name,
            self.view(from_z, from_x, from_y, piece, own=True),
            self.view(from_z, from_x, from_y, piece),
            **partner,
        )

    def begin(self, kz):
        self.send(("z", kz), 0, 0, 0, None, kz=kz)

    def first(self, kz):
        if kz:
            self.copies.arrived(("z", kz))
        self.send(("y0", kz, 0), kz, 0, 0, 0, ky=1)
        self.send(("y1", kz), kz, 0, 0, 1, ky=1)
        self.send(("x0", kz), kz, 0, 0, 0, kx=1)
        self.send(("x1", kz, 0), kz, 0, 0, 1, kx=1)
        self.send(("c", kz), kz, 0, 0, None, kc=1)

    def second_y(self, kz):
        self.copies.arrived(("y1", kz))
        self.send(("x1", kz, 1), kz, 0, 1, 1, kx=1)
        self.send(("c01", kz), kz, 0, 1, 1, kc=1)
        self.copies.arrived(("y0", kz, 0))
        self.send(("c00", kz), kz, 0, 1, 0, kc=1)

    def second_x(self, kz):
        self.copies.arrived(("x0", kz))
        self.send(("y0", kz, 1), kz, 1, 0, 0, ky=1)
        self.send(("c10", kz), kz, 1, 0, 0, kc=1)
        self.copies.arrived(("x1", kz, 0))
        self.send(("c11", kz), kz, 1, 0, 1, kc=1)

    def third(self, kz):
        self.copies.arrived(("y0", kz, 1))
        self.send(("c20", kz), kz, 1, 1, 0, kc=1)
        self.copies.arrived(("x1", kz, 1))
        self.send(("c21", kz), kz, 1, 1, 1, kc=1)

    def have(self, kz, kx):
        for name in ("c10", "c11", "c20", "c21") if kx else ("c", "c00", "c01"):
            self.copies.arrived((name, kz))


class Sums:
    def __init__(self, place, copies, tag, held, from_y0, from_y1, from_x0, from_x1, from_z):
        self.place, self.copies, self.tag, self.held = place, copies, tag, held
        self.from_y0, self.from_y1 = from_y0, from_y1
        self.from_x0, self.from_x1, self.from_z = from_x0, from_x1, from_z
        self.rows = held.shape[1]
        self.half = self.rows // 2

    def slot(self, kz, kx, ky, piece=None):
        at = kz * 4 + kx * 2 + ky
        if piece is None:
            return self.held.at[at]
        return self.held.at[at, pl.ds(piece * self.half, self.half)]

    def staged_part(self, staged):
        def view(ky, kc):
            start = (self.place.y_of(ky) * 2 + self.place.c_of(kc)) * self.rows
            return staged.at[pl.ds(pl.multiple_of(start, self.rows), self.rows)]

        return view

    def add(self, into, other):
        into[...] = into[...] + other[...]

    def cores(self, kz, kx, part):
        for ky in (1, 0):
            self.copies.start((SUM_CORES, self.tag, kz, kx, ky), part(ky, 1), self.slot(kz, kx, ky), kc=1)

    def first(self, kz, kx, part):
        for ky in (1, 0):
            self.copies.arrived((SUM_CORES, self.tag, kz, kx, ky))
            self.add(self.slot(kz, kx, ky), part(ky, 0))
            if ky:
                self.copies.start(
                    ("sy0", self.tag, kz, kx), self.slot(kz, kx, 1, 0), self.from_y0.at[kz * 2 + kx], ky=1
                )
            if kx:
                self.copies.start(
                    ("sx1", self.tag, kz, ky), self.slot(kz, 1, ky, 1), self.from_x1.at[kz * 2 + ky], kx=1
                )
        for ky in (1, 0):
            self.copies.sent((SUM_CORES, self.tag, kz, kx, ky))

    def second_away(self, kz):
        self.copies.arrived(("sy0", self.tag, kz, 1))
        self.add(self.slot(kz, 1, 0, 0), self.from_y0.at[kz * 2 + 1])
        self.copies.start(("sx0", self.tag, kz), self.slot(kz, 1, 0, 0), self.from_x0.at[kz], kx=1)

    def second_here(self, kz):
        self.copies.arrived(("sx1", self.tag, kz, 1))
        self.add(self.slot(kz, 0, 1, 1), self.from_x1.at[kz * 2 + 1])
        self.copies.start(("sy1", self.tag, kz), self.slot(kz, 0, 1, 1), self.from_y1.at[kz], ky=1)
        self.copies.arrived(("sx1", self.tag, kz, 0))
        self.add(self.slot(kz, 0, 0, 1), self.from_x1.at[kz * 2])
        self.copies.arrived(("sy0", self.tag, kz, 0))
        self.add(self.slot(kz, 0, 0, 0), self.from_y0.at[kz * 2])
        self.copies.arrived(("sx0", self.tag, kz))
        self.add(self.slot(kz, 0, 0, 0), self.from_x0.at[kz])

    def third(self, kz):
        self.copies.arrived(("sy1", self.tag, kz))
        self.add(self.slot(kz, 0, 0, 1), self.from_y1.at[kz])
        if kz:
            self.copies.start(("sz", self.tag, kz), self.slot(kz, 0, 0), self.from_z.at[kz - 1], kz=kz)

    def total(self):
        total = self.slot(0, 0, 0)[...].astype(jnp.float32)
        for kz in (1, 2, 3):
            self.copies.arrived(("sz", self.tag, kz))
            total = total + self.from_z.at[kz - 1][...].astype(jnp.float32)
        return total


RAISE, OUT, BACK, CORES, BEGIN, PASS, PASS_X, PASS_Y, PASS_LAST, HAVE = range(10)
FIRST, AWAY, HERE, THIRD = range(10, 14)
ORDER = ((0, 1), (3, 1), (3, 0), (2, 1), (2, 0), (1, 1), (1, 0), (0, 0))
PLAN = (
    (PASS, 0, 0), (BEGIN, 1, 0), (BEGIN, 3, 0), (PASS_Y, 0, 0), (PASS_X, 0, 0),
    (PASS_LAST, 0, 0), (PASS, 3, 0), (HAVE, 0, 0), (RAISE, 0, 0), (BEGIN, 2, 0), (RAISE, 0, 1),
    (PASS_X, 3, 0), (PASS_Y, 3, 0), (RAISE, 0, 2), (RAISE, 0, 3), (PASS, 1, 0), (OUT, 0, 0),
    (OUT, 0, 1), (CORES, 0, 0), (BACK, 0, 0), (PASS_LAST, 3, 0), (BACK, 0, 1), (CORES, 1, 0),
    (HAVE, 1, 0), (PASS, 2, 0), (PASS_Y, 1, 0), (RAISE, 1, 0), (RAISE, 1, 1), (RAISE, 1, 2),
    (PASS_Y, 2, 0), (RAISE, 1, 3), (HAVE, 2, 0), (FIRST, 0, 0), (OUT, 1, 0), (OUT, 1, 1),
    (CORES, 0, 1), (FIRST, 1, 0), (BACK, 1, 0), (PASS_X, 2, 0), (BACK, 1, 1), (CORES, 1, 1),
    (RAISE, 2, 0), (RAISE, 2, 1), (FIRST, 0, 1), (RAISE, 2, 2), (FIRST, 1, 1), (RAISE, 2, 3),
    (OUT, 2, 0), (OUT, 2, 1), (CORES, 0, 2), (BACK, 2, 0), (BACK, 2, 1), (PASS_LAST, 2, 0),
    (CORES, 1, 2), (AWAY, 0, 3), (HAVE, 3, 0), (FIRST, 1, 2), (FIRST, 0, 2), (RAISE, 3, 0),
    (RAISE, 3, 1), (RAISE, 3, 2), (RAISE, 3, 3), (PASS_X, 1, 0), (OUT, 3, 0), (OUT, 3, 1),
    (CORES, 0, 3), (BACK, 3, 0), (AWAY, 1, 3), (HAVE, 4, 0), (BACK, 3, 1), (CORES, 1, 3),
    (HERE, 0, 3), (FIRST, 0, 3), (RAISE, 4, 0), (RAISE, 4, 1), (RAISE, 4, 2), (PASS_LAST, 1, 0),
    (FIRST, 1, 3), (RAISE, 4, 3), (HAVE, 5, 0), (OUT, 4, 0), (THIRD, 0, 3), (AWAY, 0, 2),
    (HERE, 1, 3), (OUT, 4, 1), (CORES, 0, 4), (BACK, 4, 0), (BACK, 4, 1), (FIRST, 0, 4),
    (CORES, 1, 4), (RAISE, 5, 0), (RAISE, 5, 1), (RAISE, 5, 2), (RAISE, 5, 3), (FIRST, 1, 4),
    (THIRD, 1, 3), (OUT, 5, 0), (OUT, 5, 1), (AWAY, 1, 2), (HERE, 0, 2), (CORES, 0, 5),
    (BACK, 5, 0), (BACK, 5, 1), (CORES, 1, 5), (FIRST, 0, 5), (HAVE, 6, 0), (HERE, 1, 2),
    (FIRST, 1, 5), (RAISE, 6, 0), (RAISE, 6, 1), (RAISE, 6, 2), (RAISE, 6, 3), (OUT, 6, 0),
    (THIRD, 0, 2), (HAVE, 7, 0), (OUT, 6, 1), (CORES, 0, 6), (AWAY, 0, 1), (BACK, 6, 0),
    (THIRD, 1, 2), (FIRST, 0, 6), (BACK, 6, 1), (CORES, 1, 6), (RAISE, 7, 0), (HERE, 0, 1),
    (AWAY, 1, 1), (RAISE, 7, 1), (RAISE, 7, 2), (FIRST, 1, 6), (RAISE, 7, 3), (THIRD, 0, 1),
    (OUT, 7, 0), (AWAY, 0, 0), (OUT, 7, 1), (AWAY, 1, 0), (CORES, 0, 7), (HERE, 1, 1),
    (BACK, 7, 0), (FIRST, 0, 7), (BACK, 7, 1), (CORES, 1, 7), (HERE, 0, 0), (FIRST, 1, 7),
    (THIRD, 1, 1), (HERE, 1, 0), (THIRD, 1, 0), (THIRD, 0, 0),
)


def mixture_kernel(
    sizes,
    part_ref,
    cot_ref,
    expert_in_ref,
    shared_in_ref,
    expert_out_ref,
    shared_out_ref,
    select_ref,
    place_ref,
    tokens_ref,
    gain_ref,
    router_ref,
    picked_ref,
    output_ref,
    block_ref,
    residual_grad_ref,
    logit_grad_ref,
    gain_grad_ref,
    rows_ref,
    units_ref,
    residual_all_ref,
    weight_in,
    weight_out,
    rows_buf,
    cot_buf,
    units_buf,
    dots,
    staged_out,
    staged_back,
    gates,
    *rest,
):
    rows, seq, width, owned, part, shared_part, padded, experts = sizes
    out_slots, back_slots = rest[:6], rest[6:12]
    send_sems, recv_sems, load_sems, misc_sems = rest[12:]
    bf16, f32 = jnp.bfloat16, jnp.float32
    place = Place()
    copies = Copies(place, send_sems, recv_sems)
    gather = Gather(place, copies, block_ref, rows_ref, rows)
    sums_out = Sums(place, copies, 0, *out_slots)
    sums_back = Sums(place, copies, 1, *back_slots)
    both = (sums_out, sums_back)

    own = pltpu.make_async_copy(block_ref, gather.view(0, 0, 0, None), misc_sems.at[0])
    attended = sums_out.staged_part(part_ref)
    mine = [
        pltpu.make_async_copy(
            attended(ky, 0),
            staged_back.at[pl.ds(ky * rows, rows), pl.ds(0, width)],
            misc_sems.at[4 + ky],
        )
        for ky in (0, 1)
    ]
    mine.append(
        pltpu.make_async_copy(
            tokens_ref,
            staged_back.at[pl.ds(2 * rows, rows), pl.ds(0, width)],
            misc_sems.at[6],
        )
    )
    for load in mine:
        load.start()
    moves = []
    for c in (0, 1):
        for e in range(owned):
            moves.append(
                (
                    expert_in_ref.at[pl.ds((2 * e + c) * part, part)],
                    weight_in.at[pl.ds(c * padded + e * part, part)],
                )
            )
        moves.append(
            (
                shared_in_ref.at[pl.ds(c * shared_part, shared_part)],
                weight_in.at[pl.ds(c * padded + owned * part, shared_part)],
            )
        )
    moves.append((expert_out_ref, weight_out.at[pl.ds(0, owned * part)]))
    moves.append((shared_out_ref, weight_out.at[pl.ds(owned * part, shared_part)]))
    loads = [
        pltpu.make_async_copy(source, target, load_sems.at[i])
        for i, (source, target) in enumerate(moves)
    ]
    for load in loads:
        load.start()

    order = ORDER

    def span(step):
        return pl.ds(pl.multiple_of(place.sequence(*order[step]) * seq, seq), seq)

    def rows_load(step):
        return pltpu.make_async_copy(rows_ref.at[span(step)], rows_buf, misc_sems.at[1])

    def cot_load(step):
        return pltpu.make_async_copy(cot_ref.at[span(step)], cot_buf, misc_sems.at[2])

    def units_write(step):
        return pltpu.make_async_copy(units_buf, units_ref.at[span(step)], misc_sems.at[3])

    cot_load(0).start()
    used = owned * part + shared_part
    for at in (used, padded + used):
        weight_in[pl.ds(at, padded - used), :] = jnp.zeros((padded - used, width), bf16)
    weight_out[pl.ds(used, padded - used), :] = jnp.zeros((padded - used, width), bf16)
    greet(place, PARTNERS)

    def third_of(ref, i):
        return ref.at[pl.ds(i * rows, rows), pl.ds(0, width)]

    for ky in (1, 0):
        copies.start(("pc", ky), attended(ky, 1), third_of(staged_out, ky), kc=1)
    mine[1].wait()
    copies.arrived(("pc", 1))
    third_of(staged_out, 1)[...] = third_of(staged_out, 1)[...] + third_of(staged_back, 1)[...]
    copies.start(("py", 0), third_of(staged_out, 1), third_of(staged_out, 2), ky=1)
    mine[0].wait()
    copies.arrived(("pc", 0))
    total = third_of(staged_out, 0)[...].astype(f32) + third_of(staged_back, 0)[...].astype(f32)
    mine[2].wait()
    total = total + third_of(staged_back, 2)[...].astype(f32)
    copies.arrived(("py", 0))
    total = total + third_of(staged_out, 2)[...].astype(f32)
    residual_grad_ref[...] = total
    factor = lax.rsqrt(jnp.mean(total * total, axis=-1, keepdims=True) + EPSILON)
    block_ref[:, pl.ds(0, width)] = (total * factor * gain_ref[...]).astype(bf16)
    logits = lax.dot_general(
        block_ref[:, pl.ds(0, width)], router_ref[...], NT_DIMS, preferred_element_type=f32
    )
    lane = lax.broadcasted_iota(jnp.int32, (rows, EXTRA), 1)
    routed = lane < experts
    highest = jnp.max(jnp.where(routed, logits, MASKED), axis=-1, keepdims=True)
    raised = jnp.where(routed, jnp.exp(jnp.where(routed, logits, highest) - highest), 0.0)
    probs = raised / jnp.sum(raised, axis=-1, keepdims=True)
    gates[...] = jnp.where(lane == experts, jax.nn.sigmoid(logits), probs)
    weights = jnp.where(routed, probs * picked_ref[...], gates[...])
    coarse = weights.astype(bf16)
    fine = (weights - coarse.astype(f32)).astype(bf16)
    across = lax.broadcasted_iota(jnp.int32, (EXTRA, EXTRA), 1)
    down = lax.broadcasted_iota(jnp.int32, (EXTRA, EXTRA), 0)
    moved = jnp.where(across == down + experts + 1, 1.0, 0.0).astype(bf16)
    block_ref[:, pl.ds(width, EXTRA)] = (
        coarse.astype(f32) + jnp.dot(fine, moved, preferred_element_type=f32)
    ).astype(bf16)
    copies.sent(("py", 0))
    own.start()

    def raise_tile(at, count):
        here, above = pl.ds(at, count), pl.ds(at + padded, count)
        pair = jnp.concatenate([weight_in[here, :], weight_in[above, :]], axis=0)
        raised = lax.dot_general(
            rows_buf[:, pl.ds(0, width)], pair, NT_DIMS, preferred_element_type=f32
        )
        back = lax.dot_general(
            cot_buf[...], weight_out[here, :], NT_DIMS, preferred_element_type=f32
        )
        scale = jnp.dot(
            rows_buf[:, pl.ds(width, EXTRA)], select_ref[:, here], preferred_element_type=f32
        )
        gate, up = raised[:, :count], raised[:, count:]
        sigmoid_gate = jax.nn.sigmoid(gate)
        active = gate * sigmoid_gate
        hidden = active * up
        dots[...] += jnp.dot(
            (back * hidden).astype(bf16), place_ref[here, :], preferred_element_type=f32
        )
        scaled = back * scale
        units_buf[:, pl.ds(at + 2 * padded, count)] = (hidden * scale).astype(bf16)
        units_buf[:, here] = (
            scaled * up * sigmoid_gate * (1.0 + gate * (1.0 - sigmoid_gate))
        ).astype(bf16)
        units_buf[:, above] = (scaled * active).astype(bf16)

    tile, wide = 256, 512

    tiles = padded // tile
    pieces = tiles + (1 if padded % tile else 0)
    strips = width // wide // 2

    def raise_some(step, first, last):
        if first == 0:
            rows_load(step).wait()
            cot_load(step).wait()
            if step:
                units_write(step - 1).wait()
            else:
                for load in loads:
                    load.wait()
            dots[...] = jnp.zeros_like(dots)
        if min(last, tiles) - first == 1:
            raise_tile(first * tile, tile)
        elif min(last, tiles) > first:

            @pl.loop(first, min(last, tiles))
            def _(j):
                raise_tile(pl.multiple_of(j * tile, tile), tile)

        if last > tiles:
            raise_tile(tiles * tile, padded % tile)
        if last == pieces:
            units_write(step).start()
            if step + 1 < len(order):
                cot_load(step + 1).start()

    def project(first, last, units, weight, staged):
        @pl.loop(first * strips, last * strips)
        def _(n):
            at = pl.ds(pl.multiple_of(n * wide, wide), wide)
            staged[:, at] = jnp.dot(
                units_buf[:, units], weight[:, at], preferred_element_type=f32
            ).astype(bf16)

    def out_some(step, first, last):
        project(first, last, pl.ds(2 * padded, padded), weight_out, staged_out)

    def back_some(step, first, last):
        project(first, last, pl.ds(0, 2 * padded), weight_in, staged_back)
        if last == 2:
            staged_back[:, pl.ds(width, EXTRA)] = dots[...].astype(bf16)

    def have(step):
        if order[step] == (0, 0):
            own.wait()
        gather.have(*order[step])
        rows_load(step).start()

    work = {RAISE: raise_some, OUT: out_some, BACK: back_some}
    moves = {
        BEGIN: gather.begin,
        PASS: gather.first,
        PASS_X: gather.second_x,
        PASS_Y: gather.second_y,
        PASS_LAST: gather.third,
        HAVE: have,
    }
    stages = (staged_out, staged_back)
    at = 0
    while at < len(PLAN):
        kind, a, b = PLAN[at]
        at += 1
        if kind in work:
            last = b + 1
            while at < len(PLAN) and PLAN[at] == (kind, a, last):
                last, at = last + 1, at + 1
            work[kind](a, b, last)
        elif kind in moves:
            moves[kind](a)
        elif kind == CORES:
            both[a].cores(*order[b], both[a].staged_part(stages[a]))
        elif kind == FIRST:
            both[a].first(*order[b], both[a].staged_part(stages[a]))
        elif kind == AWAY:
            both[a].second_away(b)
        elif kind == HERE:
            both[a].second_here(b)
        else:
            both[a].third(b)
    last = len(order) - 1
    own_cot = pltpu.make_async_copy(
        cot_ref.at[pl.ds(pl.multiple_of(place.block(0, 0, 0, 0) * rows, rows), rows)],
        cot_buf.at[pl.ds(0, rows)],
        misc_sems.at[7],
    )
    own_cot.start()
    total = residual_grad_ref[...]
    output_ref[...] = (total + sums_out.total()).astype(bf16)
    own_cot.wait()
    back = sums_back.total()
    factor = lax.rsqrt(jnp.mean(total * total, axis=-1, keepdims=True) + EPSILON)
    normed = total * factor
    held = gates[...]
    extra = back[:, width:]
    pick_grads = jnp.where(routed, extra * picked_ref[...], 0.0)
    probs = jnp.where(routed, held, 0.0)
    inner = jnp.sum(pick_grads * probs, axis=-1, keepdims=True)
    logit_grad = jnp.where(
        lane == experts, extra * held * (1.0 - held), probs * (pick_grads - inner)
    ).astype(bf16)
    logit_grad_ref[...] = logit_grad
    second_grad = back[:, :width] + jnp.dot(
        logit_grad, router_ref[...], preferred_element_type=f32
    )
    scaled = second_grad * gain_ref[...]
    inner = jnp.mean(scaled * normed, axis=-1, keepdims=True)
    cotangent = cot_buf[pl.ds(0, rows), :].astype(f32)
    residual_grad = cotangent + factor * (scaled - normed * inner)
    residual_grad_ref[...] = residual_grad
    gain_grad_ref[...] = jnp.sum(second_grad * normed, axis=0, keepdims=True)
    for ky in (0, 1):
        copies.sent((SUM_CORES, 0) + order[last] + (ky,))
    third_of(staged_out, 0)[...] = residual_grad.astype(bf16)

    def spot(ky, kc):
        start = (place.y_of(ky) * 2 + place.c_of(kc)) * rows
        return residual_all_ref.at[pl.ds(pl.multiple_of(start, rows), rows)]

    shown = pltpu.make_async_copy(third_of(staged_out, 0), spot(0, 0), misc_sems.at[6])
    shown.start()
    copies.start(("gy", 0), third_of(staged_out, 0), spot(0, 0), ky=1)
    copies.start(("gc", 0), third_of(staged_out, 0), spot(0, 0), kc=1)
    copies.arrived(("gy", 0))
    copies.start(("gf", 0), spot(1, 0), spot(1, 0), kc=1)
    units_write(last).wait()
    copies.arrived(("gc", 0))
    copies.arrived(("gf", 0))
    shown.wait()
    for name in copies.made:
        copies.sent(name)


def sum_slots(rows, packed):
    half = rows // 2
    bf16 = jnp.bfloat16
    return [
        pltpu.VMEM((16, rows, packed), bf16),
        pltpu.VMEM((8, half, packed), bf16),
        pltpu.VMEM((4, half, packed), bf16),
        pltpu.VMEM((4, half, packed), bf16),
        pltpu.VMEM((8, half, packed), bf16),
        pltpu.VMEM((3, rows, packed), bf16),
    ]


def mixture(
    attn_part,
    cot_all,
    expert_in,
    shared_win,
    expert_out,
    shared_wout,
    select,
    spots,
    tokens,
    gain,
    router_wide,
    picked,
    experts,
):
    rows, width = tokens.shape
    packed = width + EXTRA
    total_rows = cot_all.shape[0]
    owned, part = expert_out.shape[0], expert_out.shape[1]
    shared_part = shared_wout.shape[0]
    seq = attn_part.shape[0]
    padded = select.shape[1]
    bf16, f32 = jnp.bfloat16, jnp.float32
    vmem = pl.BlockSpec(memory_space=pltpu.VMEM)
    anywhere = pl.BlockSpec(memory_space=pl.ANY)
    copies = GATHER_COPIES + 2 * SUM_COPIES + 6
    return pl.pallas_call(
        functools.partial(
            mixture_kernel, (rows, seq, width, owned, part, shared_part, padded, experts)
        ),
        out_shape=(
            jax.ShapeDtypeStruct((rows, width), bf16),
            jax.ShapeDtypeStruct((rows, packed), bf16),
            jax.ShapeDtypeStruct((rows, width), f32),
            jax.ShapeDtypeStruct((rows, EXTRA), bf16),
            jax.ShapeDtypeStruct((1, width), f32),
            jax.ShapeDtypeStruct((total_rows, packed), bf16),
            jax.ShapeDtypeStruct((total_rows, 3 * padded), bf16),
            jax.ShapeDtypeStruct((seq, width), bf16),
        ),
        in_specs=[anywhere] * 6 + [vmem] * 2 + [anywhere] + [vmem] * 3,
        out_specs=(vmem,) * 5 + (anywhere,) * 3,
        scratch_shapes=[
            pltpu.VMEM((2 * padded, width), bf16),
            pltpu.VMEM((padded, width), bf16),
            pltpu.VMEM((seq, packed), bf16),
            pltpu.VMEM((seq, width), bf16),
            pltpu.VMEM((seq, 3 * padded), bf16),
            pltpu.VMEM((seq, EXTRA), f32),
            pltpu.VMEM((seq, width), bf16),
            pltpu.VMEM((seq, packed), bf16),
            pltpu.VMEM((rows, EXTRA), f32),
        ]
        + sum_slots(rows, width)
        + sum_slots(rows, packed)
        + [
            pltpu.SemaphoreType.DMA((copies,)),
            pltpu.SemaphoreType.DMA((copies,)),
            pltpu.SemaphoreType.DMA((2 * owned + 4,)),
            pltpu.SemaphoreType.DMA((8,)),
        ],
        compiler_params=pltpu.CompilerParams(
            collective_id=0, has_side_effects=True, vmem_limit_bytes=63 * 2**20
        ),
        cost_estimate=pl.CostEstimate(
            flops=2 * total_rows * width * padded * 6,
            bytes_accessed=100 * 2**20,
            transcendentals=total_rows * padded,
        ),
        name="mixture",
    )(
        attn_part,
        cot_all,
        expert_in.transpose(0, 2, 3, 1).reshape(2 * owned * part, width),
        shared_win,
        expert_out.reshape(owned * part, width),
        shared_wout,
        select,
        spots,
        tokens,
        gain,
        router_wide,
        picked,
    )


class Totals:
    def __init__(self, place, copies, value, from_c, from_y, from_x, by_z):
        self.place, self.copies, self.value = place, copies, value
        self.slots = {CORE: from_c, ROW: from_y, COLUMN: from_x}
        self.by_z = by_z

    def send(self, axis):
        self.copies.start((TOTAL, axis), self.value, self.slots[axis], **{axis: 1})

    def add(self, axis):
        self.copies.arrived((TOTAL, axis))
        self.copies.sent((TOTAL, axis))
        self.value[...] = self.value[...] + self.slots[axis][...]

    def send_z(self):
        mine = self.by_z.at[self.place.z]
        mine[...] = self.value[...]
        for kz in (1, 2, 3):
            self.copies.start(("tz", kz), mine, mine, kz=kz)

    def finish(self):
        for kz in (1, 2, 3):
            self.copies.arrived(("tz", kz))
        by_z = self.by_z
        return (by_z[0] + by_z[1]) + (by_z[2] + by_z[3])


class OwnerSums:
    def __init__(self, place, copies, sources, mine, from_x, from_z, sems):
        self.place, self.copies, self.sources = place, copies, sources
        self.mine, self.from_x, self.from_z, self.sems = mine, from_x, from_z, sems

    def view(self, i, kz, kx):
        width = self.mine[i].shape[-2] if i == 0 else self.mine[i].shape[-1]
        at = pl.ds(pl.multiple_of(self.place.sequence(kz, kx) * width, width), width)
        return self.sources[i].at[:, at]

    def begin(self, kz):
        for i in (0, 1):
            self.copies.start(("ox", i, kz), self.view(i, kz, 1), self.from_x[i].at[kz], kx=1)

    def load(self, kz):
        return [
            pltpu.make_async_copy(
                self.view(i, kz, 0), self.mine[i].at[kz], self.sems.at[2 * kz + i]
            )
            for i in (0, 1)
        ]

    def add(self, kz):
        for load in self.load(kz):
            load.wait()
        for i in (0, 1):
            self.copies.arrived(("ox", i, kz))
            held = self.from_x[i].at[kz]
            held[...] = held[...] + self.mine[i][kz]
            if kz in (1, 3):
                self.copies.start(("oz", i, kz), held, self.from_z[i].at[kz // 2], kz=1)

    def relay(self):
        for i in (0, 1):
            self.copies.arrived(("oz", i, 3))
            held = self.from_x[i].at[2]
            held[...] = held[...] + self.from_z[i][1]
            self.copies.start(("oz", i, 2), held, self.from_z[i].at[2], kz=2)

    def finish(self, i, out_ref):
        total = self.from_x[i][0].astype(jnp.float32)
        for kz, slot in ((1, 0), (2, 2)):
            self.copies.arrived(("oz", i, kz))
            total = total + self.from_z[i][slot].astype(jnp.float32)
        out_ref[...] = total


CLOSING_COPIES = 14 + 14 + 6 + 3
TURN, PRODUCT, GIVE, BEGIN_X, ADD, RELAY, TOTALS, PASS_FIRST, END_FIRST = range(9)
CLOSING_ORDER = (2, 3, 1, 0)
CLOSING_PLAN = (
    (TURN, 0, 0, 0), (PASS_FIRST, 0, 0, 0), (TURN, 1, 0, 0), (BEGIN_X, 3, 0, 0), (TURN, 2, 0, 0),
    (TURN, 3, 0, 0), (TURN, 4, 0, 0), (TURN, 5, 0, 0), (TURN, 6, 0, 0), (TURN, 7, 0, 0),
    (TURN, 8, 0, 0), (END_FIRST, 0, 0, 0), (TOTALS, 0, 0, 0), (TURN, 9, 0, 0), (TURN, 10, 0, 0),
    (TURN, 11, 0, 0), (TURN, 12, 0, 0), (TOTALS, 1, 0, 0), (TURN, 13, 0, 0), (TURN, 14, 0, 0),
    (TURN, 15, 0, 0), (TURN, 16, 0, 0), (BEGIN_X, 2, 0, 0), (TURN, 17, 0, 0), (TURN, 18, 0, 0),
    (TOTALS, 2, 0, 0), (TURN, 19, 0, 0), (TURN, 20, 0, 0), (BEGIN_X, 1, 0, 0), (ADD, 3, 0, 0),
    (PRODUCT, 2, 0, 0), (PRODUCT, 2, 0, 1), (PRODUCT, 2, 1, 0), (PRODUCT, 2, 1, 1),
    (GIVE, 0, 2, 0), (TOTALS, 3, 0, 0), (PRODUCT, 2, 2, 0), (PRODUCT, 2, 2, 1), (GIVE, 1, 2, 0),
    (PRODUCT, 3, 0, 0), (PRODUCT, 3, 0, 1), (PRODUCT, 3, 1, 0), (PRODUCT, 3, 1, 1),
    (GIVE, 0, 3, 0), (PRODUCT, 3, 2, 0), (PRODUCT, 3, 2, 1), (GIVE, 1, 3, 0), (PRODUCT, 1, 0, 0),
    (PRODUCT, 1, 0, 1), (PRODUCT, 1, 1, 0), (PRODUCT, 1, 1, 1), (GIVE, 0, 1, 0), (ADD, 2, 0, 0),
    (PRODUCT, 1, 2, 0), (RELAY, 0, 0, 0), (PRODUCT, 1, 2, 1), (ADD, 1, 0, 0), (BEGIN_X, 0, 0, 0),
    (GIVE, 1, 1, 0), (PRODUCT, 0, 0, 0), (PRODUCT, 0, 0, 1), (PRODUCT, 0, 1, 0),
    (PRODUCT, 0, 1, 1), (GIVE, 0, 0, 0), (ADD, 0, 0, 0), (PRODUCT, 0, 2, 0), (PRODUCT, 0, 2, 1),
    (GIVE, 1, 0, 0),
)


def closing_kernel(
    sizes,
    rows_ref,
    cot_ref,
    units_ref,
    att_in_ref,
    att_out_ref,
    first_ref,
    small_ref,
    tokens_ref,
    residual_grad_ref,
    gain_ref,
    input_grad_ref,
    att_in_out,
    att_out_out,
    small_out,
    expert_in_out,
    expert_out_out,
    shared_in_out,
    shared_out_out,
    chunks,
    turned,
    columns,
    grads,
    shared_in_send,
    shared_out_send,
    own_in,
    own_out,
    in_x,
    out_x,
    in_z,
    out_z,
    small,
    small_c,
    small_y,
    small_x,
    small_z,
    first_mine,
    first_got,
    send_sems,
    recv_sems,
    own_sems,
    chunk_sems,
    column_sems,
    write_sems,
    keep_sems,
):
    width, owned, part, shared_part, owner_width, padded, gain_row = sizes
    rows = tokens_ref.shape[0]
    f32, bf16 = jnp.float32, jnp.bfloat16
    place = Place()
    copies = Copies(place, send_sems, recv_sems)
    totals = Totals(place, copies, small, small_c, small_y, small_x, small_z)
    owners = OwnerSums(
        place,
        copies,
        (att_in_ref, att_out_ref),
        (own_in, own_out),
        (in_x, out_x),
        (in_z, out_z),
        own_sems,
    )
    wide = 2 * owner_width
    cut = owned * part
    lanes = 128
    per_kind = padded // lanes

    def chunk_load(i, slot):
        at = pl.ds(pl.multiple_of(i * lanes, lanes), lanes)
        return pltpu.make_async_copy(
            units_ref.at[:, at], chunks.at[slot], chunk_sems.at[slot]
        )

    def column_load(kz, which):
        source = (rows_ref, cot_ref)[which]
        at = pl.ds(pl.multiple_of(place.z_of(kz) * wide, wide), wide)
        return pltpu.make_async_copy(source.at[:, at], columns.at[which], column_sems.at[which])

    order = CLOSING_ORDER
    chunk_load(0, 0).start()
    for kz in range(4):
        for load in owners.load(kz):
            load.start()
    small[...] = small_ref[...]

    def first_part(ky, kc):
        start = (place.y_of(ky) * 2 + place.c_of(kc)) * rows
        return first_ref.at[pl.ds(pl.multiple_of(start, rows), rows)]

    first_loads = [
        pltpu.make_async_copy(first_part(ky, 0), first_mine.at[ky], keep_sems.at[2 + ky])
        for ky in (0, 1)
    ]
    for load in first_loads:
        load.start()
    greet(place, PARTNERS + FARTHER)
    for ky in (1, 0):
        copies.start(("fc", ky), first_part(ky, 1), first_got.at[ky], kc=1)
    column_load(order[0], 0).start()
    column_load(order[0], 1).start()

    def turn(first, last):
        @pl.loop(first, last)
        def _(i):
            slot = i % 2
            chunk_load(i, slot).wait()

            @pl.when(i + 1 < 3 * per_kind)
            def _():
                chunk_load(i + 1, 1 - slot).start()

            to = pl.ds(pl.multiple_of(i * lanes, lanes), lanes)

            @pl.loop(0, turned.shape[1] // wide)
            def _(r):
                at = pl.ds(pl.multiple_of(r * wide, wide), wide)
                turned[to, at] = chunks[slot, at, :].T

    def span(kz):
        return pl.ds(pl.multiple_of(place.z_of(kz) * wide, wide), wide)

    def writes(kz, kind):
        found = []
        for e in range(owned):
            if kind < 2:
                target = expert_in_out.at[pl.ds((2 * e + kind) * part, part), span(kz)]
            else:
                target = expert_out_out.at[pl.ds(e * part, part), span(kz)]
            found.append(
                pltpu.make_async_copy(
                    grads.at[kind, pl.ds(e * part, part)], target, write_sems.at[kind * owned + e]
                )
            )
        return found

    def share(kz, which):
        sent = (shared_in_send, shared_out_send)[which]
        target = (shared_in_out, shared_out_out)[which].at[place.sequence(0, 0)]
        for kx in (1, 0):
            at = pl.ds(pl.multiple_of(place.x_of(kx) * owner_width, owner_width), owner_width)
            source = sent.at[kz, :, at]
            if kz or kx:
                copies.start((SHARE, which, kz, kx), source, target, kz=kz, kx=kx)
            else:
                pltpu.make_async_copy(source, target, keep_sems.at[which]).start()

    def product(kz, kind, first, last):
        which, step = kind // 2, order.index(kz)
        if first == 0:
            if kind != 1:
                column_load(kz, which).wait()
            if step:
                for write in writes(order[step - 1], kind):
                    write.wait()

        @pl.loop(first, last)
        def _(n):
            at = pl.ds(pl.multiple_of(n * owner_width, owner_width), owner_width)
            grads[kind, :, at] = jnp.dot(
                turned[pl.ds(kind * padded, padded), :],
                columns[which, :, at],
                preferred_element_type=f32,
            ).astype(bf16)

        if last < 2:
            return
        if step < 3 and kind:
            column_load(order[step + 1], which).start()
        for write in writes(kz, kind):
            write.start()
        shared = grads[kind, pl.ds(cut, shared_part), :]
        if kind < 2:
            shared_in_send[kz, pl.ds(kind * shared_part, shared_part), :] = shared
        else:
            shared_out_send[kz] = shared

    def pass_first():
        first_loads[1].wait()
        copies.arrived(("fc", 1))
        first_got[1] = first_got[1] + first_mine[1]
        copies.start(("fy", 0), first_got.at[1], first_got.at[2], ky=1)

    def end_first():
        first_loads[0].wait()
        copies.arrived(("fc", 0))
        copies.arrived(("fy", 0))
        grad = first_got[0].astype(f32) + first_mine[0].astype(f32)
        grad = grad + first_got[2].astype(f32)
        inputs = tokens_ref[...].astype(f32)
        factor = lax.rsqrt(jnp.mean(inputs * inputs, axis=-1, keepdims=True) + EPSILON)
        normed = inputs * factor
        scaled = grad * gain_ref[...]
        inner = jnp.mean(scaled * normed, axis=-1, keepdims=True)
        input_grad_ref[...] = residual_grad_ref[...] + factor * (scaled - normed * inner)
        small[pl.ds(gain_row, 1), :] = jnp.sum(grad * normed, axis=0, keepdims=True)

    axes = (CORE, ROW, COLUMN)

    def totals_step(n):
        if n:
            totals.add(axes[n - 1])
        if n < 3:
            totals.send(axes[n])
        else:
            totals.send_z()

    at = 0
    while at < len(CLOSING_PLAN):
        kind, a, b, c = CLOSING_PLAN[at]
        at += 1
        if kind == TURN:
            last = a + 1
            while CLOSING_PLAN[at] == (TURN, last, 0, 0):
                last, at = last + 1, at + 1
            turn(a, last)
        elif kind == PRODUCT:
            last = c + 1
            if CLOSING_PLAN[at] == (PRODUCT, a, b, last):
                last, at = last + 1, at + 1
            product(a, b, c, last)
        elif kind == GIVE:
            share(b, a)
        elif kind == BEGIN_X:
            owners.begin(a)
        elif kind == ADD:
            owners.add(a)
        elif kind == RELAY:
            owners.relay()
        elif kind == PASS_FIRST:
            pass_first()
        elif kind == END_FIRST:
            end_first()
        else:
            totals_step(a)
    small_out[...] = totals.finish()
    owners.finish(0, att_in_out)
    owners.finish(1, att_out_out)
    for kind in (0, 1, 2):
        for write in writes(order[-1], kind):
            write.wait()
    for which in (0, 1):
        sent = (shared_in_send, shared_out_send)[which]
        target = (shared_in_out, shared_out_out)[which].at[place.sequence(0, 0)]
        at = pl.ds(pl.multiple_of(place.x_of(0) * owner_width, owner_width), owner_width)
        pltpu.make_async_copy(sent.at[0, :, at], target, keep_sems.at[which]).wait()
    for name in copies.made:
        if name[0] == SHARE:
            copies.arrived(name)
    for name in copies.made:
        copies.sent(name)


def closing(
    rows_all,
    cot_all,
    units_all,
    att_in,
    att_out,
    first_rows,
    small,
    tokens,
    residual_grad,
    gain,
    gain_row,
    owned,
    part,
    shared_part,
):
    total_rows, width = cot_all.shape
    rows = tokens.shape[0]
    padded = units_all.shape[1] // 3
    owners = lax.axis_size(EXPERT)
    owner_width = width // owners
    wide = 2 * owner_width
    heads_width = att_in.shape[2]
    bf16, f32 = jnp.bfloat16, jnp.float32
    vmem = pl.BlockSpec(memory_space=pltpu.VMEM)
    anywhere = pl.BlockSpec(memory_space=pl.ANY)
    block_in = (3, owner_width, heads_width)
    block_out = (heads_width, owner_width)
    return pl.pallas_call(
        functools.partial(
            closing_kernel, (width, owned, part, shared_part, owner_width, padded, gain_row)
        ),
        out_shape=(
            jax.ShapeDtypeStruct((rows, width), f32),
            jax.ShapeDtypeStruct(block_in, f32),
            jax.ShapeDtypeStruct(block_out, f32),
            jax.ShapeDtypeStruct(small.shape, f32),
            jax.ShapeDtypeStruct((2 * owned * part, width), bf16),
            jax.ShapeDtypeStruct((owned * part, width), bf16),
            jax.ShapeDtypeStruct((owners, 2 * shared_part, owner_width), bf16),
            jax.ShapeDtypeStruct((owners, shared_part, owner_width), bf16),
        ),
        in_specs=[anywhere] * 6 + [vmem] * 4,
        out_specs=(vmem,) * 4 + (anywhere,) * 4,
        scratch_shapes=[
            pltpu.VMEM((2, total_rows, 128), bf16),
            pltpu.VMEM((3 * padded, total_rows), bf16),
            pltpu.VMEM((2, total_rows, wide), bf16),
            pltpu.VMEM((3, padded, wide), bf16),
            pltpu.VMEM((4, 2 * shared_part, wide), bf16),
            pltpu.VMEM((4, shared_part, wide), bf16),
            pltpu.VMEM((4,) + block_in, bf16),
            pltpu.VMEM((4,) + block_out, bf16),
            pltpu.VMEM((4,) + block_in, bf16),
            pltpu.VMEM((4,) + block_out, bf16),
            pltpu.VMEM((3,) + block_in, bf16),
            pltpu.VMEM((3,) + block_out, bf16),
        ]
        + [pltpu.VMEM(small.shape, f32)] * 4
        + [
            pltpu.VMEM((4,) + small.shape, f32),
            pltpu.VMEM((2, rows, width), bf16),
            pltpu.VMEM((3, rows, width), bf16),
            pltpu.SemaphoreType.DMA((CLOSING_COPIES,)),
            pltpu.SemaphoreType.DMA((CLOSING_COPIES,)),
            pltpu.SemaphoreType.DMA((8,)),
            pltpu.SemaphoreType.DMA((2,)),
            pltpu.SemaphoreType.DMA((2,)),
            pltpu.SemaphoreType.DMA((3 * owned,)),
            pltpu.SemaphoreType.DMA((4,)),
        ],
        compiler_params=pltpu.CompilerParams(
            collective_id=1, has_side_effects=True, vmem_limit_bytes=62 * 2**20
        ),
        cost_estimate=pl.CostEstimate(
            flops=2 * total_rows * width * padded * 3,
            bytes_accessed=150 * 2**20,
            transcendentals=0,
        ),
        name="closing",
    )(
        rows_all,
        cot_all,
        units_all,
        att_in,
        att_out,
        first_rows,
        small,
        tokens,
        residual_grad,
        gain,
    )


OPENING_COPIES = 6 + 8 + 3 + 14 + 31
SPREAD_Z, RELAY_Z, PASS_ON_X, SLICES, NORMED = range(5)
COT_Z, COT_RELAY, COT_X, COT_Y, COT_CORE = range(5, 10)
OPENING_PLAN = (
    (SPREAD_Z, 1, 0), (COT_X, 0, 0), (COT_Z, 2, 0), (PASS_ON_X, 0, 0), (COT_X, 2, 0),
    (PASS_ON_X, 1, 0), (COT_Z, 1, 0), (SPREAD_Z, 2, 0), (COT_Y, 2, 0), (COT_Y, 0, 1),
    (SLICES, 2, 1), (COT_Y, 2, 1), (COT_X, 1, 0), (COT_RELAY, 0, 0), (COT_Y, 1, 0),
    (COT_CORE, 2, 0), (COT_Y, 0, 0), (COT_X, 3, 0), (SLICES, 1, 0), (COT_CORE, 1, 0),
    (COT_Y, 1, 1), (SLICES, 0, 1), (RELAY_Z, 0, 0), (COT_CORE, 0, 0), (PASS_ON_X, 2, 0),
    (COT_Y, 3, 0), (SLICES, 3, 1), (COT_Y, 3, 1), (COT_CORE, 3, 1), (COT_CORE, 0, 1),
    (COT_CORE, 2, 1), (SLICES, 2, 0), (NORMED, 0, 0), (COT_CORE, 1, 1), (SLICES, 1, 1),
    (SLICES, 3, 0), (PASS_ON_X, 3, 0), (COT_CORE, 3, 0),
)


def opening_kernel(
    sizes,
    normed_ref,
    att_in_ref,
    att_out_ref,
    shared_in_ref,
    shared_out_ref,
    cot_ref,
    normed_all,
    att_in_all,
    att_out_all,
    shared_in_all,
    shared_out_all,
    cot_all,
    send_sems,
    recv_sems,
    own_sems,
):
    rows, owner_width, shared_part = sizes
    place = Place()
    copies = Copies(place, send_sems, recv_sems)

    def in_view(kz, kx):
        at = pl.ds(pl.multiple_of(place.sequence(kz, kx) * owner_width, owner_width), owner_width)
        return att_in_all.at[:, at]

    def out_view(kz, kx):
        return att_out_all.at[place.sequence(kz, kx)]

    here = pl.ds(
        pl.multiple_of(place.sequence(0, 0) * owner_width, owner_width), owner_width
    )
    spot = pl.ds(pl.multiple_of((place.y * 2 + place.c) * rows, rows), rows)

    def shared_block(kz, kx):
        owner = place.sequence(kz, kx)
        at = pl.ds(pl.multiple_of(owner * shared_part, shared_part), shared_part)
        return (
            (shared_in_ref.at[owner], shared_in_all.at[:, here]),
            (shared_out_ref.at[at], shared_out_all.at[:, here]),
        )

    def cot_view(kz, kx, ky):
        start = place.block(kz, kx, ky, 0) * rows
        return cot_all.at[pl.ds(pl.multiple_of(start, rows), rows)]

    keeps = [
        (normed_ref, normed_all.at[spot]),
        (att_in_ref, in_view(0, 0)),
        (att_out_ref, out_view(0, 0)),
        (cot_ref, cot_view(0, 0, 0)),
    ] + list(shared_block(0, 0))
    keeps = [
        pltpu.make_async_copy(source, target, own_sems.at[i])
        for i, (source, target) in enumerate(keeps)
    ]
    for keep in keeps:
        keep.start()
    greet(place, PARTNERS + FARTHER + [dict(ky=1, kc=1)])

    def spread_z(kz, _):
        copies.start(("zi", kz), att_in_ref, in_view(0, 0), kz=kz)
        copies.start(("zo", kz), att_out_ref, out_view(0, 0), kz=kz)

    def relay_z(_, __):
        copies.arrived(("zi", 2))
        copies.start(("zi", 3), in_view(2, 0), in_view(2, 0), kz=1)
        copies.arrived(("zo", 2))
        copies.start(("zo", 3), out_view(2, 0), out_view(2, 0), kz=1)

    def pass_x(kz, _):
        if kz:
            copies.arrived(("zi", kz))
        source = in_view(kz, 0) if kz else att_in_ref
        copies.start(("xi", kz), source, in_view(kz, 0), kx=1)
        if kz:
            copies.arrived(("zo", kz))
        source = out_view(kz, 0) if kz else att_out_ref
        copies.start(("xo", kz), source, out_view(kz, 0), kx=1)

    def slices(kz, kx):
        for which, (source, target) in enumerate(shared_block(kz, kx)):
            copies.start((SHARE, which, kz, kx), source, target, kz=kz, kx=kx)

    def spread_normed(_, __):
        for ky, kc in ((0, 1), (1, 0), (1, 1)):
            copies.start(("n", ky, kc), normed_ref, normed_all.at[spot], ky=ky, kc=kc)

    def cot_send(name, from_z, from_x, from_y, **partner):
        held = cot_view(from_z, from_x, from_y)
        source = held if from_z or from_x or from_y else cot_ref
        copies.start(name, source, held, **partner)

    def cot_z(kz, _):
        cot_send(("cz", kz), 0, 0, 0, kz=kz)

    def cot_relay(_, __):
        copies.arrived(("cz", 2))
        cot_send(("cz", 3), 2, 0, 0, kz=1)

    def cot_x(kz, _):
        if kz:
            copies.arrived(("cz", kz))
        cot_send(("cx", kz), kz, 0, 0, kx=1)
        cot_send(("cs", kz, 0, 0), kz, 0, 0, kc=1)

    def cot_y(kz, kx):
        if kx:
            copies.arrived(("cx", kz))
        cot_send(("cy", kz, kx), kz, kx, 0, ky=1)
        if kx:
            cot_send(("cs", kz, 1, 0), kz, 1, 0, kc=1)

    def cot_core(kz, kx):
        copies.arrived(("cy", kz, kx))
        cot_send(("cs", kz, kx, 1), kz, kx, 1, kc=1)

    moves = {
        SPREAD_Z: spread_z,
        RELAY_Z: relay_z,
        PASS_ON_X: pass_x,
        SLICES: slices,
        NORMED: spread_normed,
        COT_Z: cot_z,
        COT_RELAY: cot_relay,
        COT_X: cot_x,
        COT_Y: cot_y,
        COT_CORE: cot_core,
    }
    for kind, a, b in OPENING_PLAN:
        moves[kind](a, b)
    for keep in keeps:
        keep.wait()
    for name in copies.made:
        copies.arrived(name)
    for name in copies.made:
        copies.sent(name)


def opening(normed, att_in, att_out, shared_in, shared_out, cotangent):
    rows, width = normed.shape
    parts, owner_width, heads_width = att_in.shape
    owners = lax.axis_size(EXPERT)
    shards = lax.axis_size(SHARD)
    shared_part = shared_out.shape[0] // owners
    anywhere = pl.BlockSpec(memory_space=pl.ANY)
    bf16 = jnp.bfloat16
    return pl.pallas_call(
        functools.partial(opening_kernel, (rows, owner_width, shared_part)),
        out_shape=(
            jax.ShapeDtypeStruct((rows * shards, width), bf16),
            jax.ShapeDtypeStruct((parts, owner_width * owners, heads_width), bf16),
            jax.ShapeDtypeStruct((owners,) + att_out.shape, bf16),
            jax.ShapeDtypeStruct((2 * shared_part, width), bf16),
            jax.ShapeDtypeStruct((shared_part, width), bf16),
            jax.ShapeDtypeStruct((rows * shards * owners, width), bf16),
        ),
        in_specs=[anywhere] * 6,
        out_specs=(anywhere,) * 6,
        scratch_shapes=[
            pltpu.SemaphoreType.DMA((OPENING_COPIES,)),
            pltpu.SemaphoreType.DMA((OPENING_COPIES,)),
            pltpu.SemaphoreType.DMA((6,)),
        ],
        compiler_params=pltpu.CompilerParams(
            collective_id=2, has_side_effects=True, vmem_limit_bytes=62 * 2**20
        ),
        cost_estimate=pl.CostEstimate(
            flops=10**11, bytes_accessed=600 * 2**20, transcendentals=0
        ),
        name="opening",
    )(normed, att_in, att_out, shared_in, shared_out, cotangent)


def attention_forward(queries, keys_all, values, score_scale):
    scores = block_scores(queries, keys_all, 0, score_scale)
    highest = jnp.max(scores, axis=-1, keepdims=True)
    raised = jnp.exp(scores - highest)
    probs = raised / jnp.sum(raised, axis=-1, keepdims=True)
    mixed_out = jnp.einsum(
        "hqk,khd->qhd", probs.astype(jnp.bfloat16), values, preferred_element_type=jnp.float32
    )
    return mixed_out, probs


def attention_backward(queries, keys_all, values, probs, grad_out, score_scale):
    value_grad = jnp.einsum(
        "hqk,qhd->khd", probs.astype(jnp.bfloat16), grad_out, preferred_element_type=jnp.float32
    )
    prob_grad = jnp.einsum("qhd,khd->hqk", grad_out, values, preferred_element_type=jnp.float32)
    score_grad = (
        probs * (prob_grad - jnp.sum(prob_grad * probs, axis=-1, keepdims=True))
    ).astype(jnp.bfloat16)
    query_grad = jnp.einsum(
        "hqk,khd->qhd", score_grad, keys_all, preferred_element_type=jnp.float32
    )
    key_grad = jnp.einsum("hqk,qhd->khd", score_grad, queries, preferred_element_type=jnp.float32)
    return query_grad * score_scale, key_grad * score_scale, value_grad


def local_gather(
    tokens,
    first_gain,
    attention_in,
    attention_bias,
    attention_out,
    second_gain,
    router,
    shared_gate,
    shared_in,
    shared_out,
    expert_in,
    expert_out,
    cotangent,
    expert_picks,
):
    bf16, f32 = jnp.bfloat16, jnp.float32
    local_rows, width = tokens.shape
    shards = lax.axis_size(SHARD)
    owners = lax.axis_size(EXPERT)
    owner = lax.axis_index(EXPERT)
    seq_length = local_rows * shards
    experts = router.shape[1]
    owned = expert_in.shape[0]
    part = expert_in.shape[3]
    heads_here = attention_bias.shape[1]
    head_dim = attention_bias.shape[2] * owners
    score_scale = head_dim ** (-0.5)
    shared_part = shared_in.shape[2] // owners
    slice_rows = width // owners
    cosine_table, sine_table = rope_tables(seq_length, head_dim)

    inputs = tokens.astype(f32)
    first_norm, first_factor = normalize(inputs)
    first_low = (first_norm * first_gain).astype(bf16)
    small = jnp.concatenate(
        [router.reshape(-1), shared_gate, attention_bias.reshape(-1)]
    )
    small_rows = -(-small.shape[0] // slice_rows)
    small_rows = -(-small_rows // 16) * 16
    small = jnp.pad(small, (0, small_rows * slice_rows - small.shape[0]))
    small = small.reshape(small_rows, slice_rows)
    shared_blocks = shared_in.transpose(1, 2, 0).reshape(2, owners, shared_part, slice_rows)
    shared_blocks = shared_blocks.transpose(1, 0, 2, 3).reshape(owners, -1, slice_rows)
    normed_all, att_in, out_small, shared_win, shared_wout, cot_all = opening(
        first_low,
        attention_in.transpose(1, 0, 2),
        jnp.concatenate([attention_out, small], axis=0),
        shared_blocks,
        shared_out,
        cotangent,
    )
    att_out = out_small[:, : attention_out.shape[0]].transpose(1, 0, 2)
    att_out = att_out.reshape(attention_out.shape[0], width)
    small_all = out_small[:, attention_out.shape[0] :].reshape(owners, -1)
    router_size = router.size
    router_full = small_all[:, :router_size].reshape(width, experts)
    gate_full = small_all[:, router_size : router_size + slice_rows].reshape(width)
    bias_start = router_size + slice_rows
    att_bias = small_all[:, bias_start : bias_start + attention_bias.size]
    att_bias = att_bias.reshape((owners,) + attention_bias.shape).transpose(1, 2, 0, 3)
    att_bias = att_bias.reshape(3, heads_here * head_dim)

    projected = jnp.einsum("sd,cdf->scf", normed_all, att_in, preferred_element_type=f32)
    projected = projected + att_bias.astype(f32)[None]
    projected = projected.reshape(seq_length, 3, heads_here, head_dim)
    queries = rotate(projected[:, 0], cosine_table, sine_table).astype(bf16)
    keys_all = rotate(projected[:, 1], cosine_table, sine_table).astype(bf16)
    values = projected[:, 2].astype(bf16)
    attended, probs = attention_forward(queries, keys_all, values, score_scale)
    attended_low = attended.astype(bf16).reshape(seq_length, -1)
    attn_part = jnp.dot(attended_low, att_out, preferred_element_type=f32)
    router_wide = jnp.concatenate([router_full.T, gate_full[None]], axis=0)
    router_wide = jnp.pad(router_wide, ((0, EXTRA - experts - 1), (0, 0)))
    picked = jnp.sum(
        (
            expert_picks[:, :, None] == jnp.arange(EXTRA, dtype=jnp.int32)[None, None, :]
        ).astype(f32),
        axis=1,
    )
    units = owned * part + shared_part
    padded = -(-units // 128) * 128
    unit = jnp.arange(padded)
    column = jnp.where(unit < owned * part, owner * owned + unit // part, experts)
    column = jnp.where(unit < units, column, -1)
    kinds = jnp.arange(EXTRA)
    spots = (kinds[None, :] == column[:, None]).astype(bf16)
    finer = jnp.where(unit < units, column + experts + 1, -1)
    select = (kinds[:, None] == column[None, :]) | (kinds[:, None] == finer[None, :])
    (
        output,
        second_block,
        residual_grad,
        logit_grad,
        second_gain_grad,
        rows_all,
        units_all,
        residual_all,
    ) = mixture(
        attn_part.astype(bf16),
        cot_all,
        expert_in,
        shared_win,
        expert_out,
        shared_wout,
        select.astype(bf16),
        spots,
        tokens,
        second_gain[None],
        router_wide,
        picked,
        experts,
    )
    first_dims = (((0,), (0,)), ((), ()))
    att_out_grad = lax.dot_general(
        attended_low, residual_all, first_dims, preferred_element_type=f32
    )
    attended_grad = lax.dot_general(
        residual_all, att_out, (((1,), (1,)), ((), ())), preferred_element_type=f32
    )
    attended_grad = attended_grad.astype(bf16).reshape(seq_length, heads_here, head_dim)
    query_grad, key_grad, value_grad = attention_backward(
        queries, keys_all, values, probs, attended_grad, score_scale
    )
    projected_grad = jnp.stack(
        [
            rotate_back(query_grad, cosine_table, sine_table),
            rotate_back(key_grad, cosine_table, sine_table),
            value_grad,
        ],
        axis=1,
    )
    projected_grad = projected_grad.astype(bf16).reshape(seq_length, 3, heads_here * head_dim)
    att_in_grad = jnp.einsum("sd,scf->cdf", normed_all, projected_grad, preferred_element_type=f32)
    att_bias_grad = jnp.sum(projected_grad.astype(f32), axis=0)
    first_part = jnp.einsum("scf,cdf->sd", projected_grad, att_in, preferred_element_type=f32)
    vec_grads = lax.dot_general(
        logit_grad[:, : experts + 1],
        second_block[:, :width],
        first_dims,
        preferred_element_type=f32,
    )
    bias_wide = jnp.zeros((3, shards, heads_here * head_dim), f32)
    bias_wide = lax.dynamic_update_slice_in_dim(
        bias_wide, att_bias_grad[:, None], lax.axis_index(SHARD), 1
    )
    bias_rows = bias_wide.size // width
    first_bias = experts + 3
    small = jnp.concatenate(
        [vec_grads, second_gain_grad, jnp.zeros((1, width), f32), bias_wide.reshape(-1, width)]
    )
    small = jnp.pad(small, ((0, -small.shape[0] % 8), (0, 0)))
    (
        input_grad,
        att_in_local,
        att_out_local,
        summed,
        expert_in_grad,
        expert_out_grad,
        shared_in_local,
        shared_out_local,
    ) = closing(
        rows_all,
        cot_all,
        units_all,
        att_in_grad.astype(bf16),
        att_out_grad.astype(bf16),
        first_part.astype(bf16),
        small,
        tokens,
        residual_grad,
        first_gain[None],
        experts + 2,
        owned,
        part,
        shared_part,
    )
    expert_in_grad = expert_in_grad.reshape(owned, 2, part, width).transpose(0, 3, 1, 2)
    expert_in_grad = expert_in_grad.astype(f32)
    expert_out_grad = expert_out_grad.reshape(owned, part, width).astype(f32)
    shared_in_local = shared_in_local.reshape(owners, 2, shared_part, slice_rows)
    shared_in_local = shared_in_local.transpose(3, 1, 0, 2).reshape(slice_rows, 2, -1).astype(f32)
    shared_out_local = shared_out_local.reshape(-1, slice_rows).astype(f32)
    vec_local = lax.dynamic_slice_in_dim(
        summed[: experts + 1], owner * slice_rows, slice_rows, axis=1
    )
    bias_all = summed[first_bias : first_bias + bias_rows].reshape(
        3, shards, heads_here, owners, head_dim // owners
    )
    att_bias_local = lax.dynamic_index_in_dim(bias_all, lax.axis_index(SHARD), 1, False)
    att_bias_local = lax.dynamic_index_in_dim(att_bias_local, owner, 2, False)
    return (
        output,
        input_grad,
        summed[experts + 2],
        att_in_local.transpose(1, 0, 2),
        att_bias_local,
        att_out_local,
        summed[experts + 1],
        vec_local[:experts].T,
        vec_local[experts],
        shared_in_local,
        shared_out_local,
        expert_in_grad,
        expert_out_grad,
    )


def solution(mesh):
    in_specs = (
        P((EXPERT, SHARD), None),
        P(),
        P(EXPERT, None, SHARD),
        P(None, SHARD, EXPERT),
        P(SHARD, EXPERT),
        P(),
        P(EXPERT, None),
        P(EXPERT),
        P(EXPERT, None, SHARD),
        P(SHARD, EXPERT),
        P(EXPERT, None, None, SHARD),
        P(EXPERT, SHARD, None),
        P((EXPERT, SHARD), None),
        P((EXPERT, SHARD), None),
    )
    out_specs = (
        P((EXPERT, SHARD), None),
        P((EXPERT, SHARD), None),
        P(),
        P(EXPERT, None, SHARD),
        P(None, SHARD, EXPERT),
        P(SHARD, EXPERT),
        P(),
        P(EXPERT, None),
        P(EXPERT),
        P(EXPERT, None, SHARD),
        P(SHARD, EXPERT),
        P(EXPERT, None, None, SHARD),
        P(EXPERT, SHARD, None),
    )
    plan = local_gather if mesh.size <= 32 else local_exchange
    return jax.shard_map(plan, mesh=mesh, in_specs=in_specs, out_specs=out_specs, check_vma=False)
```

```python
import functools

import jax
import jax.numpy as jnp
from jax import lax
from jax.experimental import pallas as pl
from jax.experimental.pallas import tpu as pltpu
from jax.sharding import PartitionSpec as P

EPSILON = 1e-06
ROPE_BASE = 1000000.0
MASKED = -1e30
EXPERT, SHARD = "expert", "shard"
CORE, ROW, COLUMN = "kc", "ky", "kx"
SUM_CORES, SHARE, TOTAL = "sc", "share", "t"


def normalize(activations):
    factor = lax.rsqrt(jnp.mean(activations * activations, axis=-1, keepdims=True) + EPSILON)
    return (activations * factor, factor)


def norm_back(incoming, normed, factor, gain_vec):
    scaled = incoming * gain_vec
    inner_mean = jnp.mean(scaled * normed, axis=-1, keepdims=True)
    return (factor * (scaled - normed * inner_mean), jnp.sum(incoming * normed, axis=0))


def rope_tables(length, head_dim):
    half_dim = head_dim // 2
    frequency = jnp.power(ROPE_BASE, -jnp.arange(half_dim, dtype=jnp.float32) * (2.0 / head_dim))
    angles = jnp.arange(length, dtype=jnp.float32)[:, None] * frequency[None, :]
    return (
        jnp.concatenate([jnp.cos(angles), jnp.cos(angles)], axis=-1),
        jnp.concatenate([jnp.sin(angles), jnp.sin(angles)], axis=-1),
    )


def rotate(values, cosine_table, sine_table):
    half_dim = values.shape[-1] // 2
    turned = jnp.concatenate([-values[..., half_dim:], values[..., :half_dim]], axis=-1)
    return values * cosine_table[:, None, :] + turned * sine_table[:, None, :]


def rotate_back(incoming, cosine_table, sine_table):
    half_dim = incoming.shape[-1] // 2
    scaled = incoming * sine_table[:, None, :]
    turned = jnp.concatenate([scaled[..., half_dim:], -scaled[..., :half_dim]], axis=-1)
    return incoming * cosine_table[:, None, :] + turned


def block_scores(query_block, keys_all, first_row, score_scale):
    scores = (
        jnp.einsum("qhd,khd->hqk", query_block, keys_all, preferred_element_type=jnp.float32)
        * score_scale
    )
    row_pos = first_row + jnp.arange(query_block.shape[0], dtype=jnp.int32)
    col_pos = jnp.arange(keys_all.shape[0], dtype=jnp.int32)
    return jnp.where(col_pos[None, None, :] <= row_pos[None, :, None], scores, MASKED)


def attend(queries, keys_all, values, block_rows, score_scale):
    blocks = queries.shape[0] // block_rows
    starts = jnp.arange(blocks, dtype=jnp.int32) * block_rows

    def one_block(block_item):
        query_block, first_row = block_item
        scores = block_scores(query_block, keys_all, first_row, score_scale)
        highest = jnp.max(scores, axis=-1, keepdims=True)
        raised = jnp.exp(scores - highest)
        row_total = jnp.sum(raised, axis=-1, keepdims=True)
        weights = (raised / row_total).astype(jnp.bfloat16)
        mixed_out = jnp.einsum("hqk,khd->qhd", weights, values, preferred_element_type=jnp.float32)
        return (mixed_out, (highest + jnp.log(row_total))[..., 0])

    shape_blocks = (blocks, block_rows) + queries.shape[1:]
    mixed_out, logsum = lax.map(one_block, (queries.reshape(shape_blocks), starts))
    return (mixed_out.reshape(queries.shape), logsum)


def attend_back(queries, keys_all, values, logsum, grad_out, block_rows, score_scale):
    blocks = queries.shape[0] // block_rows
    starts = jnp.arange(blocks, dtype=jnp.int32) * block_rows
    shape_blocks = (blocks, block_rows) + queries.shape[1:]

    def one_block(running, block_item):
        key_grad, value_grad = running
        query_block, grad_block, logsum_block, first_row = block_item
        scores = block_scores(query_block, keys_all, first_row, score_scale)
        block_probs = jnp.exp(scores - logsum_block[..., None])
        value_grad = value_grad + jnp.einsum(
            "hqk,qhd->khd",
            block_probs.astype(jnp.bfloat16),
            grad_block,
            preferred_element_type=jnp.float32,
        )
        prob_grad = jnp.einsum(
            "qhd,khd->hqk", grad_block, values, preferred_element_type=jnp.float32
        )
        score_grad = (
            block_probs * (prob_grad - jnp.sum(prob_grad * block_probs, axis=-1, keepdims=True))
        ).astype(jnp.bfloat16)
        query_grad = (
            jnp.einsum("hqk,khd->qhd", score_grad, keys_all, preferred_element_type=jnp.float32)
            * score_scale
        )
        key_grad = (
            key_grad
            + jnp.einsum(
                "hqk,qhd->khd", score_grad, query_block, preferred_element_type=jnp.float32
            )
            * score_scale
        )
        return ((key_grad, value_grad), query_grad)

    zero_keys = jnp.zeros(keys_all.shape, jnp.float32)
    (key_grad, value_grad), query_grad = lax.scan(
        one_block,
        (zero_keys, zero_keys),
        (queries.reshape(shape_blocks), grad_out.reshape(shape_blocks), logsum, starts),
    )
    return (query_grad.reshape(queries.shape), key_grad, value_grad)


def gate_up_forward(activations, weight_in, weight_out):
    raised = jnp.einsum(
        "rekd,edcf->rekcf", activations, weight_in, preferred_element_type=jnp.float32
    )
    hidden = (jax.nn.silu(raised[..., 0, :]) * raised[..., 1, :]).astype(jnp.bfloat16)
    result = jnp.einsum("rekf,efd->rekd", hidden, weight_out, preferred_element_type=jnp.float32)
    return (raised, hidden, result)


def gate_up_back(activations, weight_in, weight_out, raised, hidden, incoming):
    out_grad = jnp.einsum("rekf,rekd->efd", hidden, incoming, preferred_element_type=jnp.float32)
    hidden_grad = jnp.einsum(
        "rekd,efd->rekf", incoming, weight_out, preferred_element_type=jnp.float32
    )
    gate_part = raised[..., 0, :]
    up_part = raised[..., 1, :]
    sigmoid_gate = jax.nn.sigmoid(gate_part)
    gate_grad = (
        hidden_grad * up_part * sigmoid_gate * (1.0 + gate_part * (1.0 - sigmoid_gate))
    ).astype(jnp.bfloat16)
    up_grad = (hidden_grad * gate_part * sigmoid_gate).astype(jnp.bfloat16)
    gate_wgrad = jnp.einsum(
        "rekd,rekf->edf", activations, gate_grad, preferred_element_type=jnp.float32
    )
    up_wgrad = jnp.einsum(
        "rekd,rekf->edf", activations, up_grad, preferred_element_type=jnp.float32
    )
    both_grad = jnp.stack([gate_grad, up_grad], axis=-2)
    row_grad = jnp.einsum(
        "rekcf,edcf->rekd", both_grad, weight_in, preferred_element_type=jnp.float32
    )
    return (gate_wgrad, up_wgrad, out_grad, row_grad)


def local_exchange(
    tokens,
    first_gain,
    attention_in,
    attention_bias,
    attention_out,
    second_gain,
    router,
    shared_gate,
    shared_in,
    shared_out,
    expert_in,
    expert_out,
    cotangent,
    expert_picks,
):
    local_rows, model_width = tokens.shape
    shard_count = lax.axis_size(SHARD)
    owner_count = lax.axis_size(EXPERT)
    seq_length = local_rows * shard_count
    expert_count = router.shape[1]
    pick_count = expert_picks.shape[1]
    owned_count = expert_in.shape[0]
    capacity = max(2, 2 * local_rows * pick_count // expert_count)
    heads_here = attention_bias.shape[1]
    head_dim = attention_bias.shape[2] * owner_count
    score_scale = head_dim ** (-0.5)
    block_rows = min(seq_length, 512)
    cosine_table, sine_table = rope_tables(seq_length, head_dim)

    def fetch_dense():
        return (
            lax.all_gather(attention_in, EXPERT, axis=0, tiled=True),
            lax.all_gather(attention_bias, EXPERT, axis=2, tiled=True),
            lax.all_gather(attention_out, EXPERT, axis=1, tiled=True),
            lax.all_gather(router, EXPERT, axis=0, tiled=True),
            lax.all_gather(shared_gate, EXPERT, axis=0, tiled=True),
            lax.all_gather(shared_in, EXPERT, axis=0, tiled=True),
            lax.all_gather(shared_out, EXPERT, axis=1, tiled=True),
        )

    def fetch_rows(normed_low):
        return (
            lax.all_gather(normed_low, SHARD, axis=0, tiled=True),
            lax.all_gather(expert_in, SHARD, axis=3, tiled=True),
            lax.all_gather(expert_out, SHARD, axis=1, tiled=True),
        )

    inputs = tokens.astype(jnp.float32)
    first_norm, first_factor = normalize(inputs)
    first_low = (first_norm * first_gain).astype(jnp.bfloat16)
    att_in, att_bias, att_out, router_full, gate_full, shared_inw, shared_outw = fetch_dense()
    normed_all, expert_inw, expert_outw = fetch_rows(first_low)
    projected = jnp.einsum("sd,dcf->scf", normed_all, att_in, preferred_element_type=jnp.float32)
    projected = projected + att_bias.reshape(3, -1).astype(jnp.float32)[None]
    projected = projected.reshape(seq_length, 3, heads_here, head_dim)
    queries = rotate(projected[:, 0], cosine_table, sine_table).astype(jnp.bfloat16)
    keys_all = rotate(projected[:, 1], cosine_table, sine_table).astype(jnp.bfloat16)
    values = projected[:, 2].astype(jnp.bfloat16)
    attended, logsum = attend(queries, keys_all, values, block_rows, score_scale)
    attended_low = attended.astype(jnp.bfloat16).reshape(seq_length, -1)
    attn_part = jnp.dot(attended_low, att_out, preferred_element_type=jnp.float32)
    attn_local = lax.psum_scatter(
        attn_part.astype(jnp.bfloat16), SHARD, scatter_dimension=0, tiled=True
    ).astype(jnp.float32)
    residual = inputs + attn_local
    second_norm, second_factor = normalize(residual)
    second_low = (second_norm * second_gain).astype(jnp.bfloat16)
    logits = jnp.dot(second_low, router_full, preferred_element_type=jnp.float32)
    route_probs = jax.nn.softmax(logits, axis=-1)
    picked = (
        expert_picks[:, :, None] == jnp.arange(expert_count, dtype=jnp.int32)[None, None, :]
    ).astype(jnp.float32)
    gate_values = jnp.sum(picked * route_probs[:, None, :], axis=-1)
    flat_picks = expert_picks.reshape(-1)
    flat_hot = (flat_picks[:, None] == jnp.arange(expert_count, dtype=jnp.int32)[None, :]).astype(
        jnp.int32
    )
    slot_ranks = jnp.sum((jnp.cumsum(flat_hot, axis=0) - flat_hot) * flat_hot, axis=1)
    slot_rows = flat_picks * capacity + slot_ranks
    outgoing = jnp.zeros((expert_count * capacity, model_width), jnp.bfloat16)
    outgoing = outgoing.at[slot_rows].set(jnp.repeat(second_low, pick_count, axis=0))
    arrived = lax.all_to_all(
        outgoing.reshape(owner_count, owned_count, capacity, model_width),
        EXPERT,
        split_axis=0,
        concat_axis=0,
        tiled=True,
    )
    mixed_all = lax.all_gather(second_low, SHARD, axis=0, tiled=True)
    shared_raised, shared_hidden, shared_part = gate_up_forward(
        mixed_all[:, None, None, :], shared_inw[None], shared_outw[None]
    )
    shared_rows = lax.psum_scatter(
        shared_part[:, 0, 0, :].astype(jnp.bfloat16), SHARD, scatter_dimension=0, tiled=True
    ).astype(jnp.float32)
    expert_raised, expert_hidden, expert_part = gate_up_forward(arrived, expert_inw, expert_outw)
    expert_result = expert_part.astype(jnp.bfloat16)
    shared_scale = jax.nn.sigmoid(
        jnp.dot(second_low, gate_full, preferred_element_type=jnp.float32)
    )
    out_grad = cotangent.astype(jnp.float32)
    slot_values = (
        (gate_values[:, :, None] * out_grad[:, None, :])
        .reshape(-1, model_width)
        .astype(jnp.bfloat16)
    )
    grad_send = (
        jnp.zeros((expert_count * capacity, model_width), jnp.bfloat16)
        .at[slot_rows]
        .set(slot_values)
    )
    returned, owner_grads = (
        lax.all_to_all(expert_result, EXPERT, split_axis=0, concat_axis=0, tiled=True),
        lax.all_to_all(
            grad_send.reshape(owner_count, owned_count, capacity, model_width),
            EXPERT,
            split_axis=0,
            concat_axis=0,
            tiled=True,
        ),
    )
    gathered_out = returned.reshape(expert_count * capacity, model_width)[slot_rows]
    gathered_out = gathered_out.reshape(local_rows, pick_count, model_width).astype(jnp.float32)
    routed = jnp.sum(gate_values[:, :, None] * gathered_out, axis=1)
    output = (residual + shared_scale[:, None] * shared_rows + routed).astype(jnp.bfloat16)
    pick_grad = jnp.sum(out_grad[:, None, :] * gathered_out, axis=-1)
    route_grad = jnp.sum(picked * pick_grad[:, :, None], axis=1)
    logit_grad = (
        route_probs * (route_grad - jnp.sum(route_grad * route_probs, axis=-1, keepdims=True))
    ).astype(jnp.bfloat16)
    scale_grad = jnp.sum(out_grad * shared_rows, axis=-1)
    gate_logit_grad = (scale_grad * shared_scale * (1.0 - shared_scale)).astype(jnp.bfloat16)
    shared_grad = (shared_scale[:, None] * out_grad).astype(jnp.bfloat16)
    shared_grad_all, logit_grad_all, gate_grad_all = (
        lax.all_gather(shared_grad, SHARD, axis=0, tiled=True),
        lax.all_gather(logit_grad, SHARD, axis=0, tiled=True),
        lax.all_gather(gate_logit_grad, SHARD, axis=0, tiled=True),
    )
    att_in, att_bias, att_out, router_full, gate_full, shared_inw, shared_outw = fetch_dense()
    normed_all, expert_inw, expert_outw = fetch_rows(first_low)
    expert_gate_w, expert_up_w, expert_down_w, owner_row_grad = gate_up_back(
        arrived, expert_inw, expert_outw, expert_raised, expert_hidden, owner_grads
    )
    shared_gate_w, shared_up_w, shared_down_w, shared_row_grad = gate_up_back(
        mixed_all[:, None, None, :],
        shared_inw[None],
        shared_outw[None],
        shared_raised,
        shared_hidden,
        shared_grad_all[:, None, None, :],
    )
    owner_low = owner_row_grad.astype(jnp.bfloat16)
    shared_back = lax.psum_scatter(
        shared_row_grad[:, 0, 0, :].astype(jnp.bfloat16), SHARD, scatter_dimension=0, tiled=True
    ).astype(jnp.float32)
    returned_grad = lax.all_to_all(owner_low, EXPERT, split_axis=0, concat_axis=0, tiled=True)
    routed_back = returned_grad.reshape(expert_count * capacity, model_width)[slot_rows]
    routed_back = jnp.sum(
        routed_back.reshape(local_rows, pick_count, model_width).astype(jnp.float32), axis=1
    )
    local_back = jnp.einsum(
        "te,de->td", logit_grad, router_full, preferred_element_type=jnp.float32
    )
    local_back = (
        local_back
        + gate_logit_grad.astype(jnp.float32)[:, None] * gate_full.astype(jnp.float32)[None, :]
    )
    second_grad = local_back + shared_back + routed_back
    residual_back, second_gain_grad = norm_back(
        second_grad, second_norm, second_factor, second_gain
    )
    residual_grad = out_grad + residual_back
    residual_all = lax.all_gather(residual_grad.astype(jnp.bfloat16), SHARD, axis=0, tiled=True)
    att_out_grad = jnp.einsum(
        "sf,sd->fd", attended_low, residual_all, preferred_element_type=jnp.float32
    )
    attended_grad = jnp.einsum(
        "sd,fd->sf", residual_all, att_out, preferred_element_type=jnp.float32
    )
    attended_grad = attended_grad.astype(jnp.bfloat16).reshape(seq_length, heads_here, head_dim)
    query_grad, key_grad, value_grad = attend_back(
        queries, keys_all, values, logsum, attended_grad, block_rows, score_scale
    )
    projected_grad = jnp.stack(
        [
            rotate_back(query_grad, cosine_table, sine_table),
            rotate_back(key_grad, cosine_table, sine_table),
            value_grad,
        ],
        axis=1,
    )
    projected_grad = projected_grad.astype(jnp.bfloat16).reshape(
        seq_length, 3, heads_here * head_dim
    )
    att_in_grad = jnp.einsum(
        "sd,scf->dcf", normed_all, projected_grad, preferred_element_type=jnp.float32
    )
    att_bias_grad = jnp.sum(projected_grad.astype(jnp.float32), axis=0).reshape(
        3, heads_here, head_dim
    )
    first_part = jnp.einsum(
        "scf,dcf->sd", projected_grad, att_in, preferred_element_type=jnp.float32
    )
    first_grad, expert_gate_l, expert_up_l, expert_down_l = (
        lax.psum_scatter(
            first_part.astype(jnp.bfloat16), SHARD, scatter_dimension=0, tiled=True
        ).astype(jnp.float32),
        lax.psum_scatter(
            expert_gate_w.astype(jnp.bfloat16), SHARD, scatter_dimension=2, tiled=True
        ).astype(jnp.float32),
        lax.psum_scatter(
            expert_up_w.astype(jnp.bfloat16), SHARD, scatter_dimension=2, tiled=True
        ).astype(jnp.float32),
        lax.psum_scatter(
            expert_down_w.astype(jnp.bfloat16), SHARD, scatter_dimension=1, tiled=True
        ).astype(jnp.float32),
    )
    input_back, first_gain_grad = norm_back(first_grad, first_norm, first_factor, first_gain)
    input_grad = residual_grad + input_back
    router_grad = jnp.einsum(
        "sd,se->de", mixed_all, logit_grad_all, preferred_element_type=jnp.float32
    )
    gate_vec_grad = jnp.einsum(
        "sd,s->d", mixed_all, gate_grad_all, preferred_element_type=jnp.float32
    )
    shared_in_grad = jnp.stack([shared_gate_w[0], shared_up_w[0]], axis=1)
    (
        att_in_local,
        att_bias_local,
        att_out_local,
        router_local,
        gate_vec_local,
        shared_in_local,
        shared_out_local,
    ) = (
        lax.psum_scatter(
            att_in_grad.astype(jnp.bfloat16), EXPERT, scatter_dimension=0, tiled=True
        ).astype(jnp.float32),
        lax.psum_scatter(
            att_bias_grad.astype(jnp.bfloat16), EXPERT, scatter_dimension=2, tiled=True
        ).astype(jnp.float32),
        lax.psum_scatter(
            att_out_grad.astype(jnp.bfloat16), EXPERT, scatter_dimension=1, tiled=True
        ).astype(jnp.float32),
        lax.psum_scatter(
            router_grad.astype(jnp.bfloat16), EXPERT, scatter_dimension=0, tiled=True
        ).astype(jnp.float32),
        lax.psum_scatter(
            gate_vec_grad.astype(jnp.bfloat16), EXPERT, scatter_dimension=0, tiled=True
        ).astype(jnp.float32),
        lax.psum_scatter(
            shared_in_grad.astype(jnp.bfloat16), EXPERT, scatter_dimension=0, tiled=True
        ).astype(jnp.float32),
        lax.psum_scatter(
            shared_down_w[0].astype(jnp.bfloat16), EXPERT, scatter_dimension=1, tiled=True
        ).astype(jnp.float32),
    )
    first_gain_all, second_gain_all = lax.psum(
        (first_gain_grad, second_gain_grad), (EXPERT, SHARD)
    )
    expert_in_grad = jnp.stack([expert_gate_l, expert_up_l], axis=2)
    return (
        output,
        input_grad,
        first_gain_all,
        att_in_local,
        att_bias_local,
        att_out_local,
        second_gain_all,
        router_local,
        gate_vec_local,
        shared_in_local,
        shared_out_local,
        expert_in_grad,
        expert_down_l,
    )


MESH = pl.DeviceIdType.MESH
EXTRA = 128
NT_DIMS = (((1,), (1,)), ((), ()))


class Place:
    def __init__(self):
        e, s = lax.axis_index(EXPERT), lax.axis_index(SHARD)
        self.z, self.x, self.y, self.c = e // 2, e % 2, s // 2, s % 2

    def z_of(self, kz):
        z = self.z
        return (z, z + 1 - 2 * (z % 2), (z + 2) % 4, 3 - z)[kz]

    def x_of(self, kx):
        return (self.x, 1 - self.x)[kx]

    def y_of(self, ky):
        return (self.y, 1 - self.y)[ky]

    def c_of(self, kc):
        return (self.c, 1 - self.c)[kc]

    def device(self, kz=0, kx=0, ky=0, kc=0):
        return (self.z_of(kz) * 2 + self.x_of(kx), self.y_of(ky) * 2 + self.c_of(kc))

    def sequence(self, kz, kx):
        return self.z_of(kz) * 2 + self.x_of(kx)

    def block(self, kz, kx, ky, kc):
        return self.sequence(kz, kx) * 4 + self.y_of(ky) * 2 + self.c_of(kc)


PARTNERS = [dict(kz=1), dict(kz=2), dict(kz=3), dict(kx=1), dict(ky=1), dict(kc=1)]
FARTHER = [dict(kz=1, kx=1), dict(kz=2, kx=1), dict(kz=3, kx=1)]


def greet(place, partners):
    barrier = pltpu.get_barrier_semaphore()
    for partner in partners:
        pl.semaphore_signal(
            barrier, inc=1, device_id=place.device(**partner), device_id_type=MESH
        )
    pl.semaphore_wait(barrier, len(partners))


class Copies:
    def __init__(self, place, send_sems, recv_sems):
        self.place, self.send_sems, self.recv_sems = place, send_sems, recv_sems
        self.made, self.got, self.left = {}, set(), set()

    def start(self, name, source, target, **partner):
        at = len(self.made)
        copy = pltpu.make_async_remote_copy(
            src_ref=source,
            dst_ref=target,
            send_sem=self.send_sems.at[at],
            recv_sem=self.recv_sems.at[at],
            device_id=self.place.device(**partner),
            device_id_type=MESH,
        )
        copy.start()
        self.made[name] = copy

    def arrived(self, name):
        if name not in self.got:
            self.got.add(name)
            self.made[name].wait_recv()

    def sent(self, name):
        if name not in self.left:
            self.left.add(name)
            self.made[name].wait_send()


GATHER_COPIES = 55
SUM_COPIES = 43


class Gather:
    def __init__(self, place, copies, block_ref, all_ref, rows):
        self.place, self.copies = place, copies
        self.block_ref, self.all_ref, self.rows = block_ref, all_ref, rows

    def view(self, kz, kx, ky, piece, own=False):
        half = self.rows // 2
        first = 0 if piece in (None, 0) else half
        count = self.rows if piece is None else half
        if own and (kz, kx, ky) == (0, 0, 0):
            return self.block_ref.at[pl.ds(first, count)]
        start = self.place.block(kz, kx, ky, 0) * self.rows + first
        return self.all_ref.at[pl.ds(pl.multiple_of(start, half), count)]

    def send(self, name, from_z, from_x, from_y, piece, **partner):
        self.copies.start(
            name,
            self.view(from_z, from_x, from_y, piece, own=True),
            self.view(from_z, from_x, from_y, piece),
            **partner,
        )

    def begin(self, kz):
        self.send(("z", kz), 0, 0, 0, None, kz=kz)

    def first(self, kz):
        if kz:
            self.copies.arrived(("z", kz))
        self.send(("y0", kz, 0), kz, 0, 0, 0, ky=1)
        self.send(("y1", kz), kz, 0, 0, 1, ky=1)
        self.send(("x0", kz), kz, 0, 0, 0, kx=1)
        self.send(("x1", kz, 0), kz, 0, 0, 1, kx=1)
        self.send(("c", kz), kz, 0, 0, None, kc=1)

    def second_y(self, kz):
        self.copies.arrived(("y1", kz))
        self.send(("x1", kz, 1), kz, 0, 1, 1, kx=1)
        self.send(("c01", kz), kz, 0, 1, 1, kc=1)
        self.copies.arrived(("y0", kz, 0))
        self.send(("c00", kz), kz, 0, 1, 0, kc=1)

    def second_x(self, kz):
        self.copies.arrived(("x0", kz))
        self.send(("y0", kz, 1), kz, 1, 0, 0, ky=1)
        self.send(("c10", kz), kz, 1, 0, 0, kc=1)
        self.copies.arrived(("x1", kz, 0))
        self.send(("c11", kz), kz, 1, 0, 1, kc=1)

    def third(self, kz):
        self.copies.arrived(("y0", kz, 1))
        self.send(("c20", kz), kz, 1, 1, 0, kc=1)
        self.copies.arrived(("x1", kz, 1))
        self.send(("c21", kz), kz, 1, 1, 1, kc=1)

    def have(self, kz, kx):
        for name in ("c10", "c11", "c20", "c21") if kx else ("c", "c00", "c01"):
            self.copies.arrived((name, kz))


class Sums:
    def __init__(self, place, copies, tag, held, from_y0, from_y1, from_x0, from_x1, from_z):
        self.place, self.copies, self.tag, self.held = place, copies, tag, held
        self.from_y0, self.from_y1 = from_y0, from_y1
        self.from_x0, self.from_x1, self.from_z = from_x0, from_x1, from_z
        self.rows = held.shape[1]
        self.half = self.rows // 2

    def slot(self, kz, kx, ky, piece=None):
        at = kz * 4 + kx * 2 + ky
        if piece is None:
            return self.held.at[at]
        return self.held.at[at, pl.ds(piece * self.half, self.half)]

    def staged_part(self, staged):
        def view(ky, kc):
            start = (self.place.y_of(ky) * 2 + self.place.c_of(kc)) * self.rows
            return staged.at[pl.ds(pl.multiple_of(start, self.rows), self.rows)]

        return view

    def add(self, into, other):
        into[...] = into[...] + other[...]

    def cores(self, kz, kx, part):
        for ky in (1, 0):
            self.copies.start((SUM_CORES, self.tag, kz, kx, ky), part(ky, 1), self.slot(kz, kx, ky), kc=1)

    def first(self, kz, kx, part):
        for ky in (1, 0):
            self.copies.arrived((SUM_CORES, self.tag, kz, kx, ky))
            self.add(self.slot(kz, kx, ky), part(ky, 0))
            if ky:
                self.copies.start(
                    ("sy0", self.tag, kz, kx), self.slot(kz, kx, 1, 0), self.from_y0.at[kz * 2 + kx], ky=1
                )
            if kx:
                self.copies.start(
                    ("sx1", self.tag, kz, ky), self.slot(kz, 1, ky, 1), self.from_x1.at[kz * 2 + ky], kx=1
                )
        for ky in (1, 0):
            self.copies.sent((SUM_CORES, self.tag, kz, kx, ky))

    def second_away(self, kz):
        self.copies.arrived(("sy0", self.tag, kz, 1))
        self.add(self.slot(kz, 1, 0, 0), self.from_y0.at[kz * 2 + 1])
        self.copies.start(("sx0", self.tag, kz), self.slot(kz, 1, 0, 0), self.from_x0.at[kz], kx=1)

    def second_here(self, kz):
        self.copies.arrived(("sx1", self.tag, kz, 1))
        self.add(self.slot(kz, 0, 1, 1), self.from_x1.at[kz * 2 + 1])
        self.copies.start(("sy1", self.tag, kz), self.slot(kz, 0, 1, 1), self.from_y1.at[kz], ky=1)
        self.copies.arrived(("sx1", self.tag, kz, 0))
        self.add(self.slot(kz, 0, 0, 1), self.from_x1.at[kz * 2])
        self.copies.arrived(("sy0", self.tag, kz, 0))
        self.add(self.slot(kz, 0, 0, 0), self.from_y0.at[kz * 2])
        self.copies.arrived(("sx0", self.tag, kz))
        self.add(self.slot(kz, 0, 0, 0), self.from_x0.at[kz])

    def third(self, kz):
        self.copies.arrived(("sy1", self.tag, kz))
        self.add(self.slot(kz, 0, 0, 1), self.from_y1.at[kz])
        if kz:
            self.copies.start(("sz", self.tag, kz), self.slot(kz, 0, 0), self.from_z.at[kz - 1], kz=kz)

    def total(self):
        total = self.slot(0, 0, 0)[...].astype(jnp.float32)
        for kz in (1, 2, 3):
            self.copies.arrived(("sz", self.tag, kz))
            total = total + self.from_z.at[kz - 1][...].astype(jnp.float32)
        return total


RAISE, OUT, BACK, CORES, BEGIN, PASS, PASS_X, PASS_Y, PASS_LAST, HAVE = range(10)
FIRST, AWAY, HERE, THIRD = range(10, 14)
ORDER = ((0, 1), (3, 1), (3, 0), (2, 1), (2, 0), (1, 1), (1, 0), (0, 0))
PLAN = (
    (PASS, 0, 0), (BEGIN, 1, 0), (BEGIN, 3, 0), (PASS_Y, 0, 0), (PASS_X, 0, 0),
    (PASS_LAST, 0, 0), (PASS, 3, 0), (HAVE, 0, 0), (RAISE, 0, 0), (BEGIN, 2, 0), (RAISE, 0, 1),
    (PASS_X, 3, 0), (PASS_Y, 3, 0), (RAISE, 0, 2), (RAISE, 0, 3), (PASS, 1, 0), (OUT, 0, 0),
    (OUT, 0, 1), (CORES, 0, 0), (BACK, 0, 0), (PASS_LAST, 3, 0), (BACK, 0, 1), (CORES, 1, 0),
    (HAVE, 1, 0), (PASS, 2, 0), (PASS_Y, 1, 0), (RAISE, 1, 0), (RAISE, 1, 1), (RAISE, 1, 2),
    (PASS_Y, 2, 0), (RAISE, 1, 3), (HAVE, 2, 0), (FIRST, 0, 0), (OUT, 1, 0), (OUT, 1, 1),
    (CORES, 0, 1), (FIRST, 1, 0), (BACK, 1, 0), (PASS_X, 2, 0), (BACK, 1, 1), (CORES, 1, 1),
    (RAISE, 2, 0), (RAISE, 2, 1), (FIRST, 0, 1), (RAISE, 2, 2), (FIRST, 1, 1), (RAISE, 2, 3),
    (OUT, 2, 0), (OUT, 2, 1), (CORES, 0, 2), (BACK, 2, 0), (BACK, 2, 1), (PASS_LAST, 2, 0),
    (CORES, 1, 2), (AWAY, 0, 3), (HAVE, 3, 0), (FIRST, 1, 2), (FIRST, 0, 2), (RAISE, 3, 0),
    (RAISE, 3, 1), (RAISE, 3, 2), (RAISE, 3, 3), (PASS_X, 1, 0), (OUT, 3, 0), (OUT, 3, 1),
    (CORES, 0, 3), (BACK, 3, 0), (AWAY, 1, 3), (HAVE, 4, 0), (BACK, 3, 1), (CORES, 1, 3),
    (HERE, 0, 3), (FIRST, 0, 3), (RAISE, 4, 0), (RAISE, 4, 1), (RAISE, 4, 2), (PASS_LAST, 1, 0),
    (FIRST, 1, 3), (RAISE, 4, 3), (HAVE, 5, 0), (OUT, 4, 0), (THIRD, 0, 3), (AWAY, 0, 2),
    (HERE, 1, 3), (OUT, 4, 1), (CORES, 0, 4), (BACK, 4, 0), (BACK, 4, 1), (FIRST, 0, 4),
    (CORES, 1, 4), (RAISE, 5, 0), (RAISE, 5, 1), (RAISE, 5, 2), (RAISE, 5, 3), (FIRST, 1, 4),
    (THIRD, 1, 3), (OUT, 5, 0), (OUT, 5, 1), (AWAY, 1, 2), (HERE, 0, 2), (CORES, 0, 5),
    (BACK, 5, 0), (BACK, 5, 1), (CORES, 1, 5), (FIRST, 0, 5), (HAVE, 6, 0), (HERE, 1, 2),
    (FIRST, 1, 5), (RAISE, 6, 0), (RAISE, 6, 1), (RAISE, 6, 2), (RAISE, 6, 3), (OUT, 6, 0),
    (THIRD, 0, 2), (HAVE, 7, 0), (OUT, 6, 1), (CORES, 0, 6), (AWAY, 0, 1), (BACK, 6, 0),
    (THIRD, 1, 2), (FIRST, 0, 6), (BACK, 6, 1), (CORES, 1, 6), (RAISE, 7, 0), (HERE, 0, 1),
    (AWAY, 1, 1), (RAISE, 7, 1), (RAISE, 7, 2), (FIRST, 1, 6), (RAISE, 7, 3), (THIRD, 0, 1),
    (OUT, 7, 0), (AWAY, 0, 0), (OUT, 7, 1), (AWAY, 1, 0), (CORES, 0, 7), (HERE, 1, 1),
    (BACK, 7, 0), (FIRST, 0, 7), (BACK, 7, 1), (CORES, 1, 7), (HERE, 0, 0), (FIRST, 1, 7),
    (THIRD, 1, 1), (HERE, 1, 0), (THIRD, 1, 0), (THIRD, 0, 0),
)


def mixture_kernel(
    sizes,
    part_ref,
    cot_ref,
    expert_in_ref,
    shared_in_ref,
    expert_out_ref,
    shared_out_ref,
    select_ref,
    place_ref,
    tokens_ref,
    gain_ref,
    router_ref,
    picked_ref,
    output_ref,
    block_ref,
    residual_grad_ref,
    logit_grad_ref,
    gain_grad_ref,
    rows_ref,
    units_ref,
    residual_all_ref,
    weight_in,
    weight_out,
    rows_buf,
    cot_buf,
    units_buf,
    dots,
    staged_out,
    staged_back,
    gates,
    *rest,
):
    rows, seq, width, owned, part, shared_part, padded, experts = sizes
    out_slots, back_slots = rest[:6], rest[6:12]
    send_sems, recv_sems, load_sems, misc_sems = rest[12:]
    bf16, f32 = jnp.bfloat16, jnp.float32
    place = Place()
    copies = Copies(place, send_sems, recv_sems)
    gather = Gather(place, copies, block_ref, rows_ref, rows)
    sums_out = Sums(place, copies, 0, *out_slots)
    sums_back = Sums(place, copies, 1, *back_slots)
    both = (sums_out, sums_back)

    own = pltpu.make_async_copy(block_ref, gather.view(0, 0, 0, None), misc_sems.at[0])
    attended = sums_out.staged_part(part_ref)
    mine = [
        pltpu.make_async_copy(
            attended(ky, 0),
            staged_back.at[pl.ds(ky * rows, rows), pl.ds(0, width)],
            misc_sems.at[4 + ky],
        )
        for ky in (0, 1)
    ]
    mine.append(
        pltpu.make_async_copy(
            tokens_ref,
            staged_back.at[pl.ds(2 * rows, rows), pl.ds(0, width)],
            misc_sems.at[6],
        )
    )
    for load in mine:
        load.start()
    moves = []
    for c in (0, 1):
        for e in range(owned):
            moves.append(
                (
                    expert_in_ref.at[pl.ds((2 * e + c) * part, part)],
                    weight_in.at[pl.ds(c * padded + e * part, part)],
                )
            )
        moves.append(
            (
                shared_in_ref.at[pl.ds(c * shared_part, shared_part)],
                weight_in.at[pl.ds(c * padded + owned * part, shared_part)],
            )
        )
    moves.append((expert_out_ref, weight_out.at[pl.ds(0, owned * part)]))
    moves.append((shared_out_ref, weight_out.at[pl.ds(owned * part, shared_part)]))
    loads = [
        pltpu.make_async_copy(source, target, load_sems.at[i])
        for i, (source, target) in enumerate(moves)
    ]
    for load in loads:
        load.start()

    order = ORDER

    def span(step):
        return pl.ds(pl.multiple_of(place.sequence(*order[step]) * seq, seq), seq)

    def rows_load(step):
        return pltpu.make_async_copy(rows_ref.at[span(step)], rows_buf, misc_sems.at[1])

    def cot_load(step):
        return pltpu.make_async_copy(cot_ref.at[span(step)], cot_buf, misc_sems.at[2])

    def units_write(step):
        return pltpu.make_async_copy(units_buf, units_ref.at[span(step)], misc_sems.at[3])

    cot_load(0).start()
    used = owned * part + shared_part
    for at in (used, padded + used):
        weight_in[pl.ds(at, padded - used), :] = jnp.zeros((padded - used, width), bf16)
    weight_out[pl.ds(used, padded - used), :] = jnp.zeros((padded - used, width), bf16)
    greet(place, PARTNERS)

    def third_of(ref, i):
        return ref.at[pl.ds(i * rows, rows), pl.ds(0, width)]

    for ky in (1, 0):
        copies.start(("pc", ky), attended(ky, 1), third_of(staged_out, ky), kc=1)
    mine[1].wait()
    copies.arrived(("pc", 1))
    third_of(staged_out, 1)[...] = third_of(staged_out, 1)[...] + third_of(staged_back, 1)[...]
    copies.start(("py", 0), third_of(staged_out, 1), third_of(staged_out, 2), ky=1)
    mine[0].wait()
    copies.arrived(("pc", 0))
    total = third_of(staged_out, 0)[...].astype(f32) + third_of(staged_back, 0)[...].astype(f32)
    mine[2].wait()
    total = total + third_of(staged_back, 2)[...].astype(f32)
    copies.arrived(("py", 0))
    total = total + third_of(staged_out, 2)[...].astype(f32)
    residual_grad_ref[...] = total
    factor = lax.rsqrt(jnp.mean(total * total, axis=-1, keepdims=True) + EPSILON)
    block_ref[:, pl.ds(0, width)] = (total * factor * gain_ref[...]).astype(bf16)
    logits = lax.dot_general(
        block_ref[:, pl.ds(0, width)], router_ref[...], NT_DIMS, preferred_element_type=f32
    )
    lane = lax.broadcasted_iota(jnp.int32, (rows, EXTRA), 1)
    routed = lane < experts
    highest = jnp.max(jnp.where(routed, logits, MASKED), axis=-1, keepdims=True)
    raised = jnp.where(routed, jnp.exp(jnp.where(routed, logits, highest) - highest), 0.0)
    probs = raised / jnp.sum(raised, axis=-1, keepdims=True)
    gates[...] = jnp.where(lane == experts, jax.nn.sigmoid(logits), probs)
    weights = jnp.where(routed, probs * picked_ref[...], gates[...])
    coarse = weights.astype(bf16)
    fine = (weights - coarse.astype(f32)).astype(bf16)
    across = lax.broadcasted_iota(jnp.int32, (EXTRA, EXTRA), 1)
    down = lax.broadcasted_iota(jnp.int32, (EXTRA, EXTRA), 0)
    moved = jnp.where(across == down + experts + 1, 1.0, 0.0).astype(bf16)
    block_ref[:, pl.ds(width, EXTRA)] = (
        coarse.astype(f32) + jnp.dot(fine, moved, preferred_element_type=f32)
    ).astype(bf16)
    copies.sent(("py", 0))
    own.start()

    tile, wide = 256, 512

    def raise_tile(at, count):
        here, above = pl.ds(at, count), pl.ds(at + padded, count)
        low_rows = rows_buf[:, pl.ds(0, width)]
        if count == tile:
            gate, up = (
                lax.dot_general(
                    low_rows, weight_in[at_rows, :], NT_DIMS, preferred_element_type=f32
                )
                for at_rows in (here, above)
            )
        else:
            pair = jnp.concatenate([weight_in[here, :], weight_in[above, :]], axis=0)
            raised = lax.dot_general(low_rows, pair, NT_DIMS, preferred_element_type=f32)
            gate, up = raised[:, :count], raised[:, count:]
        back = lax.dot_general(
            cot_buf[...], weight_out[here, :], NT_DIMS, preferred_element_type=f32
        )
        scale = jnp.dot(
            rows_buf[:, pl.ds(width, EXTRA)], select_ref[:, here], preferred_element_type=f32
        )
        sigmoid_gate = jax.nn.sigmoid(gate)
        active = gate * sigmoid_gate
        hidden = active * up
        dots[...] += jnp.dot(
            (back * hidden).astype(bf16), place_ref[here, :], preferred_element_type=f32
        )
        scaled = back * scale
        units_buf[:, pl.ds(at + 2 * padded, count)] = (hidden * scale).astype(bf16)
        units_buf[:, here] = (
            scaled * up * (sigmoid_gate + active * (1.0 - sigmoid_gate))
        ).astype(bf16)
        units_buf[:, above] = (scaled * active).astype(bf16)

    tiles = padded // tile
    pieces = tiles + (1 if padded % tile else 0)
    strips = width // wide // 2

    def raise_some(step, first, last):
        if first == 0:
            rows_load(step).wait()
            cot_load(step).wait()
            if step:
                units_write(step - 1).wait()
            else:
                for load in loads:
                    load.wait()
            dots[...] = jnp.zeros_like(dots)
        if min(last, tiles) - first == 1:
            raise_tile(first * tile, tile)
        elif min(last, tiles) > first:

            @pl.loop(first, min(last, tiles))
            def _(j):
                raise_tile(pl.multiple_of(j * tile, tile), tile)

        if last > tiles:
            raise_tile(tiles * tile, padded % tile)
        if last == pieces:
            units_write(step).start()
            if step + 1 < len(order):
                cot_load(step + 1).start()

    def project(first, last, units, weight, staged):
        @pl.loop(first * strips, last * strips)
        def _(n):
            at = pl.ds(pl.multiple_of(n * wide, wide), wide)
            staged[:, at] = jnp.dot(
                units_buf[:, units], weight[:, at], preferred_element_type=f32
            ).astype(bf16)

    def out_some(step, first, last):
        project(first, last, pl.ds(2 * padded, padded), weight_out, staged_out)

    def back_some(step, first, last):
        project(first, last, pl.ds(0, 2 * padded), weight_in, staged_back)
        if last == 2:
            staged_back[:, pl.ds(width, EXTRA)] = dots[...].astype(bf16)

    def have(step):
        if order[step] == (0, 0):
            own.wait()
        gather.have(*order[step])
        rows_load(step).start()

    work = {RAISE: raise_some, OUT: out_some, BACK: back_some}
    moves = {
        BEGIN: gather.begin,
        PASS: gather.first,
        PASS_X: gather.second_x,
        PASS_Y: gather.second_y,
        PASS_LAST: gather.third,
        HAVE: have,
    }
    stages = (staged_out, staged_back)
    at = 0
    while at < len(PLAN):
        kind, a, b = PLAN[at]
        at += 1
        if kind in work:
            last = b + 1
            while at < len(PLAN) and PLAN[at] == (kind, a, last):
                last, at = last + 1, at + 1
            work[kind](a, b, last)
        elif kind in moves:
            moves[kind](a)
        elif kind == CORES:
            both[a].cores(*order[b], both[a].staged_part(stages[a]))
        elif kind == FIRST:
            both[a].first(*order[b], both[a].staged_part(stages[a]))
        elif kind == AWAY:
            both[a].second_away(b)
        elif kind == HERE:
            both[a].second_here(b)
        else:
            both[a].third(b)
    last = len(order) - 1
    own_cot = pltpu.make_async_copy(
        cot_ref.at[pl.ds(pl.multiple_of(place.block(0, 0, 0, 0) * rows, rows), rows)],
        cot_buf.at[pl.ds(0, rows)],
        misc_sems.at[7],
    )
    own_cot.start()
    total = residual_grad_ref[...]
    output_ref[...] = (total + sums_out.total()).astype(bf16)
    own_cot.wait()
    back = sums_back.total()
    factor = lax.rsqrt(jnp.mean(total * total, axis=-1, keepdims=True) + EPSILON)
    normed = total * factor
    held = gates[...]
    extra = back[:, width:]
    pick_grads = jnp.where(routed, extra * picked_ref[...], 0.0)
    probs = jnp.where(routed, held, 0.0)
    inner = jnp.sum(pick_grads * probs, axis=-1, keepdims=True)
    logit_grad = jnp.where(
        lane == experts, extra * held * (1.0 - held), probs * (pick_grads - inner)
    ).astype(bf16)
    logit_grad_ref[...] = logit_grad
    second_grad = back[:, :width] + jnp.dot(
        logit_grad, router_ref[...], preferred_element_type=f32
    )
    scaled = second_grad * gain_ref[...]
    inner = jnp.mean(scaled * normed, axis=-1, keepdims=True)
    cotangent = cot_buf[pl.ds(0, rows), :].astype(f32)
    residual_grad = cotangent + factor * (scaled - normed * inner)
    residual_grad_ref[...] = residual_grad
    gain_grad_ref[...] = jnp.sum(second_grad * normed, axis=0, keepdims=True)
    for ky in (0, 1):
        copies.sent((SUM_CORES, 0) + order[last] + (ky,))
    third_of(staged_out, 0)[...] = residual_grad.astype(bf16)

    def spot(ky, kc):
        start = (place.y_of(ky) * 2 + place.c_of(kc)) * rows
        return residual_all_ref.at[pl.ds(pl.multiple_of(start, rows), rows)]

    shown = pltpu.make_async_copy(third_of(staged_out, 0), spot(0, 0), misc_sems.at[6])
    shown.start()
    copies.start(("gy", 0), third_of(staged_out, 0), spot(0, 0), ky=1)
    copies.start(("gc", 0), third_of(staged_out, 0), spot(0, 0), kc=1)
    copies.arrived(("gy", 0))
    copies.start(("gf", 0), spot(1, 0), spot(1, 0), kc=1)
    units_write(last).wait()
    copies.arrived(("gc", 0))
    copies.arrived(("gf", 0))
    shown.wait()
    for name in copies.made:
        copies.sent(name)


def sum_slots(rows, packed):
    half = rows // 2
    bf16 = jnp.bfloat16
    return [
        pltpu.VMEM((16, rows, packed), bf16),
        pltpu.VMEM((8, half, packed), bf16),
        pltpu.VMEM((4, half, packed), bf16),
        pltpu.VMEM((4, half, packed), bf16),
        pltpu.VMEM((8, half, packed), bf16),
        pltpu.VMEM((3, rows, packed), bf16),
    ]


def mixture(
    attn_part,
    cot_all,
    expert_in,
    shared_win,
    expert_out,
    shared_wout,
    select,
    spots,
    tokens,
    gain,
    router_wide,
    picked,
    experts,
):
    rows, width = tokens.shape
    packed = width + EXTRA
    total_rows = cot_all.shape[0]
    owned, part = expert_out.shape[0], expert_out.shape[1]
    shared_part = shared_wout.shape[0]
    seq = attn_part.shape[0]
    padded = select.shape[1]
    bf16, f32 = jnp.bfloat16, jnp.float32
    vmem = pl.BlockSpec(memory_space=pltpu.VMEM)
    anywhere = pl.BlockSpec(memory_space=pl.ANY)
    copies = GATHER_COPIES + 2 * SUM_COPIES + 6
    return pl.pallas_call(
        functools.partial(
            mixture_kernel, (rows, seq, width, owned, part, shared_part, padded, experts)
        ),
        out_shape=(
            jax.ShapeDtypeStruct((rows, width), bf16),
            jax.ShapeDtypeStruct((rows, packed), bf16),
            jax.ShapeDtypeStruct((rows, width), f32),
            jax.ShapeDtypeStruct((rows, EXTRA), bf16),
            jax.ShapeDtypeStruct((1, width), f32),
            jax.ShapeDtypeStruct((total_rows, packed), bf16),
            jax.ShapeDtypeStruct((total_rows, 3 * padded), bf16),
            jax.ShapeDtypeStruct((seq, width), bf16),
        ),
        in_specs=[anywhere] * 6 + [vmem] * 2 + [anywhere] + [vmem] * 3,
        out_specs=(vmem,) * 5 + (anywhere,) * 3,
        scratch_shapes=[
            pltpu.VMEM((2 * padded, width), bf16),
            pltpu.VMEM((padded, width), bf16),
            pltpu.VMEM((seq, packed), bf16),
            pltpu.VMEM((seq, width), bf16),
            pltpu.VMEM((seq, 3 * padded), bf16),
            pltpu.VMEM((seq, EXTRA), f32),
            pltpu.VMEM((seq, width), bf16),
            pltpu.VMEM((seq, packed), bf16),
            pltpu.VMEM((rows, EXTRA), f32),
        ]
        + sum_slots(rows, width)
        + sum_slots(rows, packed)
        + [
            pltpu.SemaphoreType.DMA((copies,)),
            pltpu.SemaphoreType.DMA((copies,)),
            pltpu.SemaphoreType.DMA((2 * owned + 4,)),
            pltpu.SemaphoreType.DMA((8,)),
        ],
        compiler_params=pltpu.CompilerParams(
            collective_id=0, has_side_effects=True, vmem_limit_bytes=63 * 2**20
        ),
        cost_estimate=pl.CostEstimate(
            flops=2 * total_rows * width * padded * 6,
            bytes_accessed=100 * 2**20,
            transcendentals=total_rows * padded,
        ),
        name="mixture",
    )(
        attn_part,
        cot_all,
        expert_in.transpose(0, 2, 3, 1).reshape(2 * owned * part, width),
        shared_win,
        expert_out.reshape(owned * part, width),
        shared_wout,
        select,
        spots,
        tokens,
        gain,
        router_wide,
        picked,
    )


class Totals:
    def __init__(self, place, copies, value, from_c, from_y, from_x, by_z):
        self.place, self.copies, self.value = place, copies, value
        self.slots = {CORE: from_c, ROW: from_y, COLUMN: from_x}
        self.by_z = by_z

    def send(self, axis):
        self.copies.start((TOTAL, axis), self.value, self.slots[axis], **{axis: 1})

    def add(self, axis):
        self.copies.arrived((TOTAL, axis))
        self.copies.sent((TOTAL, axis))
        self.value[...] = self.value[...] + self.slots[axis][...]

    def send_z(self):
        mine = self.by_z.at[self.place.z]
        mine[...] = self.value[...]
        for kz in (1, 2, 3):
            self.copies.start(("tz", kz), mine, mine, kz=kz)

    def finish(self):
        for kz in (1, 2, 3):
            self.copies.arrived(("tz", kz))
        by_z = self.by_z
        return (by_z[0] + by_z[1]) + (by_z[2] + by_z[3])


class OwnerSums:
    def __init__(self, place, copies, sources, mine, from_x, from_z, sems):
        self.place, self.copies, self.sources = place, copies, sources
        self.mine, self.from_x, self.from_z, self.sems = mine, from_x, from_z, sems

    def view(self, i, kz, kx):
        width = self.mine[i].shape[-2] if i == 0 else self.mine[i].shape[-1]
        at = pl.ds(pl.multiple_of(self.place.sequence(kz, kx) * width, width), width)
        return self.sources[i].at[:, at]

    def begin(self, kz):
        for i in (0, 1):
            self.copies.start(("ox", i, kz), self.view(i, kz, 1), self.from_x[i].at[kz], kx=1)

    def load(self, kz):
        return [
            pltpu.make_async_copy(
                self.view(i, kz, 0), self.mine[i].at[kz], self.sems.at[2 * kz + i]
            )
            for i in (0, 1)
        ]

    def add(self, kz):
        for load in self.load(kz):
            load.wait()
        for i in (0, 1):
            self.copies.arrived(("ox", i, kz))
            held = self.from_x[i].at[kz]
            held[...] = held[...] + self.mine[i][kz]
            if kz in (1, 3):
                self.copies.start(("oz", i, kz), held, self.from_z[i].at[kz // 2], kz=1)

    def relay(self):
        for i in (0, 1):
            self.copies.arrived(("oz", i, 3))
            held = self.from_x[i].at[2]
            held[...] = held[...] + self.from_z[i][1]
            self.copies.start(("oz", i, 2), held, self.from_z[i].at[2], kz=2)

    def finish(self, i, out_ref):
        total = self.from_x[i][0].astype(jnp.float32)
        for kz, slot in ((1, 0), (2, 2)):
            self.copies.arrived(("oz", i, kz))
            total = total + self.from_z[i][slot].astype(jnp.float32)
        out_ref[...] = total


CLOSING_COPIES = 14 + 14 + 6 + 3
TURN, PRODUCT, GIVE, BEGIN_X, ADD, RELAY, TOTALS, PASS_FIRST, END_FIRST = range(9)
CLOSING_ORDER = (2, 3, 1, 0)
CLOSING_PLAN = (
    (TURN, 0, 0, 0), (PASS_FIRST, 0, 0, 0), (TURN, 1, 0, 0), (BEGIN_X, 3, 0, 0), (TURN, 2, 0, 0),
    (TURN, 3, 0, 0), (TURN, 4, 0, 0), (TURN, 5, 0, 0), (TURN, 6, 0, 0), (TURN, 7, 0, 0),
    (TURN, 8, 0, 0), (END_FIRST, 0, 0, 0), (TOTALS, 0, 0, 0), (TURN, 9, 0, 0), (TURN, 10, 0, 0),
    (TURN, 11, 0, 0), (TURN, 12, 0, 0), (TOTALS, 1, 0, 0), (TURN, 13, 0, 0), (TURN, 14, 0, 0),
    (TURN, 15, 0, 0), (TURN, 16, 0, 0), (BEGIN_X, 2, 0, 0), (TURN, 17, 0, 0), (TURN, 18, 0, 0),
    (TOTALS, 2, 0, 0), (TURN, 19, 0, 0), (TURN, 20, 0, 0), (BEGIN_X, 1, 0, 0), (ADD, 3, 0, 0),
    (PRODUCT, 2, 0, 0), (PRODUCT, 2, 0, 1), (PRODUCT, 2, 1, 0), (PRODUCT, 2, 1, 1),
    (GIVE, 0, 2, 0), (TOTALS, 3, 0, 0), (PRODUCT, 2, 2, 0), (PRODUCT, 2, 2, 1), (GIVE, 1, 2, 0),
    (PRODUCT, 3, 0, 0), (PRODUCT, 3, 0, 1), (PRODUCT, 3, 1, 0), (PRODUCT, 3, 1, 1),
    (GIVE, 0, 3, 0), (PRODUCT, 3, 2, 0), (PRODUCT, 3, 2, 1), (GIVE, 1, 3, 0), (PRODUCT, 1, 0, 0),
    (PRODUCT, 1, 0, 1), (PRODUCT, 1, 1, 0), (PRODUCT, 1, 1, 1), (GIVE, 0, 1, 0), (ADD, 2, 0, 0),
    (PRODUCT, 1, 2, 0), (RELAY, 0, 0, 0), (PRODUCT, 1, 2, 1), (ADD, 1, 0, 0), (BEGIN_X, 0, 0, 0),
    (GIVE, 1, 1, 0), (PRODUCT, 0, 0, 0), (PRODUCT, 0, 0, 1), (PRODUCT, 0, 1, 0),
    (PRODUCT, 0, 1, 1), (GIVE, 0, 0, 0), (ADD, 0, 0, 0), (PRODUCT, 0, 2, 0), (PRODUCT, 0, 2, 1),
    (GIVE, 1, 0, 0),
)


def closing_kernel(
    sizes,
    rows_ref,
    cot_ref,
    units_ref,
    att_in_ref,
    att_out_ref,
    first_ref,
    small_ref,
    tokens_ref,
    residual_grad_ref,
    gain_ref,
    input_grad_ref,
    att_in_out,
    att_out_out,
    small_out,
    expert_in_out,
    expert_out_out,
    shared_in_out,
    shared_out_out,
    chunks,
    turned,
    columns,
    grads,
    shared_in_send,
    shared_out_send,
    own_in,
    own_out,
    in_x,
    out_x,
    in_z,
    out_z,
    small,
    small_c,
    small_y,
    small_x,
    small_z,
    first_mine,
    first_got,
    send_sems,
    recv_sems,
    own_sems,
    chunk_sems,
    column_sems,
    write_sems,
    keep_sems,
):
    width, owned, part, shared_part, owner_width, padded, gain_row = sizes
    rows = tokens_ref.shape[0]
    f32, bf16 = jnp.float32, jnp.bfloat16
    place = Place()
    copies = Copies(place, send_sems, recv_sems)
    totals = Totals(place, copies, small, small_c, small_y, small_x, small_z)
    owners = OwnerSums(
        place,
        copies,
        (att_in_ref, att_out_ref),
        (own_in, own_out),
        (in_x, out_x),
        (in_z, out_z),
        own_sems,
    )
    wide = 2 * owner_width
    cut = owned * part
    lanes = 128
    per_kind = padded // lanes

    def chunk_load(i, slot):
        at = pl.ds(pl.multiple_of(i * lanes, lanes), lanes)
        return pltpu.make_async_copy(
            units_ref.at[:, at], chunks.at[slot], chunk_sems.at[slot]
        )

    def column_load(kz, which):
        source = (rows_ref, cot_ref)[which]
        at = pl.ds(pl.multiple_of(place.z_of(kz) * wide, wide), wide)
        return pltpu.make_async_copy(source.at[:, at], columns.at[which], column_sems.at[which])

    order = CLOSING_ORDER
    chunk_load(0, 0).start()
    for kz in range(4):
        for load in owners.load(kz):
            load.start()
    small[...] = small_ref[...]

    def first_part(ky, kc):
        start = (place.y_of(ky) * 2 + place.c_of(kc)) * rows
        return first_ref.at[pl.ds(pl.multiple_of(start, rows), rows)]

    first_loads = [
        pltpu.make_async_copy(first_part(ky, 0), first_mine.at[ky], keep_sems.at[2 + ky])
        for ky in (0, 1)
    ]
    for load in first_loads:
        load.start()
    greet(place, PARTNERS + FARTHER)
    for ky in (1, 0):
        copies.start(("fc", ky), first_part(ky, 1), first_got.at[ky], kc=1)
    column_load(order[0], 0).start()
    column_load(order[0], 1).start()

    def turn(first, last):
        @pl.loop(first, last)
        def _(i):
            slot = i % 2
            chunk_load(i, slot).wait()

            @pl.when(i + 1 < 3 * per_kind)
            def _():
                chunk_load(i + 1, 1 - slot).start()

            to = pl.ds(pl.multiple_of(i * lanes, lanes), lanes)

            @pl.loop(0, turned.shape[1] // wide)
            def _(r):
                at = pl.ds(pl.multiple_of(r * wide, wide), wide)
                turned[to, at] = chunks[slot, at, :].T

    def span(kz):
        return pl.ds(pl.multiple_of(place.z_of(kz) * wide, wide), wide)

    def writes(kz, kind):
        found = []
        for e in range(owned):
            if kind < 2:
                target = expert_in_out.at[pl.ds((2 * e + kind) * part, part), span(kz)]
            else:
                target = expert_out_out.at[pl.ds(e * part, part), span(kz)]
            found.append(
                pltpu.make_async_copy(
                    grads.at[kind, pl.ds(e * part, part)], target, write_sems.at[kind * owned + e]
                )
            )
        return found

    def share(kz, which):
        sent = (shared_in_send, shared_out_send)[which]
        target = (shared_in_out, shared_out_out)[which].at[place.sequence(0, 0)]
        for kx in (1, 0):
            at = pl.ds(pl.multiple_of(place.x_of(kx) * owner_width, owner_width), owner_width)
            source = sent.at[kz, :, at]
            if kz or kx:
                copies.start((SHARE, which, kz, kx), source, target, kz=kz, kx=kx)
            else:
                pltpu.make_async_copy(source, target, keep_sems.at[which]).start()

    def product(kz, kind, first, last):
        which, step = kind // 2, order.index(kz)
        if first == 0:
            if kind != 1:
                column_load(kz, which).wait()
            if step:
                for write in writes(order[step - 1], kind):
                    write.wait()

        @pl.loop(first, last)
        def _(n):
            at = pl.ds(pl.multiple_of(n * owner_width, owner_width), owner_width)
            grads[kind, :, at] = jnp.dot(
                turned[pl.ds(kind * padded, padded), :],
                columns[which, :, at],
                preferred_element_type=f32,
            ).astype(bf16)

        if last < 2:
            return
        if step < 3 and kind:
            column_load(order[step + 1], which).start()
        for write in writes(kz, kind):
            write.start()
        shared = grads[kind, pl.ds(cut, shared_part), :]
        if kind < 2:
            shared_in_send[kz, pl.ds(kind * shared_part, shared_part), :] = shared
        else:
            shared_out_send[kz] = shared

    def pass_first():
        first_loads[1].wait()
        copies.arrived(("fc", 1))
        first_got[1] = first_got[1] + first_mine[1]
        copies.start(("fy", 0), first_got.at[1], first_got.at[2], ky=1)

    def end_first():
        first_loads[0].wait()
        copies.arrived(("fc", 0))
        copies.arrived(("fy", 0))
        grad = first_got[0].astype(f32) + first_mine[0].astype(f32)
        grad = grad + first_got[2].astype(f32)
        inputs = tokens_ref[...].astype(f32)
        factor = lax.rsqrt(jnp.mean(inputs * inputs, axis=-1, keepdims=True) + EPSILON)
        normed = inputs * factor
        scaled = grad * gain_ref[...]
        inner = jnp.mean(scaled * normed, axis=-1, keepdims=True)
        input_grad_ref[...] = residual_grad_ref[...] + factor * (scaled - normed * inner)
        small[pl.ds(gain_row, 1), :] = jnp.sum(grad * normed, axis=0, keepdims=True)

    axes = (CORE, ROW, COLUMN)

    def totals_step(n):
        if n:
            totals.add(axes[n - 1])
        if n < 3:
            totals.send(axes[n])
        else:
            totals.send_z()

    at = 0
    while at < len(CLOSING_PLAN):
        kind, a, b, c = CLOSING_PLAN[at]
        at += 1
        if kind == TURN:
            last = a + 1
            while CLOSING_PLAN[at] == (TURN, last, 0, 0):
                last, at = last + 1, at + 1
            turn(a, last)
        elif kind == PRODUCT:
            last = c + 1
            if CLOSING_PLAN[at] == (PRODUCT, a, b, last):
                last, at = last + 1, at + 1
            product(a, b, c, last)
        elif kind == GIVE:
            share(b, a)
        elif kind == BEGIN_X:
            owners.begin(a)
        elif kind == ADD:
            owners.add(a)
        elif kind == RELAY:
            owners.relay()
        elif kind == PASS_FIRST:
            pass_first()
        elif kind == END_FIRST:
            end_first()
        else:
            totals_step(a)
    small_out[...] = totals.finish()
    owners.finish(0, att_in_out)
    owners.finish(1, att_out_out)
    for kind in (0, 1, 2):
        for write in writes(order[-1], kind):
            write.wait()
    for which in (0, 1):
        sent = (shared_in_send, shared_out_send)[which]
        target = (shared_in_out, shared_out_out)[which].at[place.sequence(0, 0)]
        at = pl.ds(pl.multiple_of(place.x_of(0) * owner_width, owner_width), owner_width)
        pltpu.make_async_copy(sent.at[0, :, at], target, keep_sems.at[which]).wait()
    for name in copies.made:
        if name[0] == SHARE:
            copies.arrived(name)
    for name in copies.made:
        copies.sent(name)


def closing(
    rows_all,
    cot_all,
    units_all,
    att_in,
    att_out,
    first_rows,
    small,
    tokens,
    residual_grad,
    gain,
    gain_row,
    owned,
    part,
    shared_part,
):
    total_rows, width = cot_all.shape
    rows = tokens.shape[0]
    padded = units_all.shape[1] // 3
    owners = lax.axis_size(EXPERT)
    owner_width = width // owners
    wide = 2 * owner_width
    heads_width = att_in.shape[2]
    bf16, f32 = jnp.bfloat16, jnp.float32
    vmem = pl.BlockSpec(memory_space=pltpu.VMEM)
    anywhere = pl.BlockSpec(memory_space=pl.ANY)
    block_in = (3, owner_width, heads_width)
    block_out = (heads_width, owner_width)
    return pl.pallas_call(
        functools.partial(
            closing_kernel, (width, owned, part, shared_part, owner_width, padded, gain_row)
        ),
        out_shape=(
            jax.ShapeDtypeStruct((rows, width), f32),
            jax.ShapeDtypeStruct(block_in, f32),
            jax.ShapeDtypeStruct(block_out, f32),
            jax.ShapeDtypeStruct(small.shape, f32),
            jax.ShapeDtypeStruct((2 * owned * part, width), bf16),
            jax.ShapeDtypeStruct((owned * part, width), bf16),
            jax.ShapeDtypeStruct((owners, 2 * shared_part, owner_width), bf16),
            jax.ShapeDtypeStruct((owners, shared_part, owner_width), bf16),
        ),
        in_specs=[anywhere] * 6 + [vmem] * 4,
        out_specs=(vmem,) * 4 + (anywhere,) * 4,
        scratch_shapes=[
            pltpu.VMEM((2, total_rows, 128), bf16),
            pltpu.VMEM((3 * padded, total_rows), bf16),
            pltpu.VMEM((2, total_rows, wide), bf16),
            pltpu.VMEM((3, padded, wide), bf16),
            pltpu.VMEM((4, 2 * shared_part, wide), bf16),
            pltpu.VMEM((4, shared_part, wide), bf16),
            pltpu.VMEM((4,) + block_in, bf16),
            pltpu.VMEM((4,) + block_out, bf16),
            pltpu.VMEM((4,) + block_in, bf16),
            pltpu.VMEM((4,) + block_out, bf16),
            pltpu.VMEM((3,) + block_in, bf16),
            pltpu.VMEM((3,) + block_out, bf16),
        ]
        + [pltpu.VMEM(small.shape, f32)] * 4
        + [
            pltpu.VMEM((4,) + small.shape, f32),
            pltpu.VMEM((2, rows, width), bf16),
            pltpu.VMEM((3, rows, width), bf16),
            pltpu.SemaphoreType.DMA((CLOSING_COPIES,)),
            pltpu.SemaphoreType.DMA((CLOSING_COPIES,)),
            pltpu.SemaphoreType.DMA((8,)),
            pltpu.SemaphoreType.DMA((2,)),
            pltpu.SemaphoreType.DMA((2,)),
            pltpu.SemaphoreType.DMA((3 * owned,)),
            pltpu.SemaphoreType.DMA((4,)),
        ],
        compiler_params=pltpu.CompilerParams(
            collective_id=1, has_side_effects=True, vmem_limit_bytes=62 * 2**20
        ),
        cost_estimate=pl.CostEstimate(
            flops=2 * total_rows * width * padded * 3,
            bytes_accessed=150 * 2**20,
            transcendentals=0,
        ),
        name="closing",
    )(
        rows_all,
        cot_all,
        units_all,
        att_in,
        att_out,
        first_rows,
        small,
        tokens,
        residual_grad,
        gain,
    )


OPENING_COPIES = 6 + 8 + 3 + 14 + 31
SPREAD_Z, RELAY_Z, PASS_ON_X, SLICES, NORMED = range(5)
COT_Z, COT_RELAY, COT_X, COT_Y, COT_CORE = range(5, 10)
OPENING_PLAN = (
    (SPREAD_Z, 1, 0), (COT_X, 0, 0), (COT_Z, 2, 0), (PASS_ON_X, 0, 0), (COT_X, 2, 0),
    (PASS_ON_X, 1, 0), (COT_Z, 1, 0), (SPREAD_Z, 2, 0), (COT_Y, 2, 0), (COT_Y, 0, 1),
    (SLICES, 2, 1), (COT_Y, 2, 1), (COT_X, 1, 0), (COT_RELAY, 0, 0), (COT_Y, 1, 0),
    (COT_CORE, 2, 0), (COT_Y, 0, 0), (COT_X, 3, 0), (SLICES, 1, 0), (COT_CORE, 1, 0),
    (COT_Y, 1, 1), (SLICES, 0, 1), (RELAY_Z, 0, 0), (COT_CORE, 0, 0), (PASS_ON_X, 2, 0),
    (COT_Y, 3, 0), (SLICES, 3, 1), (COT_Y, 3, 1), (COT_CORE, 3, 1), (COT_CORE, 0, 1),
    (COT_CORE, 2, 1), (SLICES, 2, 0), (NORMED, 0, 0), (COT_CORE, 1, 1), (SLICES, 1, 1),
    (SLICES, 3, 0), (PASS_ON_X, 3, 0), (COT_CORE, 3, 0),
)


def opening_kernel(
    sizes,
    normed_ref,
    att_in_ref,
    att_out_ref,
    shared_in_ref,
    shared_out_ref,
    cot_ref,
    normed_all,
    att_in_all,
    att_out_all,
    shared_in_all,
    shared_out_all,
    cot_all,
    send_sems,
    recv_sems,
    own_sems,
):
    rows, owner_width, shared_part = sizes
    place = Place()
    copies = Copies(place, send_sems, recv_sems)

    def in_view(kz, kx):
        at = pl.ds(pl.multiple_of(place.sequence(kz, kx) * owner_width, owner_width), owner_width)
        return att_in_all.at[:, at]

    def out_view(kz, kx):
        return att_out_all.at[place.sequence(kz, kx)]

    here = pl.ds(
        pl.multiple_of(place.sequence(0, 0) * owner_width, owner_width), owner_width
    )
    spot = pl.ds(pl.multiple_of((place.y * 2 + place.c) * rows, rows), rows)

    def shared_block(kz, kx):
        owner = place.sequence(kz, kx)
        at = pl.ds(pl.multiple_of(owner * shared_part, shared_part), shared_part)
        return (
            (shared_in_ref.at[owner], shared_in_all.at[:, here]),
            (shared_out_ref.at[at], shared_out_all.at[:, here]),
        )

    def cot_view(kz, kx, ky):
        start = place.block(kz, kx, ky, 0) * rows
        return cot_all.at[pl.ds(pl.multiple_of(start, rows), rows)]

    keeps = [
        (normed_ref, normed_all.at[spot]),
        (att_in_ref, in_view(0, 0)),
        (att_out_ref, out_view(0, 0)),
        (cot_ref, cot_view(0, 0, 0)),
    ] + list(shared_block(0, 0))
    keeps = [
        pltpu.make_async_copy(source, target, own_sems.at[i])
        for i, (source, target) in enumerate(keeps)
    ]
    for keep in keeps:
        keep.start()
    greet(place, PARTNERS + FARTHER + [dict(ky=1, kc=1)])

    def spread_z(kz, _):
        copies.start(("zi", kz), att_in_ref, in_view(0, 0), kz=kz)
        copies.start(("zo", kz), att_out_ref, out_view(0, 0), kz=kz)

    def relay_z(_, __):
        copies.arrived(("zi", 2))
        copies.start(("zi", 3), in_view(2, 0), in_view(2, 0), kz=1)
        copies.arrived(("zo", 2))
        copies.start(("zo", 3), out_view(2, 0), out_view(2, 0), kz=1)

    def pass_x(kz, _):
        if kz:
            copies.arrived(("zi", kz))
        source = in_view(kz, 0) if kz else att_in_ref
        copies.start(("xi", kz), source, in_view(kz, 0), kx=1)
        if kz:
            copies.arrived(("zo", kz))
        source = out_view(kz, 0) if kz else att_out_ref
        copies.start(("xo", kz), source, out_view(kz, 0), kx=1)

    def slices(kz, kx):
        for which, (source, target) in enumerate(shared_block(kz, kx)):
            copies.start((SHARE, which, kz, kx), source, target, kz=kz, kx=kx)

    def spread_normed(_, __):
        for ky, kc in ((0, 1), (1, 0), (1, 1)):
            copies.start(("n", ky, kc), normed_ref, normed_all.at[spot], ky=ky, kc=kc)

    def cot_send(name, from_z, from_x, from_y, **partner):
        held = cot_view(from_z, from_x, from_y)
        source = held if from_z or from_x or from_y else cot_ref
        copies.start(name, source, held, **partner)

    def cot_z(kz, _):
        cot_send(("cz", kz), 0, 0, 0, kz=kz)

    def cot_relay(_, __):
        copies.arrived(("cz", 2))
        cot_send(("cz", 3), 2, 0, 0, kz=1)

    def cot_x(kz, _):
        if kz:
            copies.arrived(("cz", kz))
        cot_send(("cx", kz), kz, 0, 0, kx=1)
        cot_send(("cs", kz, 0, 0), kz, 0, 0, kc=1)

    def cot_y(kz, kx):
        if kx:
            copies.arrived(("cx", kz))
        cot_send(("cy", kz, kx), kz, kx, 0, ky=1)
        if kx:
            cot_send(("cs", kz, 1, 0), kz, 1, 0, kc=1)

    def cot_core(kz, kx):
        copies.arrived(("cy", kz, kx))
        cot_send(("cs", kz, kx, 1), kz, kx, 1, kc=1)

    moves = {
        SPREAD_Z: spread_z,
        RELAY_Z: relay_z,
        PASS_ON_X: pass_x,
        SLICES: slices,
        NORMED: spread_normed,
        COT_Z: cot_z,
        COT_RELAY: cot_relay,
        COT_X: cot_x,
        COT_Y: cot_y,
        COT_CORE: cot_core,
    }
    for kind, a, b in OPENING_PLAN:
        moves[kind](a, b)
    for keep in keeps:
        keep.wait()
    for name in copies.made:
        copies.arrived(name)
    for name in copies.made:
        copies.sent(name)


def opening(normed, att_in, att_out, shared_in, shared_out, cotangent):
    rows, width = normed.shape
    parts, owner_width, heads_width = att_in.shape
    owners = lax.axis_size(EXPERT)
    shards = lax.axis_size(SHARD)
    shared_part = shared_out.shape[0] // owners
    anywhere = pl.BlockSpec(memory_space=pl.ANY)
    bf16 = jnp.bfloat16
    return pl.pallas_call(
        functools.partial(opening_kernel, (rows, owner_width, shared_part)),
        out_shape=(
            jax.ShapeDtypeStruct((rows * shards, width), bf16),
            jax.ShapeDtypeStruct((parts, owner_width * owners, heads_width), bf16),
            jax.ShapeDtypeStruct((owners,) + att_out.shape, bf16),
            jax.ShapeDtypeStruct((2 * shared_part, width), bf16),
            jax.ShapeDtypeStruct((shared_part, width), bf16),
            jax.ShapeDtypeStruct((rows * shards * owners, width), bf16),
        ),
        in_specs=[anywhere] * 6,
        out_specs=(anywhere,) * 6,
        scratch_shapes=[
            pltpu.SemaphoreType.DMA((OPENING_COPIES,)),
            pltpu.SemaphoreType.DMA((OPENING_COPIES,)),
            pltpu.SemaphoreType.DMA((6,)),
        ],
        compiler_params=pltpu.CompilerParams(
            collective_id=2, has_side_effects=True, vmem_limit_bytes=62 * 2**20
        ),
        cost_estimate=pl.CostEstimate(
            flops=10**11, bytes_accessed=600 * 2**20, transcendentals=0
        ),
        name="opening",
    )(normed, att_in, att_out, shared_in, shared_out, cotangent)


def attention_forward(queries, keys_all, values, score_scale):
    scores = block_scores(queries, keys_all, 0, score_scale)
    highest = jnp.max(scores, axis=-1, keepdims=True)
    raised = jnp.exp(scores - highest)
    probs = raised / jnp.sum(raised, axis=-1, keepdims=True)
    mixed_out = jnp.einsum(
        "hqk,khd->qhd", probs.astype(jnp.bfloat16), values, preferred_element_type=jnp.float32
    )
    return mixed_out, probs


def attention_backward(queries, keys_all, values, probs, grad_out, score_scale):
    value_grad = jnp.einsum(
        "hqk,qhd->khd", probs.astype(jnp.bfloat16), grad_out, preferred_element_type=jnp.float32
    )
    prob_grad = jnp.einsum("qhd,khd->hqk", grad_out, values, preferred_element_type=jnp.float32)
    score_grad = (
        probs * (prob_grad - jnp.sum(prob_grad * probs, axis=-1, keepdims=True))
    ).astype(jnp.bfloat16)
    query_grad = jnp.einsum(
        "hqk,khd->qhd", score_grad, keys_all, preferred_element_type=jnp.float32
    )
    key_grad = jnp.einsum("hqk,qhd->khd", score_grad, queries, preferred_element_type=jnp.float32)
    return query_grad * score_scale, key_grad * score_scale, value_grad


def local_gather(
    tokens,
    first_gain,
    attention_in,
    attention_bias,
    attention_out,
    second_gain,
    router,
    shared_gate,
    shared_in,
    shared_out,
    expert_in,
    expert_out,
    cotangent,
    expert_picks,
):
    bf16, f32 = jnp.bfloat16, jnp.float32
    local_rows, width = tokens.shape
    shards = lax.axis_size(SHARD)
    owners = lax.axis_size(EXPERT)
    owner = lax.axis_index(EXPERT)
    seq_length = local_rows * shards
    experts = router.shape[1]
    owned = expert_in.shape[0]
    part = expert_in.shape[3]
    heads_here = attention_bias.shape[1]
    head_dim = attention_bias.shape[2] * owners
    score_scale = head_dim ** (-0.5)
    shared_part = shared_in.shape[2] // owners
    slice_rows = width // owners
    cosine_table, sine_table = rope_tables(seq_length, head_dim)

    inputs = tokens.astype(f32)
    first_norm, first_factor = normalize(inputs)
    first_low = (first_norm * first_gain).astype(bf16)
    small = jnp.concatenate(
        [router.reshape(-1), shared_gate, attention_bias.reshape(-1)]
    )
    small_rows = -(-small.shape[0] // slice_rows)
    small_rows = -(-small_rows // 16) * 16
    small = jnp.pad(small, (0, small_rows * slice_rows - small.shape[0]))
    small = small.reshape(small_rows, slice_rows)
    shared_blocks = shared_in.transpose(1, 2, 0).reshape(2, owners, shared_part, slice_rows)
    shared_blocks = shared_blocks.transpose(1, 0, 2, 3).reshape(owners, -1, slice_rows)
    normed_all, att_in, out_small, shared_win, shared_wout, cot_all = opening(
        first_low,
        attention_in.transpose(1, 0, 2),
        jnp.concatenate([attention_out, small], axis=0),
        shared_blocks,
        shared_out,
        cotangent,
    )
    att_out = out_small[:, : attention_out.shape[0]].transpose(1, 0, 2)
    att_out = att_out.reshape(attention_out.shape[0], width)
    small_all = out_small[:, attention_out.shape[0] :].reshape(owners, -1)
    router_size = router.size
    router_full = small_all[:, :router_size].reshape(width, experts)
    gate_full = small_all[:, router_size : router_size + slice_rows].reshape(width)
    bias_start = router_size + slice_rows
    att_bias = small_all[:, bias_start : bias_start + attention_bias.size]
    att_bias = att_bias.reshape((owners,) + attention_bias.shape).transpose(1, 2, 0, 3)
    att_bias = att_bias.reshape(3, heads_here * head_dim)

    projected = jnp.einsum("sd,cdf->scf", normed_all, att_in, preferred_element_type=f32)
    projected = projected + att_bias.astype(f32)[None]
    projected = projected.reshape(seq_length, 3, heads_here, head_dim)
    queries = rotate(projected[:, 0], cosine_table, sine_table).astype(bf16)
    keys_all = rotate(projected[:, 1], cosine_table, sine_table).astype(bf16)
    values = projected[:, 2].astype(bf16)
    attended, probs = attention_forward(queries, keys_all, values, score_scale)
    attended_low = attended.astype(bf16).reshape(seq_length, -1)
    attn_part = jnp.dot(attended_low, att_out, preferred_element_type=f32)
    router_wide = jnp.concatenate([router_full.T, gate_full[None]], axis=0)
    router_wide = jnp.pad(router_wide, ((0, EXTRA - experts - 1), (0, 0)))
    picked = jnp.sum(
        (
            expert_picks[:, :, None] == jnp.arange(EXTRA, dtype=jnp.int32)[None, None, :]
        ).astype(f32),
        axis=1,
    )
    units = owned * part + shared_part
    padded = -(-units // 128) * 128
    unit = jnp.arange(padded)
    column = jnp.where(unit < owned * part, owner * owned + unit // part, experts)
    column = jnp.where(unit < units, column, -1)
    kinds = jnp.arange(EXTRA)
    spots = (kinds[None, :] == column[:, None]).astype(bf16)
    finer = jnp.where(unit < units, column + experts + 1, -1)
    select = (kinds[:, None] == column[None, :]) | (kinds[:, None] == finer[None, :])
    (
        output,
        second_block,
        residual_grad,
        logit_grad,
        second_gain_grad,
        rows_all,
        units_all,
        residual_all,
    ) = mixture(
        attn_part.astype(bf16),
        cot_all,
        expert_in,
        shared_win,
        expert_out,
        shared_wout,
        select.astype(bf16),
        spots,
        tokens,
        second_gain[None],
        router_wide,
        picked,
        experts,
    )
    first_dims = (((0,), (0,)), ((), ()))
    att_out_grad = lax.dot_general(
        attended_low, residual_all, first_dims, preferred_element_type=f32
    )
    attended_grad = lax.dot_general(
        residual_all, att_out, (((1,), (1,)), ((), ())), preferred_element_type=f32
    )
    attended_grad = attended_grad.astype(bf16).reshape(seq_length, heads_here, head_dim)
    query_grad, key_grad, value_grad = attention_backward(
        queries, keys_all, values, probs, attended_grad, score_scale
    )
    projected_grad = jnp.stack(
        [
            rotate_back(query_grad, cosine_table, sine_table),
            rotate_back(key_grad, cosine_table, sine_table),
            value_grad,
        ],
        axis=1,
    )
    projected_grad = projected_grad.astype(bf16).reshape(seq_length, 3, heads_here * head_dim)
    att_in_grad = jnp.einsum("sd,scf->cdf", normed_all, projected_grad, preferred_element_type=f32)
    att_bias_grad = jnp.sum(projected_grad.astype(f32), axis=0)
    first_part = jnp.einsum("scf,cdf->sd", projected_grad, att_in, preferred_element_type=f32)
    vec_grads = lax.dot_general(
        logit_grad[:, : experts + 1],
        second_block[:, :width],
        first_dims,
        preferred_element_type=f32,
    )
    bias_wide = jnp.zeros((3, shards, heads_here * head_dim), f32)
    bias_wide = lax.dynamic_update_slice_in_dim(
        bias_wide, att_bias_grad[:, None], lax.axis_index(SHARD), 1
    )
    bias_rows = bias_wide.size // width
    first_bias = experts + 3
    small = jnp.concatenate(
        [vec_grads, second_gain_grad, jnp.zeros((1, width), f32), bias_wide.reshape(-1, width)]
    )
    small = jnp.pad(small, ((0, -small.shape[0] % 8), (0, 0)))
    (
        input_grad,
        att_in_local,
        att_out_local,
        summed,
        expert_in_grad,
        expert_out_grad,
        shared_in_local,
        shared_out_local,
    ) = closing(
        rows_all,
        cot_all,
        units_all,
        att_in_grad.astype(bf16),
        att_out_grad.astype(bf16),
        first_part.astype(bf16),
        small,
        tokens,
        residual_grad,
        first_gain[None],
        experts + 2,
        owned,
        part,
        shared_part,
    )
    expert_in_grad = expert_in_grad.reshape(owned, 2, part, width).transpose(0, 3, 1, 2)
    expert_in_grad = expert_in_grad.astype(f32)
    expert_out_grad = expert_out_grad.reshape(owned, part, width).astype(f32)
    shared_in_local = shared_in_local.reshape(owners, 2, shared_part, slice_rows)
    shared_in_local = shared_in_local.transpose(3, 1, 0, 2).reshape(slice_rows, 2, -1).astype(f32)
    shared_out_local = shared_out_local.reshape(-1, slice_rows).astype(f32)
    vec_local = lax.dynamic_slice_in_dim(
        summed[: experts + 1], owner * slice_rows, slice_rows, axis=1
    )
    bias_all = summed[first_bias : first_bias + bias_rows].reshape(
        3, shards, heads_here, owners, head_dim // owners
    )
    att_bias_local = lax.dynamic_index_in_dim(bias_all, lax.axis_index(SHARD), 1, False)
    att_bias_local = lax.dynamic_index_in_dim(att_bias_local, owner, 2, False)
    return (
        output,
        input_grad,
        summed[experts + 2],
        att_in_local.transpose(1, 0, 2),
        att_bias_local,
        att_out_local,
        summed[experts + 1],
        vec_local[:experts].T,
        vec_local[experts],
        shared_in_local,
        shared_out_local,
        expert_in_grad,
        expert_out_grad,
    )


def solution(mesh):
    in_specs = (
        P((EXPERT, SHARD), None),
        P(),
        P(EXPERT, None, SHARD),
        P(None, SHARD, EXPERT),
        P(SHARD, EXPERT),
        P(),
        P(EXPERT, None),
        P(EXPERT),
        P(EXPERT, None, SHARD),
        P(SHARD, EXPERT),
        P(EXPERT, None, None, SHARD),
        P(EXPERT, SHARD, None),
        P((EXPERT, SHARD), None),
        P((EXPERT, SHARD), None),
    )
    out_specs = (
        P((EXPERT, SHARD), None),
        P((EXPERT, SHARD), None),
        P(),
        P(EXPERT, None, SHARD),
        P(None, SHARD, EXPERT),
        P(SHARD, EXPERT),
        P(),
        P(EXPERT, None),
        P(EXPERT),
        P(EXPERT, None, SHARD),
        P(SHARD, EXPERT),
        P(EXPERT, None, None, SHARD),
        P(EXPERT, SHARD, None),
    )
    plan = local_gather if mesh.size <= 32 else local_exchange
    return jax.shard_map(plan, mesh=mesh, in_specs=in_specs, out_specs=out_specs, check_vma=False)
```
